256 devices in a mesh: dp: 16 (over z_hi, y, core), owner: 16 (over x, z_lo).
Axes of the slice: x: 4, y: 4, z: 8 (z_hi: 2, z_lo: 4; z = z_hi * 4 + z_lo), core: 2. Of those that a mesh axis runs over, the one named last changes fastest.
Arguments:
- activations: bfloat16 [32768, 4096], P(('dp', 'owner'))
- out_grads: bfloat16 [32768, 16384], P(('dp', 'owner'))
- sample_ids: int32 [4096], P(('dp', 'owner')), may hold values from 0 to 127
- damping: float32 [20], replicated, may hold values from 0.3 to 3
- weight_grad: bfloat16 [4096, 16384], P('dp', 'owner'), may hold values from -6 to 6
Outputs:
- preconditioned: bfloat16 [4096, 16384], P('dp', 'owner')
The draws below stay inside these ranges and needn't reach their ends.
Inputs may be any that keep to these rules, and one draw needn't show every extreme that they name: Entry k names token (k // 16) * 128 + sample_ids[k], a token of the same device's rows.
All inputs are finite; a program needn't handle non-finite values.
Results may differ from the reference program's by a relative error of at most 0.014.
Values may be sent and summed in bfloat16 or wider, within the bound.
No kernel may reach another device: no remote copies, remote signals or barrier semaphores. Data moves between devices by JAX's collectives and lax.ppermute only.
A program may use at most 128 MiB of HBM per device.

```python
import math
import jax
import jax.numpy as jnp
from jax import lax

B = 1024
DA = 4096
DG = 16384
TOK_DEV = 128
SAMP_DEV = 16
ITERS = 5
NA = 4
NG = 16
NBLK = 20
TOKENS = 32768
SAMPLES = 4096


def draw_activations(key, part):
    key = jax.random.fold_in(key, 11)
    col_key = jax.random.fold_in(key, 0)
    main_key = jax.random.fold_in(key, 2)
    col_scale = jnp.exp(jax.random.uniform(col_key, (1, DA), jnp.float32, jnp.log(0.5), jnp.log(2.0)))
    values = jax.random.normal(main_key, (TOKENS, DA), jnp.float32) * col_scale
    return values.astype(jnp.bfloat16)


def draw_out_grads(key, part):
    key = jax.random.fold_in(key, 12)
    col_key = jax.random.fold_in(key, 0)
    main_key = jax.random.fold_in(key, 2)
    col_scale = jnp.exp(jax.random.uniform(col_key, (1, DG), jnp.float32, jnp.log(0.5), jnp.log(2.0)))
    values = jax.random.normal(main_key, (TOKENS, DG), jnp.float32) * col_scale
    return values.astype(jnp.bfloat16)


def with_ends(drawn, own_key, least, largest):
    longest = drawn.shape.index(max(drawn.shape))
    spots = []
    for shift in (0, 1):
        where = [jax.random.randint(jax.random.fold_in(own_key, axis), (), 0, length) for axis, length in enumerate(drawn.shape)]
        where[longest] = (where[longest] + shift) % drawn.shape[longest]
        spots.append(tuple(where))
    return drawn.at[spots[0]].set(least).at[spots[1]].set(largest)


def levels(key, extent, shards, least, largest):
    gain = 1.0
    for dim, shards_of in shards:
        steps = jax.random.uniform(jax.random.fold_in(jax.random.fold_in(key, 6), dim), (shards_of,), jnp.float32, least / len(shards), largest / len(shards))
        gain = gain * jnp.repeat(jnp.exp(steps), extent[dim] // shards_of).reshape((-1,) + (1,) * (len(extent) - 1 - dim))
    return gain


def centred(rng, extent, spread, reach, shards=(), kind=jnp.bfloat16):
    drawn = jax.random.normal(rng, extent, jnp.float32) * spread
    if len(shards) > 0:
        drawn = levels(rng, extent, shards, -0.22, 0.18) * drawn
    return jnp.clip(drawn, min=-reach, max=reach).astype(kind)


def setup_inputs(seed: int = 0) -> dict:
    streams_of = jax.random.split(jax.random.key(seed), 6)
    activations = draw_activations(jax.random.fold_in(streams_of[5], 71), 0)
    out_grads = draw_out_grads(jax.random.fold_in(streams_of[5], 71), 0)
    sample_ids = with_ends(jax.random.randint(streams_of[2], (SAMPLES,), 0, TOK_DEV), jax.random.fold_in(streams_of[2], 1), 0, TOK_DEV - 1).astype(jnp.int32)
    damping = jnp.clip(jnp.exp(jax.random.uniform(streams_of[3], (NBLK,), jnp.float32, math.log(0.3), math.log(3.0))), 0.3, 3.0)
    weight_grad = centred(streams_of[4], (DA, DG), 1.0, 6.0, ((0, 16), (1, 16)))
    return {"activations": activations, "out_grads": out_grads, "sample_ids": sample_ids, "damping": damping, "weight_grad": weight_grad}


def factor_blocks(samples, block_count):
    blocks = samples.reshape(samples.shape[0], block_count, B)

    def single(block_index):
        columns = lax.dynamic_index_in_dim(blocks, block_index, 1, keepdims=False)
        return jnp.dot(columns.T, columns, preferred_element_type=jnp.float32)
    return lax.map(single, jnp.arange(block_count, dtype=jnp.int32))

def newton_schulz(factor):
    frob_norm = jnp.sqrt(jnp.sum(factor * factor))
    identity = jnp.eye(B, dtype=jnp.float32)
    factor_bf = factor.astype(jnp.bfloat16)
    iterate = identity / frob_norm
    for round_index in range(ITERS):
        iterate_bf = iterate.astype(jnp.bfloat16)
        product = jnp.dot(factor_bf, iterate_bf, preferred_element_type=jnp.float32).astype(jnp.bfloat16)
        iterate = 2.0 * iterate - jnp.dot(product, iterate_bf, preferred_element_type=jnp.float32)
    return (iterate * (frob_norm / 2.0 ** ITERS)).astype(jnp.bfloat16)

def reference(activations, out_grads, sample_ids, damping, weight_grad):
    positions = jnp.arange(sample_ids.shape[0], dtype=jnp.int32)
    owner_tok = positions // SAMP_DEV * TOK_DEV + sample_ids
    samp_x = activations[owner_tok]
    samp_g = out_grads[owner_tok]
    factors = jnp.concatenate([factor_blocks(samp_x, NA), factor_blocks(samp_g, NG)], axis=0) / SAMPLES
    factors = factors + damping[:, None, None] * jnp.eye(B, dtype=jnp.float32)[None]
    scaled = lax.map(newton_schulz, factors)
    grad_cols = weight_grad.reshape(DA, NG, B)

    def right_block(block_index):
        columns = lax.dynamic_index_in_dim(grad_cols, block_index, 1, keepdims=False)
        inverse = lax.dynamic_index_in_dim(scaled, NA + block_index, 0, keepdims=False)
        return jnp.dot(columns, inverse, preferred_element_type=jnp.float32).astype(jnp.bfloat16)
    mixed_cols = lax.map(right_block, jnp.arange(NG, dtype=jnp.int32))

    def left_block(block_index):
        row_block = lax.dynamic_slice_in_dim(mixed_cols, block_index * B, B, 1)
        inverse = lax.dynamic_index_in_dim(scaled, block_index, 0, keepdims=False)
        product_value = jnp.einsum('ab,jbc->ajc', inverse.astype(jnp.float32), row_block.astype(jnp.float32))
        return product_value.astype(jnp.bfloat16)
    result = lax.map(left_block, jnp.arange(NA, dtype=jnp.int32))
    return result.reshape(DA, DG)
```

```python
import jax
import jax.numpy as jnp
from jax import lax
from jax.experimental import pallas as pl
from jax.experimental.pallas import tpu as pltpu
from jax.sharding import PartitionSpec as P

BLOCKS_A = 4
ITERS = 5
BF16 = jnp.bfloat16
F32 = jnp.float32
MIB = 2 ** 20
UPPER = [(r, c) for r in range(4) for c in range(r, 4)]
SMEM = pl.BlockSpec(memory_space=pltpu.SMEM)
VMEM = pl.BlockSpec(memory_space=pltpu.VMEM)


def dot(a, b):
    return jnp.dot(a, b, preferred_element_type=F32)


def gram(a, b):
    return lax.dot_general(a, b, (((0,), (0,)), ((), ())), preferred_element_type=F32)


def linear(zh, y, c, x, zl):
    return ((zh * 4 + y) * 2 + c) * 16 + x * 4 + zl


def moved(value, where):
    pairs = []
    for source in range(256):
        c, x, zl = source // 16 % 2, source // 4 % 4, source % 4
        zh, y = source // 128, source // 32 % 4
        target = where(zh, y, c, x, zl)
        if target is not None:
            pairs.append((source, linear(*target)))
    return lax.ppermute(value, ("dp", "owner"), pairs)


def z_shift(zh, zl, k):
    z = zh * 4 + zl
    z = (z + {1: 1, 2: 2 if z % 2 == 0 else -2, 3: -1}[k]) % 8
    return z // 4, z % 4


def pack_kernel(place_ref, mine_ref, other_ref, *outs):
    count, size = mine_ref.shape[0], outs[0].shape[1]
    for k, out in enumerate(outs):
        for owner in range(4):
            index = owner * 4 + lax.rem(place_ref[0] + k, 4)
            cols = pl.ds(pl.multiple_of(index * size, size), size)
            out[owner * 2 * count:(owner * 2 + 1) * count, :] = mine_ref[:, cols]
            out[(owner * 2 + 1) * count:(owner * 2 + 2) * count, :] = other_ref[:, cols]


def pack(place, mine, other, size):
    return pl.pallas_call(
        pack_kernel,
        out_shape=(jax.ShapeDtypeStruct((8 * mine.shape[0], size), BF16),) * 4,
        in_specs=[SMEM, VMEM, VMEM],
        out_specs=(VMEM,) * 4,
        compiler_params=pltpu.CompilerParams(vmem_limit_bytes=8 * MIB),
    )(place, mine, other)


def deal_kernel(place_ref, h0, h1, h2, h3, *outs):
    rows = h0.shape[0] // 4
    for k, out in enumerate(outs):
        start = pl.multiple_of(lax.rem(place_ref[0] + k, 4) * rows, rows)
        for i, held in enumerate((h0, h1, h2, h3)):
            out[i * rows:(i + 1) * rows, :] = held[pl.ds(start, rows), :]


def deal(place, held):
    return pl.pallas_call(
        deal_kernel,
        out_shape=(jax.ShapeDtypeStruct(held[0].shape, BF16),) * 4,
        in_specs=[SMEM] + [VMEM] * 4,
        out_specs=(VMEM,) * 4,
        compiler_params=pltpu.CompilerParams(vmem_limit_bytes=8 * MIB),
    )(place, *held)


def cov_kernel(scale, place_ref, *refs):
    dealt, held, chunks, (all_ref, panel_ref) = refs[:4], refs[4:8], refs[8:12], refs[12:]
    count, size = held[0].shape
    tile, sub = size // 4, size // 16
    for role, pieces in enumerate((dealt, held)):
        @pl.when(place_ref[2] == role)
        def _():
            for k, piece in enumerate(pieces):
                all_ref[k * count:(k + 1) * count, :] = piece[...]
    for r in range(4):
        cols = all_ref[:, r * tile:(r + 1) * tile]
        panel_ref[:, r * tile:] = gram(cols, all_ref[:, r * tile:]) * scale
        for k, chunk in enumerate(chunks):
            start = pl.multiple_of(lax.rem(place_ref[0] + k * place_ref[1], 4) * sub, sub)
            for t, (row, c) in enumerate(UPPER):
                if row == r:
                    chunk[t * sub:(t + 1) * sub, :] = panel_ref[
                        pl.ds(start, sub), c * tile:(c + 1) * tile].astype(BF16)


def cov(place, dealt, held, scale):
    count, size = held[0].shape
    tile, sub = size // 4, size // 16
    return pl.pallas_call(
        lambda *refs: cov_kernel(scale, *refs),
        out_shape=(jax.ShapeDtypeStruct((len(UPPER) * sub, tile), BF16),) * 4,
        in_specs=[SMEM] + [VMEM] * 8,
        out_specs=(VMEM,) * 4,
        scratch_shapes=[pltpu.VMEM((4 * count, size), BF16), pltpu.VMEM((tile, size), F32)],
        compiler_params=pltpu.CompilerParams(vmem_limit_bytes=16 * MIB),
    )(place, *dealt, *held)


def rounds_kernel(place_ref, damp_ref, p0, p1, p2, p3, out_ref, a_ref, x_ref, xb_ref, p_ref):
    size = out_ref.shape[0]
    tile = size // 4
    sub = tile // 4
    base, damp = place_ref[0], damp_ref[0]
    for k, piece in enumerate((p0, p1, p2, p3)):
        start = pl.multiple_of(lax.rem(base + 4 - k, 4) * sub, sub)
        for t, (r, c) in enumerate(UPPER):
            a_ref[pl.ds(r * tile + start, sub), c * tile:(c + 1) * tile] = piece[t * sub:(t + 1) * sub, :]
    row = lax.broadcasted_iota(jnp.int32, (tile, tile), 0)
    col = lax.broadcasted_iota(jnp.int32, (tile, tile), 1)
    eye = row == col
    total = jnp.zeros((1, 1), F32)
    for r, c in UPPER:
        rows, cols = slice(r * tile, (r + 1) * tile), slice(c * tile, (c + 1) * tile)
        value = a_ref[rows, cols].astype(F32)
        if r == c:
            value = value + jnp.where(eye, damp, 0.0)
            a_ref[rows, cols] = value.astype(BF16)
            total += jnp.sum(value * value, keepdims=True)
        else:
            total += 2.0 * jnp.sum(value * value, keepdims=True)
            a_ref[cols, rows] = value.T.astype(BF16)
    frob = jnp.sqrt(total)
    inv = 1.0 / frob
    inv_bf = inv.astype(BF16).astype(F32)
    for r in range(4):
        rows = slice(r * tile, (r + 1) * tile)
        for c in range(4):
            cols = slice(c * tile, (c + 1) * tile)
            product = (a_ref[rows, cols].astype(F32) * inv_bf).astype(BF16).astype(F32)
            value = -product * inv_bf
            if r == c:
                value = value + jnp.where(eye, 2.0 * inv, 0.0)
            x_ref[rows, cols] = value
            xb_ref[0, rows, cols] = value.astype(BF16)
    for step in range(1, ITERS):
        now, later = (step - 1) % 2, step % 2
        for r in range(4):
            rows = slice(r * tile, (r + 1) * tile)
            p_ref[rows, :] = dot(a_ref[rows, :], xb_ref[now]).astype(BF16)
        for r in range(4):
            rows = slice(r * tile, (r + 1) * tile)
            value = 2.0 * x_ref[rows, :] - dot(p_ref[rows, :], xb_ref[now])
            if step < ITERS - 1:
                x_ref[rows, :] = value
                xb_ref[later, rows, :] = value.astype(BF16)
            else:
                out_ref[rows, :] = (value * (frob / 2.0 ** ITERS)).astype(BF16)


def rounds(place, damp, pieces):
    tile = pieces[0].shape[1]
    size = tile * 4
    return pl.pallas_call(
        rounds_kernel,
        out_shape=jax.ShapeDtypeStruct((size, size), BF16),
        in_specs=[SMEM, SMEM] + [VMEM] * 4,
        out_specs=VMEM,
        scratch_shapes=[
            pltpu.VMEM((size, size), BF16),
            pltpu.VMEM((size, size), F32),
            pltpu.VMEM((2, size, size), BF16),
            pltpu.VMEM((size, size), BF16),
        ],
        cost_estimate=pl.CostEstimate(flops=16 * size ** 3, transcendentals=0, bytes_accessed=4 * size * size),
        compiler_params=pltpu.CompilerParams(vmem_limit_bytes=24 * MIB),
    )(place, damp, *pieces)


def mix_kernel(place_ref, s_ref, w0, w1, w2, w3, t0_ref, t1_ref):
    tile, size = t0_ref.shape
    half = place_ref[2]

    @pl.when(place_ref[1] == 1)
    def _():
        for i, target in enumerate((t0_ref, t1_ref)):
            rows = pl.ds(pl.multiple_of((2 * half + i) * tile, tile), tile)
            value = jnp.zeros((tile, size), F32)
            for b, w in enumerate((w0, w1, w2, w3)):
                cols = pl.ds(pl.multiple_of(lax.rem(2 * half + b, 4) * tile, tile), tile)
                value += dot(s_ref[rows, cols], w[...])
            target[...] = value.astype(BF16)


def mix(place, inverse, weights):
    return pl.pallas_call(
        mix_kernel,
        out_shape=(jax.ShapeDtypeStruct(weights[0].shape, BF16),) * 2,
        in_specs=[SMEM] + [VMEM] * 5,
        out_specs=(VMEM,) * 2,
        compiler_params=pltpu.CompilerParams(vmem_limit_bytes=16 * MIB),
    )(place, inverse, *weights)


def last_kernel(place_ref, t0_ref, s_own, t1_ref, s_other, out_ref):
    @pl.when(place_ref[1] == 0)
    def _():
        out_ref[...] = dot(t0_ref[...], s_own[...]).astype(BF16)

    @pl.when(place_ref[1] == 1)
    def _():
        out_ref[...] = dot(t1_ref[...], s_other[...]).astype(BF16)


def last(place, t0, s_own, t1, s_other):
    return pl.pallas_call(
        last_kernel,
        out_shape=jax.ShapeDtypeStruct(t0.shape, BF16),
        in_specs=[SMEM] + [VMEM] * 4,
        out_specs=VMEM,
        compiler_params=pltpu.CompilerParams(vmem_limit_bytes=16 * MIB),
    )(place, t0, s_own, t1, s_other)


def pick(parts, index):
    return lax.dynamic_index_in_dim(parts, index, 0, keepdims=False)


def on_device(activations, out_grads, sample_ids, damping, weight_grad):
    d, o = lax.axis_index("dp"), lax.axis_index("owner")
    zh, y, core = d // 8, d // 2 % 4, d % 2
    x, zl = o // 4, o % 4
    size = weight_grad.shape[1]
    scale = 1.0 / (sample_ids.shape[0] * 256)
    is_g = core == 0

    hot = (sample_ids[:, None] == jnp.arange(activations.shape[0], dtype=jnp.int32)[None]).astype(BF16)
    samp_x = dot(hot, activations).astype(BF16)
    other_x = moved(samp_x, lambda zh, y, c, x, zl: (zh, y, 1, x, zl) if c == 0 else None)
    samp_g = dot(hot, out_grads).astype(BF16)
    other_g = moved(samp_g, lambda zh, y, c, x, zl: (zh, y, 0, x, zl) if c == 1 else None)

    both_x = jnp.concatenate([samp_x, other_x])
    mine_x = []
    for dz, dy in ((0, 0), (0, 1), (1, 0), (1, 1)):
        block = (zh ^ dz) * 2 + (y // 2 ^ dy)
        sent = lax.dynamic_slice_in_dim(both_x, block * size, size, 1)
        mine_x.append(sent if dz + dy == 0 else moved(
            sent, lambda zh, y, c, x, zl: (zh ^ dz, y ^ (2 * dy), 1, x, zl) if c == 1 else None))
    mine_x = jnp.concatenate(mine_x)

    packed = pack(((zl + 2) % 4).reshape(1), samp_g, other_g, size)
    own_w, *packed = lax.optimization_barrier((weight_grad, *packed))
    weights = [
        moved(own_w, lambda zh, y, c, x, zl: (zh, y, 1, x, zl) if c == 0 else None),
        moved(own_w, lambda zh, y, c, x, zl: (zh, y ^ 1, 1, x, zl) if c == 0 else None),
        moved(own_w, lambda zh, y, c, x, zl: (zh, y ^ 1, 1, x, zl) if c == 1 else None),
    ]
    held = [jnp.where(is_g, packed[0], mine_x)]
    for k in (1, 2, 3):
        held.append(moved(
            jnp.where(is_g, packed[k], mine_x),
            lambda zh, y, c, x, zl: (z_shift(zh, zl, k)[0], y, 0, x, z_shift(zh, zl, k)[1]) if c == 0
            else (zh, y, 1, (x + k) % 4, zl),
        ))

    dealt = list(deal(x.reshape(1), held))
    for k in (1, 2, 3):
        dealt[k] = moved(dealt[k], lambda zh, y, c, x, zl: (zh, y, 0, (x + k) % 4, zl) if c == 0 else None)

    weights, dealt = lax.optimization_barrier((weights, dealt))
    weights.insert(1, weight_grad)

    chunks = cov(jnp.stack([jnp.where(is_g, y, x), 1 - core, core]), dealt, held, scale)
    total = chunks[0].astype(F32)
    for k in (1, 2, 3):
        total += moved(
            chunks[k],
            lambda zh, y, c, x, zl: (zh, (y + k) % 4, 0, x, zl) if c == 0 else (zh, y, 1, x, (zl + k) % 4),
        ).astype(F32)
    part = total.astype(BF16)

    def beside(zh, zl, by):
        z = (zh * 4 + zl + by) % 8
        return z // 4, z % 4

    here = moved(part, lambda zh, y, c, x, zl: (beside(zh, zl, 2)[0], y, 0, x, beside(zh, zl, 2)[1]) if c == 0
                 else (zh, y ^ 1, 1, x, zl))
    there = moved(part, lambda zh, y, c, x, zl: (beside(zh, zl, -2)[0], y, 0, x, beside(zh, zl, -2)[1]) if c == 0
                  else None)
    piece = (here.astype(F32) + jnp.where(is_g, there, part).astype(F32)).astype(BF16)

    pieces = [piece]
    for k in (1, 2, 3):
        pieces.append(moved(
            piece,
            lambda zh, y, c, x, zl: (zh, (y + k) % 4, 0, x, zl) if c == 0 else (zh, y, 1, (x + k) % 4, zl),
        ))

    damp = pick(damping, jnp.where(is_g, BLOCKS_A + o, zh * 2 + y // 2)).reshape(1)
    place = jnp.stack([jnp.where(is_g, y, x), core, y % 2])
    inverse = rounds(place, damp, pieces)

    inv_g = moved(inverse, lambda zh, y, c, x, zl: (zh, y, 1, x, zl) if c == 0 else None)
    mixed_0, mixed_1 = mix(place, inverse, weights)
    mixed_0 = moved(mixed_0, lambda zh, y, c, x, zl: (zh, y, 0, x, zl) if c == 1 else None)
    return last(place, mixed_0, inverse, mixed_1, inv_g)


def solution(mesh):
    placed = (
        P(("dp", "owner"), None),
        P(("dp", "owner"), None),
        P(("dp", "owner")),
        P(),
        P("dp", "owner"),
    )
    return jax.shard_map(
        on_device, mesh=mesh, in_specs=placed, out_specs=P("dp", "owner"), check_vma=False
    )
```

```python
import jax
import jax.numpy as jnp
from jax import lax
from jax.experimental import pallas as pl
from jax.experimental.pallas import tpu as pltpu
from jax.sharding import PartitionSpec as P

BLOCKS_A = 4
ITERS = 5
BF16 = jnp.bfloat16
F32 = jnp.float32
MIB = 2 ** 20
UPPER = [(r, c) for r in range(4) for c in range(r, 4)]
SMEM = pl.BlockSpec(memory_space=pltpu.SMEM)
VMEM = pl.BlockSpec(memory_space=pltpu.VMEM)


def dot(a, b):
    return jnp.dot(a, b, preferred_element_type=F32)


def gram(a, b):
    return lax.dot_general(a, b, (((0,), (0,)), ((), ())), preferred_element_type=F32)


def linear(zh, y, c, x, zl):
    return ((zh * 4 + y) * 2 + c) * 16 + x * 4 + zl


def moved(value, where):
    pairs = []
    for source in range(256):
        c, x, zl = source // 16 % 2, source // 4 % 4, source % 4
        zh, y = source // 128, source // 32 % 4
        target = where(zh, y, c, x, zl)
        if target is not None:
            pairs.append((source, linear(*target)))
    return lax.ppermute(value, ("dp", "owner"), pairs)


def z_shift(zh, zl, k):
    z = zh * 4 + zl
    z = (z + {1: 1, 2: 2 if z % 2 == 0 else -2, 3: -1}[k]) % 8
    return z // 4, z % 4


def across(zh, y, x, zl, dz, dy):
    z = (zh * 4 + zl + dz * (-2 if zl < 2 else 2)) % 8
    return z // 4, 3 - y if dy else y, 1, x, z % 4


def pack_kernel(place_ref, mine_ref, other_ref, *outs):
    count, size = mine_ref.shape[0], outs[0].shape[1]
    for k, out in enumerate(outs):
        for owner in range(4):
            index = owner * 4 + lax.rem(place_ref[0] + k, 4)
            cols = pl.ds(pl.multiple_of(index * size, size), size)
            out[owner * 2 * count:(owner * 2 + 1) * count, :] = mine_ref[:, cols]
            out[(owner * 2 + 1) * count:(owner * 2 + 2) * count, :] = other_ref[:, cols]


def pack(place, mine, other, size):
    return pl.pallas_call(
        pack_kernel,
        out_shape=(jax.ShapeDtypeStruct((8 * mine.shape[0], size), BF16),) * 4,
        in_specs=[SMEM, VMEM, VMEM],
        out_specs=(VMEM,) * 4,
        compiler_params=pltpu.CompilerParams(vmem_limit_bytes=8 * MIB),
    )(place, mine, other)


def deal_kernel(place_ref, h0, h1, h2, h3, *outs):
    rows = h0.shape[0] // 4
    for k, out in enumerate(outs):
        start = pl.multiple_of(lax.rem(place_ref[0] + k, 4) * rows, rows)
        for i, held in enumerate((h0, h1, h2, h3)):
            out[i * rows:(i + 1) * rows, :] = held[pl.ds(start, rows), :]


def deal(place, held):
    return pl.pallas_call(
        deal_kernel,
        out_shape=(jax.ShapeDtypeStruct(held[0].shape, BF16),) * 4,
        in_specs=[SMEM] + [VMEM] * 4,
        out_specs=(VMEM,) * 4,
        compiler_params=pltpu.CompilerParams(vmem_limit_bytes=8 * MIB),
    )(place, *held)


def cov_kernel(scale, place_ref, *refs):
    dealt, held, chunks, (all_ref, panel_ref) = refs[:4], refs[4:8], refs[8:12], refs[12:]
    count, size = held[0].shape
    tile, sub = size // 4, size // 16
    for role, pieces in enumerate((dealt, held)):
        @pl.when(place_ref[2] == role)
        def _():
            for k, piece in enumerate(pieces):
                all_ref[k * count:(k + 1) * count, :] = piece[...]
    for r in range(4):
        cols = all_ref[:, r * tile:(r + 1) * tile]
        panel_ref[:, r * tile:] = gram(cols, all_ref[:, r * tile:]) * scale
        for k, chunk in enumerate(chunks):
            start = pl.multiple_of(lax.rem(place_ref[0] + k * place_ref[1], 4) * sub, sub)
            for t, (row, c) in enumerate(UPPER):
                if row == r:
                    chunk[t * sub:(t + 1) * sub, :] = panel_ref[
                        pl.ds(start, sub), c * tile:(c + 1) * tile].astype(BF16)


def cov(place, dealt, held, scale):
    count, size = held[0].shape
    tile, sub = size // 4, size // 16
    return pl.pallas_call(
        lambda *refs: cov_kernel(scale, *refs),
        out_shape=(jax.ShapeDtypeStruct((len(UPPER) * sub, tile), BF16),) * 4,
        in_specs=[SMEM] + [VMEM] * 8,
        out_specs=(VMEM,) * 4,
        scratch_shapes=[pltpu.VMEM((4 * count, size), BF16), pltpu.VMEM((tile, size), F32)],
        compiler_params=pltpu.CompilerParams(vmem_limit_bytes=16 * MIB),
    )(place, *dealt, *held)


def rounds_kernel(place_ref, damp_ref, p0, p1, p2, p3, out_ref, a_ref, x_ref, xb_ref, p_ref):
    size = out_ref.shape[0]
    tile = size // 4
    sub = tile // 4
    base, damp = place_ref[0], damp_ref[0]
    for k, piece in enumerate((p0, p1, p2, p3)):
        start = pl.multiple_of(lax.rem(base + 4 - k, 4) * sub, sub)
        for t, (r, c) in enumerate(UPPER):
            a_ref[pl.ds(r * tile + start, sub), c * tile:(c + 1) * tile] = piece[t * sub:(t + 1) * sub, :]
    row = lax.broadcasted_iota(jnp.int32, (tile, tile), 0)
    col = lax.broadcasted_iota(jnp.int32, (tile, tile), 1)
    eye = row == col
    total = jnp.zeros((1, 1), F32)
    for r, c in UPPER:
        rows, cols = slice(r * tile, (r + 1) * tile), slice(c * tile, (c + 1) * tile)
        value = a_ref[rows, cols].astype(F32)
        if r == c:
            value = value + jnp.where(eye, damp, 0.0)
            a_ref[rows, cols] = value.astype(BF16)
            total += jnp.sum(value * value, keepdims=True)
        else:
            total += 2.0 * jnp.sum(value * value, keepdims=True)
            a_ref[cols, rows] = value.T.astype(BF16)
    frob = jnp.sqrt(total)
    inv = 1.0 / frob
    inv_bf = inv.astype(BF16).astype(F32)
    for r in range(4):
        rows = slice(r * tile, (r + 1) * tile)
        for c in range(4):
            cols = slice(c * tile, (c + 1) * tile)
            product = (a_ref[rows, cols].astype(F32) * inv_bf).astype(BF16).astype(F32)
            value = -product * inv_bf
            if r == c:
                value = value + jnp.where(eye, 2.0 * inv, 0.0)
            x_ref[rows, cols] = value
            xb_ref[0, rows, cols] = value.astype(BF16)
    for step in range(1, ITERS):
        now, later = (step - 1) % 2, step % 2
        for r in range(4):
            rows = slice(r * tile, (r + 1) * tile)
            p_ref[rows, :] = dot(a_ref[rows, :], xb_ref[now]).astype(BF16)
        for r in range(4):
            rows = slice(r * tile, (r + 1) * tile)
            value = 2.0 * x_ref[rows, :] - dot(p_ref[rows, :], xb_ref[now])
            if step < ITERS - 1:
                x_ref[rows, :] = value
                xb_ref[later, rows, :] = value.astype(BF16)
            else:
                out_ref[rows, :] = (value * (frob / 2.0 ** ITERS)).astype(BF16)


def rounds(place, damp, pieces):
    tile = pieces[0].shape[1]
    size = tile * 4
    return pl.pallas_call(
        rounds_kernel,
        out_shape=jax.ShapeDtypeStruct((size, size), BF16),
        in_specs=[SMEM, SMEM] + [VMEM] * 4,
        out_specs=VMEM,
        scratch_shapes=[
            pltpu.VMEM((size, size), BF16),
            pltpu.VMEM((size, size), F32),
            pltpu.VMEM((2, size, size), BF16),
            pltpu.VMEM((size, size), BF16),
        ],
        cost_estimate=pl.CostEstimate(flops=16 * size ** 3, transcendentals=0, bytes_accessed=4 * size * size),
        compiler_params=pltpu.CompilerParams(vmem_limit_bytes=24 * MIB),
    )(place, damp, *pieces)


def mix_kernel(place_ref, s_ref, w0, w1, w2, w3, t0_ref, t1_ref):
    tile, size = t0_ref.shape
    half = place_ref[2]

    @pl.when(place_ref[1] == 1)
    def _():
        for i, target in enumerate((t0_ref, t1_ref)):
            rows = pl.ds(pl.multiple_of((2 * half + i) * tile, tile), tile)
            value = jnp.zeros((tile, size), F32)
            for b, w in enumerate((w0, w1, w2, w3)):
                cols = pl.ds(pl.multiple_of(lax.rem(2 * half + b, 4) * tile, tile), tile)
                value += dot(s_ref[rows, cols], w[...])
            target[...] = value.astype(BF16)


def mix(place, inverse, weights):
    return pl.pallas_call(
        mix_kernel,
        out_shape=(jax.ShapeDtypeStruct(weights[0].shape, BF16),) * 2,
        in_specs=[SMEM] + [VMEM] * 5,
        out_specs=(VMEM,) * 2,
        compiler_params=pltpu.CompilerParams(vmem_limit_bytes=16 * MIB),
    )(place, inverse, *weights)


def last_kernel(place_ref, t0_ref, s_own, t1_ref, s_other, out_ref):
    @pl.when(place_ref[1] == 0)
    def _():
        out_ref[...] = dot(t0_ref[...], s_own[...]).astype(BF16)

    @pl.when(place_ref[1] == 1)
    def _():
        out_ref[...] = dot(t1_ref[...], s_other[...]).astype(BF16)


def last(place, t0, s_own, t1, s_other):
    return pl.pallas_call(
        last_kernel,
        out_shape=jax.ShapeDtypeStruct(t0.shape, BF16),
        in_specs=[SMEM] + [VMEM] * 4,
        out_specs=VMEM,
        compiler_params=pltpu.CompilerParams(vmem_limit_bytes=16 * MIB),
    )(place, t0, s_own, t1, s_other)


def pick(parts, index):
    return lax.dynamic_index_in_dim(parts, index, 0, keepdims=False)


def on_device(activations, out_grads, sample_ids, damping, weight_grad):
    d, o = lax.axis_index("dp"), lax.axis_index("owner")
    zh, y, core = d // 8, d // 2 % 4, d % 2
    x, zl = o // 4, o % 4
    size = weight_grad.shape[1]
    scale = 1.0 / (sample_ids.shape[0] * 256)
    is_g = core == 0

    hot = (sample_ids[:, None] == jnp.arange(activations.shape[0], dtype=jnp.int32)[None]).astype(BF16)
    samp_x = dot(hot, activations).astype(BF16)
    other_x = moved(samp_x, lambda zh, y, c, x, zl: (zh, y, 1, x, zl) if c == 0 else None)
    samp_g = dot(hot, out_grads).astype(BF16)
    other_g = moved(samp_g, lambda zh, y, c, x, zl: (zh, y, 0, x, zl) if c == 1 else None)

    both_x = jnp.concatenate([samp_x, other_x])
    mine_x = []
    for dz, dy in ((0, 0), (0, 1), (1, 0), (1, 1)):
        block = (zh ^ dz) * 2 + (y // 2 ^ dy)
        sent = lax.dynamic_slice_in_dim(both_x, block * size, size, 1)
        mine_x.append(sent if dz + dy == 0 else moved(
            sent, lambda zh, y, c, x, zl: across(zh, y, x, zl, dz, dy) if c == 1 else None))
    mine_x = jnp.concatenate(mine_x)

    packed = pack(((zl + 2) % 4).reshape(1), samp_g, other_g, size)
    held = [jnp.where(is_g, packed[0], mine_x)]
    for k in (1, 2, 3):
        held.append(moved(
            jnp.where(is_g, packed[k], mine_x),
            lambda zh, y, c, x, zl: (z_shift(zh, zl, k)[0], y, 0, x, z_shift(zh, zl, k)[1]) if c == 0
            else (zh, y, 1, (x + k) % 4, zl),
        ))

    dealt = list(deal(x.reshape(1), held))
    for k in (1, 2, 3):
        dealt[k] = moved(dealt[k], lambda zh, y, c, x, zl: (zh, y, 0, (x + k) % 4, zl) if c == 0 else None)

    chunks = cov(jnp.stack([jnp.where(is_g, y, x), 1 - core, core]), dealt, held, scale)
    total = chunks[0].astype(F32)
    for k in (1, 2, 3):
        total += moved(
            chunks[k],
            lambda zh, y, c, x, zl: (zh, (y + k) % 4, 0, x, zl) if c == 0 else (zh, y, 1, x, (zl + k) % 4),
        ).astype(F32)
    part = total.astype(BF16)

    def beside(zh, zl, by):
        z = (zh * 4 + zl + by) % 8
        return z // 4, z % 4

    here = moved(part, lambda zh, y, c, x, zl: (beside(zh, zl, 2)[0], y, 0, x, beside(zh, zl, 2)[1]) if c == 0
                 else (zh, y ^ 1, 1, x, zl))
    there = moved(part, lambda zh, y, c, x, zl: (beside(zh, zl, -2)[0], y, 0, x, beside(zh, zl, -2)[1]) if c == 0
                  else None)
    piece = (here.astype(F32) + jnp.where(is_g, there, part).astype(F32)).astype(BF16)

    pieces = [piece]
    for k in (1, 2, 3):
        pieces.append(moved(
            piece,
            lambda zh, y, c, x, zl: (zh, (y + k) % 4, 0, x, zl) if c == 0 else (zh, y, 1, (x + k) % 4, zl),
        ))

    own_w, _ = lax.optimization_barrier((weight_grad, piece))
    weights = [
        moved(own_w, lambda zh, y, c, x, zl: (zh, y, 1, x, zl) if c == 0 else None),
        moved(own_w, lambda zh, y, c, x, zl: (zh, y ^ 1, 1, x, zl) if c == 0 else None),
        moved(own_w, lambda zh, y, c, x, zl: (zh, y ^ 1, 1, x, zl) if c == 1 else None),
    ]
    damp = pick(damping, jnp.where(is_g, BLOCKS_A + o, zh * 2 + y // 2)).reshape(1)
    place = jnp.stack([jnp.where(is_g, y, x), core, y % 2])
    inverse, *weights = lax.optimization_barrier((rounds(place, damp, pieces), *weights))
    weights.insert(1, weight_grad)

    inv_g = moved(inverse, lambda zh, y, c, x, zl: (zh, y, 1, x, zl) if c == 0 else None)
    mixed_0, mixed_1 = mix(place, inverse, weights)
    mixed_0 = moved(mixed_0, lambda zh, y, c, x, zl: (zh, y, 0, x, zl) if c == 1 else None)
    return last(place, mixed_0, inverse, mixed_1, inv_g)


def solution(mesh):
    placed = (
        P(("dp", "owner"), None),
        P(("dp", "owner"), None),
        P(("dp", "owner")),
        P(),
        P("dp", "owner"),
    )
    return jax.shard_map(
        on_device, mesh=mesh, in_specs=placed, out_specs=P("dp", "owner"), check_vma=False
    )
```

```python
import jax
import jax.numpy as jnp
from jax import lax
from jax.experimental import pallas as pl
from jax.experimental.pallas import tpu as pltpu
from jax.sharding import PartitionSpec as P

BLOCKS_A = 4
ITERS = 5
BF16 = jnp.bfloat16
F32 = jnp.float32
MIB = 2 ** 20
UPPER = [(r, c) for r in range(4) for c in range(r, 4)]
SMEM = pl.BlockSpec(memory_space=pltpu.SMEM)
VMEM = pl.BlockSpec(memory_space=pltpu.VMEM)


def dot(a, b):
    return jnp.dot(a, b, preferred_element_type=F32)


def gram(a, b):
    return lax.dot_general(a, b, (((0,), (0,)), ((), ())), preferred_element_type=F32)


def linear(zh, y, c, x, zl):
    return ((zh * 4 + y) * 2 + c) * 16 + x * 4 + zl


def moved(value, where):
    pairs = []
    for source in range(256):
        c, x, zl = source // 16 % 2, source // 4 % 4, source % 4
        zh, y = source // 128, source // 32 % 4
        target = where(zh, y, c, x, zl)
        if target is not None:
            pairs.append((source, linear(*target)))
    return lax.ppermute(value, ("dp", "owner"), pairs)


def z_shift(zh, zl, k):
    z = zh * 4 + zl
    z = (z + {1: 1, 2: 2 if z % 2 == 0 else -2, 3: -1}[k]) % 8
    return z // 4, z % 4


def pack_kernel(place_ref, mine_ref, other_ref, *outs):
    count, size = mine_ref.shape[0], outs[0].shape[1]
    for k, out in enumerate(outs):
        for zl in range(4):
            index = lax.rem(place_ref[0] + k, 4) * 4 + zl
            cols = pl.ds(pl.multiple_of(index * size, size), size)
            out[zl * 2 * count:(zl * 2 + 1) * count, :] = mine_ref[:, cols]
            out[(zl * 2 + 1) * count:(zl * 2 + 2) * count, :] = other_ref[:, cols]


def pack(place, mine, other, size):
    return pl.pallas_call(
        pack_kernel,
        out_shape=(jax.ShapeDtypeStruct((8 * mine.shape[0], size), BF16),) * 4,
        in_specs=[SMEM, VMEM, VMEM],
        out_specs=(VMEM,) * 4,
        compiler_params=pltpu.CompilerParams(vmem_limit_bytes=8 * MIB),
    )(place, mine, other)


def deal_kernel(place_ref, h0, h1, h2, h3, kept_ref, come_ref, *outs):
    rows = h0.shape[0] // 4
    half = kept_ref.shape[0]

    @pl.when(place_ref[1] == 0)
    def _():
        for k, out in enumerate(outs):
            start = pl.multiple_of(lax.rem(place_ref[0] + k, 4) * rows, rows)
            for i, held in enumerate((h0, h1, h2, h3)):
                out[i * rows:(i + 1) * rows, :] = held[pl.ds(start, rows), :]

    @pl.when(place_ref[1] == 1)
    def _():
        for out in outs:
            out[:half, :] = kept_ref[...]
            out[half:, :] = come_ref[...]


def deal(place, held, kept, come):
    return pl.pallas_call(
        deal_kernel,
        out_shape=(jax.ShapeDtypeStruct(held[0].shape, BF16),) * 4,
        in_specs=[SMEM] + [VMEM] * 6,
        out_specs=(VMEM,) * 4,
        compiler_params=pltpu.CompilerParams(vmem_limit_bytes=8 * MIB),
    )(place, *held, kept, come)


def cov_kernel(scale, place_ref, *refs):
    pieces, chunks, (all_ref, panel_ref) = refs[:4], refs[4:8], refs[8:]
    count, size = pieces[0].shape
    tile, sub = size // 4, size // 16
    for k, piece in enumerate(pieces):
        all_ref[k * count:(k + 1) * count, :] = piece[...]
    for r in range(4):
        cols = all_ref[:, r * tile:(r + 1) * tile]
        panel_ref[:, r * tile:] = gram(cols, all_ref[:, r * tile:]) * scale
        for k, chunk in enumerate(chunks):
            start = pl.multiple_of(lax.rem(place_ref[0] + k * place_ref[1], 4) * sub, sub)
            for t, (row, c) in enumerate(UPPER):
                if row == r:
                    chunk[t * sub:(t + 1) * sub, :] = panel_ref[
                        pl.ds(start, sub), c * tile:(c + 1) * tile].astype(BF16)


def cov(place, pieces, scale):
    count, size = pieces[0].shape
    tile, sub = size // 4, size // 16
    return pl.pallas_call(
        lambda *refs: cov_kernel(scale, *refs),
        out_shape=(jax.ShapeDtypeStruct((len(UPPER) * sub, tile), BF16),) * 4,
        in_specs=[SMEM] + [VMEM] * 4,
        out_specs=(VMEM,) * 4,
        scratch_shapes=[pltpu.VMEM((4 * count, size), BF16), pltpu.VMEM((tile, size), F32)],
        compiler_params=pltpu.CompilerParams(vmem_limit_bytes=16 * MIB),
    )(place, *pieces)


def rounds_kernel(place_ref, damp_ref, p0, p1, p2, p3, out_ref, a_ref, x_ref, xb_ref, p_ref):
    size = out_ref.shape[0]
    tile = size // 4
    sub = tile // 4
    base, damp = place_ref[0], damp_ref[0]
    for k, piece in enumerate((p0, p1, p2, p3)):
        start = pl.multiple_of(lax.rem(base + 4 - k, 4) * sub, sub)
        for t, (r, c) in enumerate(UPPER):
            a_ref[pl.ds(r * tile + start, sub), c * tile:(c + 1) * tile] = piece[t * sub:(t + 1) * sub, :]
    row = lax.broadcasted_iota(jnp.int32, (tile, tile), 0)
    col = lax.broadcasted_iota(jnp.int32, (tile, tile), 1)
    eye = row == col
    total = jnp.zeros((1, 1), F32)
    for r, c in UPPER:
        rows, cols = slice(r * tile, (r + 1) * tile), slice(c * tile, (c + 1) * tile)
        value = a_ref[rows, cols].astype(F32)
        if r == c:
            value = value + jnp.where(eye, damp, 0.0)
            a_ref[rows, cols] = value.astype(BF16)
            total += jnp.sum(value * value, keepdims=True)
        else:
            total += 2.0 * jnp.sum(value * value, keepdims=True)
            a_ref[cols, rows] = value.T.astype(BF16)
    frob = jnp.sqrt(total)
    inv = 1.0 / frob
    inv_bf = inv.astype(BF16).astype(F32)
    for r in range(4):
        rows = slice(r * tile, (r + 1) * tile)
        for c in range(4):
            cols = slice(c * tile, (c + 1) * tile)
            product = (a_ref[rows, cols].astype(F32) * inv_bf).astype(BF16).astype(F32)
            value = -product * inv_bf
            if r == c:
                value = value + jnp.where(eye, 2.0 * inv, 0.0)
            x_ref[rows, cols] = value
            xb_ref[0, rows, cols] = value.astype(BF16)
    for step in range(1, ITERS):
        now, later = (step - 1) % 2, step % 2
        for r in range(4):
            rows = slice(r * tile, (r + 1) * tile)
            p_ref[rows, :] = dot(a_ref[rows, :], xb_ref[now]).astype(BF16)
        for r in range(4):
            rows = slice(r * tile, (r + 1) * tile)
            value = 2.0 * x_ref[rows, :] - dot(p_ref[rows, :], xb_ref[now])
            if step < ITERS - 1:
                x_ref[rows, :] = value
                xb_ref[later, rows, :] = value.astype(BF16)
            else:
                out_ref[rows, :] = (value * (frob / 2.0 ** ITERS)).astype(BF16)


def rounds(place, damp, pieces):
    tile = pieces[0].shape[1]
    size = tile * 4
    return pl.pallas_call(
        rounds_kernel,
        out_shape=jax.ShapeDtypeStruct((size, size), BF16),
        in_specs=[SMEM, SMEM] + [VMEM] * 4,
        out_specs=VMEM,
        scratch_shapes=[
            pltpu.VMEM((size, size), BF16),
            pltpu.VMEM((size, size), F32),
            pltpu.VMEM((2, size, size), BF16),
            pltpu.VMEM((size, size), BF16),
        ],
        cost_estimate=pl.CostEstimate(flops=16 * size ** 3, transcendentals=0, bytes_accessed=4 * size * size),
        compiler_params=pltpu.CompilerParams(vmem_limit_bytes=24 * MIB),
    )(place, damp, *pieces)


def mix_kernel(place_ref, s_ref, w0, w1, w2, w3, t0_ref, t1_ref):
    tile, size = t0_ref.shape
    half = place_ref[2]

    @pl.when(place_ref[1] == 1)
    def _():
        for i, target in enumerate((t0_ref, t1_ref)):
            rows = pl.ds(pl.multiple_of((2 * half + i) * tile, tile), tile)
            value = jnp.zeros((tile, size), F32)
            for b, w in enumerate((w0, w1, w2, w3)):
                cols = pl.ds(pl.multiple_of(lax.rem(2 * half + b, 4) * tile, tile), tile)
                value += dot(s_ref[rows, cols], w[...])
            target[...] = value.astype(BF16)


def mix(place, inverse, weights):
    return pl.pallas_call(
        mix_kernel,
        out_shape=(jax.ShapeDtypeStruct(weights[0].shape, BF16),) * 2,
        in_specs=[SMEM] + [VMEM] * 5,
        out_specs=(VMEM,) * 2,
        compiler_params=pltpu.CompilerParams(vmem_limit_bytes=16 * MIB),
    )(place, inverse, *weights)


def last_kernel(place_ref, t0_ref, s_own, t1_ref, s_other, out_ref):
    @pl.when(place_ref[1] == 0)
    def _():
        out_ref[...] = dot(t0_ref[...], s_own[...]).astype(BF16)

    @pl.when(place_ref[1] == 1)
    def _():
        out_ref[...] = dot(t1_ref[...], s_other[...]).astype(BF16)


def last(place, t0, s_own, t1, s_other):
    return pl.pallas_call(
        last_kernel,
        out_shape=jax.ShapeDtypeStruct(t0.shape, BF16),
        in_specs=[SMEM] + [VMEM] * 4,
        out_specs=VMEM,
        compiler_params=pltpu.CompilerParams(vmem_limit_bytes=16 * MIB),
    )(place, t0, s_own, t1, s_other)


def pick(parts, index):
    return lax.dynamic_index_in_dim(parts, index, 0, keepdims=False)


def on_device(activations, out_grads, sample_ids, damping, weight_grad):
    d, o = lax.axis_index("dp"), lax.axis_index("owner")
    zh, y, core = d // 8, d // 2 % 4, d % 2
    x, zl = o // 4, o % 4
    size = weight_grad.shape[1]
    scale = 1.0 / (sample_ids.shape[0] * 256)
    is_g = core == 0

    hot = (sample_ids[:, None] == jnp.arange(activations.shape[0], dtype=jnp.int32)[None]).astype(BF16)
    samp_x = dot(hot, activations).astype(BF16)
    other_x = moved(samp_x, lambda zh, y, c, x, zl: (zh, y, 1, x, zl) if c == 0 else None)
    samp_g = dot(hot, out_grads).astype(BF16)
    other_g = moved(samp_g, lambda zh, y, c, x, zl: (zh, y, 0, x, zl) if c == 1 else None)

    packed = pack(x.reshape(1), samp_g, other_g, size)
    held = [packed[0]]
    for k in (2, 1, 3):
        held.append(moved(packed[k], lambda zh, y, c, x, zl: (zh, y, 0, (x + k) % 4, zl) if c == 0 else None))

    both_x = jnp.concatenate([samp_x, other_x])

    def over_z(zh, y, c, x, zl):
        z = (zh * 4 + zl + (-2 if zl < 2 else 2)) % 8
        return (z // 4, y, 1, x, z % 4) if c == 1 else None

    def columns(value, start, count):
        return lax.dynamic_slice_in_dim(value, start * size, count * size, 1)

    halves = jnp.concatenate([columns(both_x, zh * 2, 2), moved(columns(both_x, (1 - zh) * 2, 2), over_z)])
    kept = columns(halves, y // 2, 1)
    come = moved(columns(halves, 1 - y // 2, 1), lambda zh, y, c, x, zl: (zh, 3 - y, 1, x, zl) if c == 1 else None)

    samples = list(deal(jnp.stack([(zl + 2) % 4, core]), held, kept, come))
    for k in (2, 1, 3):
        samples[k] = moved(
            samples[k],
            lambda zh, y, c, x, zl: (z_shift(zh, zl, k)[0], y, 0, x, z_shift(zh, zl, k)[1]) if c == 0
            else (zh, y, 1, (x + k) % 4, zl),
        )

    chunks = cov(jnp.stack([jnp.where(is_g, y, x), 1 - core]), samples, scale)
    total = chunks[0].astype(F32)
    for k in (1, 2, 3):
        total += moved(
            chunks[k],
            lambda zh, y, c, x, zl: (zh, (y + k) % 4, 0, x, zl) if c == 0 else (zh, y, 1, x, (zl + k) % 4),
        ).astype(F32)
    part = total.astype(BF16)

    def beside(zh, zl, by):
        z = (zh * 4 + zl + by) % 8
        return z // 4, z % 4

    here = moved(part, lambda zh, y, c, x, zl: (beside(zh, zl, 2)[0], y, 0, x, beside(zh, zl, 2)[1]) if c == 0
                 else (zh, y ^ 1, 1, x, zl))
    there = moved(part, lambda zh, y, c, x, zl: (beside(zh, zl, -2)[0], y, 0, x, beside(zh, zl, -2)[1]) if c == 0
                  else None)
    piece = (here.astype(F32) + jnp.where(is_g, there, part).astype(F32)).astype(BF16)

    pieces = [piece]
    for k in (1, 2, 3):
        pieces.append(moved(
            piece,
            lambda zh, y, c, x, zl: (zh, (y + k) % 4, 0, x, zl) if c == 0 else (zh, y, 1, (x + k) % 4, zl),
        ))

    own_w, _ = lax.optimization_barrier((weight_grad, piece))
    weights = [
        moved(own_w, lambda zh, y, c, x, zl: (zh, y, 1, x, zl) if c == 0 else None),
        moved(own_w, lambda zh, y, c, x, zl: (zh, y ^ 1, 1, x, zl) if c == 0 else None),
        moved(own_w, lambda zh, y, c, x, zl: (zh, y ^ 1, 1, x, zl) if c == 1 else None),
    ]
    damp = pick(damping, jnp.where(is_g, BLOCKS_A + o, zh * 2 + y // 2)).reshape(1)
    place = jnp.stack([jnp.where(is_g, y, x), core, y % 2])
    inverse, *weights = lax.optimization_barrier((rounds(place, damp, pieces), *weights))
    weights.insert(1, weight_grad)

    inv_g = moved(inverse, lambda zh, y, c, x, zl: (zh, y, 1, x, zl) if c == 0 else None)
    mixed_0, mixed_1 = mix(place, inverse, weights)
    mixed_0 = moved(mixed_0, lambda zh, y, c, x, zl: (zh, y, 0, x, zl) if c == 1 else None)
    return last(place, mixed_0, inverse, mixed_1, inv_g)


def solution(mesh):
    placed = (
        P(("dp", "owner"), None),
        P(("dp", "owner"), None),
        P(("dp", "owner")),
        P(),
        P("dp", "owner"),
    )
    return jax.shard_map(
        on_device, mesh=mesh, in_specs=placed, out_specs=P("dp", "owner"), check_vma=False
    )
```

```python
import jax
import jax.numpy as jnp
from jax import lax
from jax.experimental import pallas as pl
from jax.experimental.pallas import tpu as pltpu
from jax.sharding import PartitionSpec as P

BLOCKS_A = 4
ITERS = 5
BF16 = jnp.bfloat16
F32 = jnp.float32
MIB = 2 ** 20
UPPER = [(r, c) for r in range(4) for c in range(r, 4)]
SMEM = pl.BlockSpec(memory_space=pltpu.SMEM)
VMEM = pl.BlockSpec(memory_space=pltpu.VMEM)


def dot(a, b):
    return jnp.dot(a, b, preferred_element_type=F32)


def gram(a, b):
    return lax.dot_general(a, b, (((0,), (0,)), ((), ())), preferred_element_type=F32)


def linear(zh, y, c, x, zl):
    return ((zh * 4 + y) * 2 + c) * 16 + x * 4 + zl


def moved(value, where):
    pairs = []
    for source in range(256):
        c, x, zl = source // 16 % 2, source // 4 % 4, source % 4
        zh, y = source // 128, source // 32 % 4
        target = where(zh, y, c, x, zl)
        if target is not None:
            pairs.append((source, linear(*target)))
    return lax.ppermute(value, ("dp", "owner"), pairs)


def z_shift(zh, zl, k):
    z = zh * 4 + zl
    z = (z + {1: 1, 2: 2 if z % 2 == 0 else -2, 3: -1}[k]) % 8
    return z // 4, z % 4


def pack_kernel(place_ref, mine_ref, other_ref, *outs):
    count, size = mine_ref.shape[0], outs[0].shape[1]
    for k, out in enumerate(outs):
        for zl in range(4):
            index = lax.rem(place_ref[0] + k, 4) * 4 + zl
            cols = pl.ds(pl.multiple_of(index * size, size), size)
            out[zl * 2 * count:(zl * 2 + 1) * count, :] = mine_ref[:, cols]
            out[(zl * 2 + 1) * count:(zl * 2 + 2) * count, :] = other_ref[:, cols]


def pack(place, mine, other, size):
    return pl.pallas_call(
        pack_kernel,
        out_shape=(jax.ShapeDtypeStruct((8 * mine.shape[0], size), BF16),) * 4,
        in_specs=[SMEM, VMEM, VMEM],
        out_specs=(VMEM,) * 4,
        compiler_params=pltpu.CompilerParams(vmem_limit_bytes=8 * MIB),
    )(place, mine, other)


def deal_kernel(place_ref, h0, h1, h2, h3, kept_ref, come_ref, *outs):
    rows = h0.shape[0] // 4
    half = kept_ref.shape[0]

    @pl.when(place_ref[1] == 0)
    def _():
        for k, out in enumerate(outs):
            start = pl.multiple_of(lax.rem(place_ref[0] + k, 4) * rows, rows)
            for i, held in enumerate((h0, h1, h2, h3)):
                out[i * rows:(i + 1) * rows, :] = held[pl.ds(start, rows), :]

    @pl.when(place_ref[1] == 1)
    def _():
        for out in outs:
            out[:half, :] = kept_ref[...]
            out[half:, :] = come_ref[...]


def deal(place, held, kept, come):
    return pl.pallas_call(
        deal_kernel,
        out_shape=(jax.ShapeDtypeStruct(held[0].shape, BF16),) * 4,
        in_specs=[SMEM] + [VMEM] * 6,
        out_specs=(VMEM,) * 4,
        compiler_params=pltpu.CompilerParams(vmem_limit_bytes=8 * MIB),
    )(place, *held, kept, come)


def cov_kernel(scale, place_ref, *refs):
    pieces, chunks, (all_ref, panel_ref) = refs[:4], refs[4:8], refs[8:]
    count, size = pieces[0].shape
    tile, sub = size // 4, size // 16
    for k, piece in enumerate(pieces):
        all_ref[k * count:(k + 1) * count, :] = piece[...]
    for r in range(4):
        cols = all_ref[:, r * tile:(r + 1) * tile]
        panel_ref[:, r * tile:] = gram(cols, all_ref[:, r * tile:]) * scale
        for k, chunk in enumerate(chunks):
            start = pl.multiple_of(lax.rem(place_ref[0] + k * place_ref[1], 4) * sub, sub)
            for t, (row, c) in enumerate(UPPER):
                if row == r:
                    chunk[t * sub:(t + 1) * sub, :] = panel_ref[
                        pl.ds(start, sub), c * tile:(c + 1) * tile].astype(BF16)


def cov(place, pieces, scale):
    count, size = pieces[0].shape
    tile, sub = size // 4, size // 16
    return pl.pallas_call(
        lambda *refs: cov_kernel(scale, *refs),
        out_shape=(jax.ShapeDtypeStruct((len(UPPER) * sub, tile), BF16),) * 4,
        in_specs=[SMEM] + [VMEM] * 4,
        out_specs=(VMEM,) * 4,
        scratch_shapes=[pltpu.VMEM((4 * count, size), BF16), pltpu.VMEM((tile, size), F32)],
        compiler_params=pltpu.CompilerParams(vmem_limit_bytes=16 * MIB),
    )(place, *pieces)


def rounds_kernel(place_ref, damp_ref, p0, p1, p2, p3, out_ref, a_ref, x_ref, xb_ref, p_ref):
    size = out_ref.shape[0]
    tile = size // 4
    sub = tile // 4
    base, damp = place_ref[0], damp_ref[0]
    blocks = [slice(i * tile, (i + 1) * tile) for i in range(4)]

    def mirrored(ref, c, value):
        ref[:(c + 1) * tile, blocks[c]] = value
        for r in range(c):
            ref[blocks[c], blocks[r]] = value[blocks[r], :].T

    for k, piece in enumerate((p0, p1, p2, p3)):
        start = pl.multiple_of(lax.rem(base + 4 - k, 4) * sub, sub)
        for t, (r, c) in enumerate(UPPER):
            a_ref[pl.ds(r * tile + start, sub), blocks[c]] = piece[t * sub:(t + 1) * sub, :]
    row = lax.broadcasted_iota(jnp.int32, (tile, tile), 0)
    col = lax.broadcasted_iota(jnp.int32, (tile, tile), 1)
    eye = row == col
    total = jnp.zeros((1, 1), F32)
    for r, c in UPPER:
        value = a_ref[blocks[r], blocks[c]].astype(F32)
        if r == c:
            value = value + jnp.where(eye, damp, 0.0)
            a_ref[blocks[r], blocks[c]] = value.astype(BF16)
            total += jnp.sum(value * value, keepdims=True)
        else:
            total += 2.0 * jnp.sum(value * value, keepdims=True)
            a_ref[blocks[c], blocks[r]] = a_ref[blocks[r], blocks[c]].T
    frob = jnp.sqrt(total)
    inv = 1.0 / frob
    inv_bf = inv.astype(BF16).astype(F32)
    for r in range(4):
        for c in range(4):
            product = (a_ref[blocks[r], blocks[c]].astype(F32) * inv_bf).astype(BF16).astype(F32)
            value = -product * inv_bf
            if r == c:
                value = value + jnp.where(eye, 2.0 * inv, 0.0)
            if r <= c:
                x_ref[blocks[r], blocks[c]] = value
            xb_ref[0, blocks[r], blocks[c]] = value.astype(BF16)
    for step in range(1, ITERS):
        now, later = xb_ref.at[(step - 1) % 2], xb_ref.at[step % 2]
        for c in (3, 2, 1, 0):
            mirrored(p_ref, c, dot(a_ref[:(c + 1) * tile, :], now[:, blocks[c]]).astype(BF16))
        for c in range(4):
            rows = slice(0, (c + 1) * tile)
            value = 2.0 * x_ref[rows, blocks[c]] - dot(p_ref[rows, :], now[:, blocks[c]])
            if step < ITERS - 1:
                x_ref[rows, blocks[c]] = value
                mirrored(later, c, value.astype(BF16))
            else:
                mirrored(out_ref, c, (value * (frob / 2.0 ** ITERS)).astype(BF16))


def rounds(place, damp, pieces):
    tile = pieces[0].shape[1]
    size = tile * 4
    return pl.pallas_call(
        rounds_kernel,
        out_shape=jax.ShapeDtypeStruct((size, size), BF16),
        in_specs=[SMEM, SMEM] + [VMEM] * 4,
        out_specs=VMEM,
        scratch_shapes=[
            pltpu.VMEM((size, size), BF16),
            pltpu.VMEM((size, size), F32),
            pltpu.VMEM((2, size, size), BF16),
            pltpu.VMEM((size, size), BF16),
        ],
        cost_estimate=pl.CostEstimate(flops=16 * size ** 3, transcendentals=0, bytes_accessed=4 * size * size),
        compiler_params=pltpu.CompilerParams(vmem_limit_bytes=24 * MIB),
    )(place, damp, *pieces)


def mix_kernel(place_ref, s_ref, w0, w1, w2, w3, out_ref, t_ref):
    tile, size = w0.shape
    half = place_ref[2]

    @pl.when(place_ref[1] == 1)
    def _():
        for i in range(2):
            rows = pl.ds(pl.multiple_of((2 * half + i) * tile, tile), tile)
            value = jnp.zeros((tile, size), F32)
            for b, w in enumerate((w0, w1, w2, w3)):
                cols = pl.ds(pl.multiple_of(lax.rem(2 * half + b, 4) * tile, tile), tile)
                value += dot(s_ref[rows, cols], w[...])
            t_ref[i * tile:(i + 1) * tile, :] = value.astype(BF16)
        out_ref[:2 * tile, :] = t_ref[...]


def mix(place, inverse, weights):
    tile, size = weights[0].shape
    return pl.pallas_call(
        mix_kernel,
        out_shape=jax.ShapeDtypeStruct(inverse.shape, BF16),
        in_specs=[SMEM] + [VMEM] * 5,
        out_specs=VMEM,
        scratch_shapes=[pltpu.VMEM((2 * tile, size), BF16)],
        input_output_aliases={1: 0},
        compiler_params=pltpu.CompilerParams(vmem_limit_bytes=16 * MIB),
    )(place, inverse, *weights)


def last_kernel(place_ref, mine_ref, other_ref, out_ref):
    tile = out_ref.shape[0]

    @pl.when(place_ref[1] == 0)
    def _():
        out_ref[...] = dot(other_ref[:tile, :], mine_ref[...]).astype(BF16)

    @pl.when(place_ref[1] == 1)
    def _():
        out_ref[...] = dot(mine_ref[tile:2 * tile, :], other_ref[...]).astype(BF16)


def last(place, mine, other, rows):
    return pl.pallas_call(
        last_kernel,
        out_shape=jax.ShapeDtypeStruct((rows, mine.shape[1]), BF16),
        in_specs=[SMEM] + [VMEM] * 2,
        out_specs=VMEM,
        compiler_params=pltpu.CompilerParams(vmem_limit_bytes=16 * MIB),
    )(place, mine, other)


def pick(parts, index):
    return lax.dynamic_index_in_dim(parts, index, 0, keepdims=False)


def on_device(activations, out_grads, sample_ids, damping, weight_grad):
    d, o = lax.axis_index("dp"), lax.axis_index("owner")
    zh, y, core = d // 8, d // 2 % 4, d % 2
    x, zl = o // 4, o % 4
    size = weight_grad.shape[1]
    scale = 1.0 / (sample_ids.shape[0] * 256)
    is_g = core == 0

    hot = (sample_ids[:, None] == jnp.arange(activations.shape[0], dtype=jnp.int32)[None]).astype(BF16)
    samp_x = dot(hot, activations).astype(BF16)
    other_x = moved(samp_x, lambda zh, y, c, x, zl: (zh, y, 1, x, zl) if c == 0 else None)
    out_grads, _ = lax.optimization_barrier((out_grads, samp_x))
    samp_g = dot(hot, out_grads).astype(BF16)
    other_g = moved(samp_g, lambda zh, y, c, x, zl: (zh, y, 0, x, zl) if c == 1 else None)

    packed = pack(x.reshape(1), samp_g, other_g, size)
    held = [packed[0]]
    for k in (1, 2, 3):
        held.append(moved(packed[k], lambda zh, y, c, x, zl: (zh, y, 0, (x + k) % 4, zl) if c == 0 else None))

    both_x = jnp.concatenate([samp_x, other_x])

    def over_z(zh, y, c, x, zl):
        z = (zh * 4 + zl + (-2 if zl < 2 else 2)) % 8
        return (z // 4, y, 1, x, z % 4) if c == 1 else None

    def columns(value, start, count):
        return lax.dynamic_slice_in_dim(value, start * size, count * size, 1)

    halves = jnp.concatenate([columns(both_x, zh * 2, 2), moved(columns(both_x, (1 - zh) * 2, 2), over_z)])
    kept = columns(halves, y // 2, 1)
    come = moved(columns(halves, 1 - y // 2, 1), lambda zh, y, c, x, zl: (zh, 3 - y, 1, x, zl) if c == 1 else None)

    samples = list(deal(jnp.stack([(zl + 2) % 4, core]), held, kept, come))
    for k in (1, 2, 3):
        samples[k] = moved(
            samples[k],
            lambda zh, y, c, x, zl: (z_shift(zh, zl, k)[0], y, 0, x, z_shift(zh, zl, k)[1]) if c == 0
            else (zh, y, 1, (x + k) % 4, zl),
        )

    chunks = cov(jnp.stack([jnp.where(is_g, y, x), 1 - core]), samples, scale)
    total = chunks[0].astype(F32)
    for k in (1, 2, 3):
        total += moved(
            chunks[k],
            lambda zh, y, c, x, zl: (zh, (y + k) % 4, 0, x, zl) if c == 0 else (zh, y, 1, x, (zl + k) % 4),
        ).astype(F32)
    part = total.astype(BF16)

    def beside(zh, zl, by):
        z = (zh * 4 + zl + by) % 8
        return z // 4, z % 4

    here = moved(part, lambda zh, y, c, x, zl: (beside(zh, zl, 2)[0], y, 0, x, beside(zh, zl, 2)[1]) if c == 0
                 else (zh, y ^ 1, 1, x, zl))
    there = moved(part, lambda zh, y, c, x, zl: (beside(zh, zl, -2)[0], y, 0, x, beside(zh, zl, -2)[1]) if c == 0
                  else None)
    piece = (here.astype(F32) + jnp.where(is_g, there, part).astype(F32)).astype(BF16)

    pieces = [piece]
    for k in (1, 2, 3):
        pieces.append(moved(
            piece,
            lambda zh, y, c, x, zl: (zh, (y + k) % 4, 0, x, zl) if c == 0 else (zh, y, 1, (x + k) % 4, zl),
        ))

    own_w, _ = lax.optimization_barrier((weight_grad, piece))
    weights = [
        moved(own_w, lambda zh, y, c, x, zl: (zh, y, 1, x, zl) if c == 0 else None),
        moved(own_w, lambda zh, y, c, x, zl: (zh, y ^ 1, 1, x, zl) if c == 0 else None),
        moved(own_w, lambda zh, y, c, x, zl: (zh, y ^ 1, 1, x, zl) if c == 1 else None),
    ]
    damp = pick(damping, jnp.where(is_g, BLOCKS_A + o, zh * 2 + y // 2)).reshape(1)
    place = jnp.stack([jnp.where(is_g, y, x), core, y % 2])
    inverse, *weights = lax.optimization_barrier((rounds(place, damp, pieces), *weights))
    weights.insert(1, weight_grad)

    mine = mix(place, inverse, weights)
    other = moved(mine, lambda zh, y, c, x, zl: (zh, y, 1 - c, x, zl))
    return last(place, mine, other, weight_grad.shape[0])


def solution(mesh):
    placed = (
        P(("dp", "owner"), None),
        P(("dp", "owner"), None),
        P(("dp", "owner")),
        P(),
        P("dp", "owner"),
    )
    return jax.shard_map(
        on_device, mesh=mesh, in_specs=placed, out_specs=P("dp", "owner"), check_vma=False
    )
```

```python
import jax
import jax.numpy as jnp
from jax import lax
from jax.experimental import pallas as pl
from jax.experimental.pallas import tpu as pltpu
from jax.sharding import PartitionSpec as P

BLOCKS_A = 4
ITERS = 5
BF16 = jnp.bfloat16
F32 = jnp.float32
MIB = 2 ** 20
UPPER = [(r, c) for r in range(4) for c in range(r, 4)]
SMEM = pl.BlockSpec(memory_space=pltpu.SMEM)
VMEM = pl.BlockSpec(memory_space=pltpu.VMEM)


def dot(a, b):
    return jnp.dot(a, b, preferred_element_type=F32)


def gram(a, b):
    return lax.dot_general(a, b, (((0,), (0,)), ((), ())), preferred_element_type=F32)


def linear(zh, y, c, x, zl):
    return ((zh * 4 + y) * 2 + c) * 16 + x * 4 + zl


def moved(value, where):
    pairs = []
    for source in range(256):
        c, x, zl = source // 16 % 2, source // 4 % 4, source % 4
        zh, y = source // 128, source // 32 % 4
        target = where(zh, y, c, x, zl)
        pairs.append((source, source if target is None else linear(*target)))
    assert len({target for _, target in pairs}) == 256
    return lax.ppermute(value, ("dp", "owner"), pairs)


def z_shift(zh, zl, k):
    z = zh * 4 + zl
    z = (z + {1: 1, 2: 2 if z % 2 == 0 else -2, 3: -1}[k]) % 8
    return z // 4, z % 4


def offer_kernel(core_ref, x_ref, g_ref, out_ref):
    @pl.when(core_ref[0] == 0)
    def _():
        out_ref[:, :x_ref.shape[1]] = x_ref[...]
        out_ref[:, x_ref.shape[1]:] = jnp.zeros((x_ref.shape[0], out_ref.shape[1] - x_ref.shape[1]), BF16)

    @pl.when(core_ref[0] == 1)
    def _():
        out_ref[...] = g_ref[...]


def offer(core, samp_x, samp_g):
    return pl.pallas_call(
        offer_kernel,
        out_shape=jax.ShapeDtypeStruct(samp_g.shape, BF16),
        in_specs=[SMEM, VMEM, VMEM],
        out_specs=VMEM,
        compiler_params=pltpu.CompilerParams(vmem_limit_bytes=8 * MIB),
    )(core, samp_x, samp_g)


def pack_kernel(place_ref, mine_ref, other_ref, *outs):
    count, size = mine_ref.shape[0], outs[0].shape[1]
    for k, out in enumerate(outs):
        for zl in range(4):
            index = lax.rem(place_ref[0] + k, 4) * 4 + zl
            cols = pl.ds(pl.multiple_of(index * size, size), size)
            out[zl * 2 * count:(zl * 2 + 1) * count, :] = mine_ref[:, cols]
            out[(zl * 2 + 1) * count:(zl * 2 + 2) * count, :] = other_ref[:, cols]


def pack(place, mine, other, size):
    return pl.pallas_call(
        pack_kernel,
        out_shape=(jax.ShapeDtypeStruct((8 * mine.shape[0], size), BF16),) * 4,
        in_specs=[SMEM, VMEM, VMEM],
        out_specs=(VMEM,) * 4,
        compiler_params=pltpu.CompilerParams(vmem_limit_bytes=8 * MIB),
    )(place, mine, other)


def deal_kernel(place_ref, h0, h1, h2, h3, kept_ref, come_ref, *outs):
    rows = h0.shape[0] // 4
    half = kept_ref.shape[0]

    @pl.when(place_ref[1] == 0)
    def _():
        for k, out in enumerate(outs):
            start = pl.multiple_of(lax.rem(place_ref[0] + k, 4) * rows, rows)
            for i, held in enumerate((h0, h1, h2, h3)):
                out[i * rows:(i + 1) * rows, :] = held[pl.ds(start, rows), :]

    @pl.when(place_ref[1] == 1)
    def _():
        for out in outs:
            out[:half, :] = kept_ref[...]
            out[half:, :] = come_ref[...]


def deal(place, held, kept, come):
    return pl.pallas_call(
        deal_kernel,
        out_shape=(jax.ShapeDtypeStruct(held[0].shape, BF16),) * 4,
        in_specs=[SMEM] + [VMEM] * 6,
        out_specs=(VMEM,) * 4,
        compiler_params=pltpu.CompilerParams(vmem_limit_bytes=8 * MIB),
    )(place, *held, kept, come)


def cov_kernel(scale, place_ref, *refs):
    pieces, chunks, (all_ref, panel_ref) = refs[:4], refs[4:8], refs[8:]
    count, size = pieces[0].shape
    tile, sub = size // 4, size // 16
    for k, piece in enumerate(pieces):
        all_ref[k * count:(k + 1) * count, :] = piece[...]
    for r in range(4):
        cols = all_ref[:, r * tile:(r + 1) * tile]
        panel_ref[:, r * tile:] = gram(cols, all_ref[:, r * tile:]) * scale
        for k, chunk in enumerate(chunks):
            start = pl.multiple_of(lax.rem(place_ref[0] + k * place_ref[1], 4) * sub, sub)
            for t, (row, c) in enumerate(UPPER):
                if row == r:
                    chunk[t * sub:(t + 1) * sub, :] = panel_ref[
                        pl.ds(start, sub), c * tile:(c + 1) * tile].astype(BF16)


def cov(place, pieces, scale):
    count, size = pieces[0].shape
    tile, sub = size // 4, size // 16
    return pl.pallas_call(
        lambda *refs: cov_kernel(scale, *refs),
        out_shape=(jax.ShapeDtypeStruct((len(UPPER) * sub, tile), BF16),) * 4,
        in_specs=[SMEM] + [VMEM] * 4,
        out_specs=(VMEM,) * 4,
        scratch_shapes=[pltpu.VMEM((4 * count, size), BF16), pltpu.VMEM((tile, size), F32)],
        compiler_params=pltpu.CompilerParams(vmem_limit_bytes=16 * MIB),
    )(place, *pieces)


def rounds_kernel(place_ref, damp_ref, p0, p1, p2, p3, out_ref, a_ref, x_ref, xb_ref, p_ref):
    size = out_ref.shape[0]
    tile = size // 4
    sub = tile // 4
    base, damp = place_ref[0], damp_ref[0]
    blocks = [slice(i * tile, (i + 1) * tile) for i in range(4)]

    def mirrored(ref, c, value):
        ref[:(c + 1) * tile, blocks[c]] = value
        for r in range(c):
            ref[blocks[c], blocks[r]] = value[blocks[r], :].T

    for k, piece in enumerate((p0, p1, p2, p3)):
        start = pl.multiple_of(lax.rem(base + 4 - k, 4) * sub, sub)
        for t, (r, c) in enumerate(UPPER):
            a_ref[pl.ds(r * tile + start, sub), blocks[c]] = piece[t * sub:(t + 1) * sub, :]
    row = lax.broadcasted_iota(jnp.int32, (tile, tile), 0)
    col = lax.broadcasted_iota(jnp.int32, (tile, tile), 1)
    eye = row == col
    total = jnp.zeros((1, 1), F32)
    for r, c in UPPER:
        value = a_ref[blocks[r], blocks[c]].astype(F32)
        if r == c:
            value = value + jnp.where(eye, damp, 0.0)
            a_ref[blocks[r], blocks[c]] = value.astype(BF16)
            total += jnp.sum(value * value, keepdims=True)
        else:
            total += 2.0 * jnp.sum(value * value, keepdims=True)
            a_ref[blocks[c], blocks[r]] = a_ref[blocks[r], blocks[c]].T
    frob = jnp.sqrt(total)
    inv = 1.0 / frob
    inv_bf = inv.astype(BF16).astype(F32)
    for r in range(4):
        for c in range(4):
            product = (a_ref[blocks[r], blocks[c]].astype(F32) * inv_bf).astype(BF16).astype(F32)
            value = -product * inv_bf
            if r == c:
                value = value + jnp.where(eye, 2.0 * inv, 0.0)
            if r <= c:
                x_ref[blocks[r], blocks[c]] = value
            xb_ref[0, blocks[r], blocks[c]] = value.astype(BF16)
    for step in range(1, ITERS):
        now, later = xb_ref.at[(step - 1) % 2], xb_ref.at[step % 2]
        for c in (3, 2, 1, 0):
            mirrored(p_ref, c, dot(a_ref[:(c + 1) * tile, :], now[:, blocks[c]]).astype(BF16))
        for c in range(4):
            rows = slice(0, (c + 1) * tile)
            value = 2.0 * x_ref[rows, blocks[c]] - dot(p_ref[rows, :], now[:, blocks[c]])
            if step < ITERS - 1:
                x_ref[rows, blocks[c]] = value
                mirrored(later, c, value.astype(BF16))
            else:
                mirrored(out_ref, c, (value * (frob / 2.0 ** ITERS)).astype(BF16))


def rounds(place, damp, pieces):
    tile = pieces[0].shape[1]
    size = tile * 4
    return pl.pallas_call(
        rounds_kernel,
        out_shape=jax.ShapeDtypeStruct((size, size), BF16),
        in_specs=[SMEM, SMEM] + [VMEM] * 4,
        out_specs=VMEM,
        scratch_shapes=[
            pltpu.VMEM((size, size), BF16),
            pltpu.VMEM((size, size), F32),
            pltpu.VMEM((2, size, size), BF16),
            pltpu.VMEM((size, size), BF16),
        ],
        cost_estimate=pl.CostEstimate(flops=16 * size ** 3, transcendentals=0, bytes_accessed=4 * size * size),
        compiler_params=pltpu.CompilerParams(vmem_limit_bytes=24 * MIB),
    )(place, damp, *pieces)


def mix_kernel(place_ref, s_ref, w0, w1, w2, w3, out_ref, t_ref):
    tile, size = w0.shape
    half = place_ref[2]

    @pl.when(place_ref[1] == 1)
    def _():
        for i in range(2):
            rows = pl.ds(pl.multiple_of((2 * half + i) * tile, tile), tile)
            value = jnp.zeros((tile, size), F32)
            for b, w in enumerate((w0, w1, w2, w3)):
                cols = pl.ds(pl.multiple_of(lax.rem(2 * half + b, 4) * tile, tile), tile)
                value += dot(s_ref[rows, cols], w[...])
            t_ref[i * tile:(i + 1) * tile, :] = value.astype(BF16)
        out_ref[:2 * tile, :] = t_ref[...]


def mix(place, inverse, weights):
    tile, size = weights[0].shape
    return pl.pallas_call(
        mix_kernel,
        out_shape=jax.ShapeDtypeStruct(inverse.shape, BF16),
        in_specs=[SMEM] + [VMEM] * 5,
        out_specs=VMEM,
        scratch_shapes=[pltpu.VMEM((2 * tile, size), BF16)],
        input_output_aliases={1: 0},
        compiler_params=pltpu.CompilerParams(vmem_limit_bytes=16 * MIB),
    )(place, inverse, *weights)


def last_kernel(place_ref, mine_ref, other_ref, out_ref):
    tile = out_ref.shape[0]

    @pl.when(place_ref[1] == 0)
    def _():
        out_ref[...] = dot(other_ref[:tile, :], mine_ref[...]).astype(BF16)

    @pl.when(place_ref[1] == 1)
    def _():
        out_ref[...] = dot(mine_ref[tile:2 * tile, :], other_ref[...]).astype(BF16)


def last(place, mine, other, rows):
    return pl.pallas_call(
        last_kernel,
        out_shape=jax.ShapeDtypeStruct((rows, mine.shape[1]), BF16),
        in_specs=[SMEM] + [VMEM] * 2,
        out_specs=VMEM,
        compiler_params=pltpu.CompilerParams(vmem_limit_bytes=16 * MIB),
    )(place, mine, other)


def pick(parts, index):
    return lax.dynamic_index_in_dim(parts, index, 0, keepdims=False)


def on_device(activations, out_grads, sample_ids, damping, weight_grad):
    d, o = lax.axis_index("dp"), lax.axis_index("owner")
    zh, y, core = d // 8, d // 2 % 4, d % 2
    x, zl = o // 4, o % 4
    size = weight_grad.shape[1]
    scale = 1.0 / (sample_ids.shape[0] * 256)
    is_g = core == 0

    hot = (sample_ids[:, None] == jnp.arange(activations.shape[0], dtype=jnp.int32)[None]).astype(BF16)
    samp_g = dot(hot, out_grads).astype(BF16)
    activations, _ = lax.optimization_barrier((activations, samp_g))
    samp_x = dot(hot, activations).astype(BF16)
    other = moved(offer(core.reshape(1), samp_x, samp_g), lambda zh, y, c, x, zl: (zh, y, 1 - c, x, zl))

    packed = pack(x.reshape(1), samp_g, other, size)
    held = [packed[0]]
    for k in (1, 2, 3):
        held.append(moved(packed[k], lambda zh, y, c, x, zl: (zh, y, 0, (x + k) % 4, zl) if c == 0 else None))

    both_x = jnp.concatenate([samp_x, other[:, :4 * size]])

    def over_z(zh, y, c, x, zl):
        z = (zh * 4 + zl + (-2 if zl < 2 else 2)) % 8
        return (z // 4, y, 1, x, z % 4) if c == 1 else None

    def columns(value, start, count):
        return lax.dynamic_slice_in_dim(value, start * size, count * size, 1)

    halves = jnp.concatenate([columns(both_x, zh * 2, 2), moved(columns(both_x, (1 - zh) * 2, 2), over_z)])
    kept = columns(halves, y // 2, 1)
    come = moved(columns(halves, 1 - y // 2, 1), lambda zh, y, c, x, zl: (zh, 3 - y, 1, x, zl) if c == 1 else None)

    samples = list(deal(jnp.stack([(zl + 2) % 4, core]), held, kept, come))
    for k in (1, 2, 3):
        samples[k] = moved(
            samples[k],
            lambda zh, y, c, x, zl: (z_shift(zh, zl, k)[0], y, 0, x, z_shift(zh, zl, k)[1]) if c == 0
            else (zh, y, 1, (x + k) % 4, zl),
        )

    chunks = cov(jnp.stack([jnp.where(is_g, y, x), 1 - core]), samples, scale)
    total = chunks[0].astype(F32)
    for k in (1, 2, 3):
        total += moved(
            chunks[k],
            lambda zh, y, c, x, zl: (zh, (y + k) % 4, 0, x, zl) if c == 0 else (zh, y, 1, x, (zl + k) % 4),
        ).astype(F32)
    part = total.astype(BF16)

    def beside(zh, zl, by):
        z = (zh * 4 + zl + by) % 8
        return z // 4, z % 4

    here = moved(part, lambda zh, y, c, x, zl: (beside(zh, zl, 2)[0], y, 0, x, beside(zh, zl, 2)[1]) if c == 0
                 else (zh, y ^ 1, 1, x, zl))
    there = moved(part, lambda zh, y, c, x, zl: (beside(zh, zl, -2)[0], y, 0, x, beside(zh, zl, -2)[1]) if c == 0
                  else None)
    piece = (here.astype(F32) + there.astype(F32)).astype(BF16)

    pieces = [piece]
    for k in (1, 2, 3):
        pieces.append(moved(
            piece,
            lambda zh, y, c, x, zl: (zh, (y + k) % 4, 0, x, zl) if c == 0 else (zh, y, 1, (x + k) % 4, zl),
        ))

    own_w, _ = lax.optimization_barrier((weight_grad, piece))
    weights = [
        moved(own_w, lambda zh, y, c, x, zl: (zh, y, 1 - c, x, zl)),
        moved(own_w, lambda zh, y, c, x, zl: (zh, y ^ 1, 1, x, zl) if c == 0 else (zh, y, 0, x, zl)),
        moved(own_w, lambda zh, y, c, x, zl: (zh, y ^ 1, 1, x, zl) if c == 1 else None),
    ]
    damp = pick(damping, jnp.where(is_g, BLOCKS_A + o, zh * 2 + y // 2)).reshape(1)
    place = jnp.stack([jnp.where(is_g, y, x), core, y % 2])
    inverse, *weights = lax.optimization_barrier((rounds(place, damp, pieces), *weights))
    weights.insert(1, weight_grad)

    mine = mix(place, inverse, weights)
    other = moved(mine, lambda zh, y, c, x, zl: (zh, y, 1 - c, x, zl))
    return last(place, mine, other, weight_grad.shape[0])


def solution(mesh):
    placed = (
        P(("dp", "owner"), None),
        P(("dp", "owner"), None),
        P(("dp", "owner")),
        P(),
        P("dp", "owner"),
    )
    return jax.shard_map(
        on_device, mesh=mesh, in_specs=placed, out_specs=P("dp", "owner"), check_vma=False
    )
```

```python
import jax
import jax.numpy as jnp
from jax import lax
from jax.experimental import pallas as pl
from jax.experimental.pallas import tpu as pltpu
from jax.sharding import PartitionSpec as P

BLOCKS_A = 4
ITERS = 5
BF16 = jnp.bfloat16
F32 = jnp.float32
MIB = 2 ** 20
UPPER = [(r, c) for r in range(4) for c in range(r, 4)]
SMEM = pl.BlockSpec(memory_space=pltpu.SMEM)
VMEM = pl.BlockSpec(memory_space=pltpu.VMEM)


def dot(a, b):
    return jnp.dot(a, b, preferred_element_type=F32)


def gram(a, b):
    return lax.dot_general(a, b, (((0,), (0,)), ((), ())), preferred_element_type=F32)


def linear(zh, y, c, x, zl):
    return ((zh * 4 + y) * 2 + c) * 16 + x * 4 + zl


def moved(value, where):
    pairs = []
    for source in range(256):
        c, x, zl = source // 16 % 2, source // 4 % 4, source % 4
        zh, y = source // 128, source // 32 % 4
        target = where(zh, y, c, x, zl)
        pairs.append((source, source if target is None else linear(*target)))
    assert len({target for _, target in pairs}) == 256
    return lax.ppermute(value, ("dp", "owner"), pairs)


def dealt(value, group_of):
    groups = []
    for device in range(256):
        c, x, zl = device // 16 % 2, device // 4 % 4, device % 4
        members = [linear(*member) for member in group_of(device // 128, device // 32 % 4, c, x, zl)]
        assert device in members
        if device == min(members):
            groups.append(members)
    assert sorted(sum(groups, [])) == list(range(256))
    return lax.all_to_all(
        value, ("dp", "owner"), split_axis=0, concat_axis=0, tiled=True, axis_index_groups=groups)


def over_x(zh, y, c, x, zl):
    return [(zh, y, c, i, zl) for i in range(4)]


def over_y(zh, y, c, x, zl):
    return [(zh, i, c, x, zl) for i in range(4)]


def over_zl(zh, y, c, x, zl):
    return [(zh, y, c, x, i) for i in range(4)]


def over_blocks(zh, y, c, x, zl):
    z = (zh * 4 + zl + (-2 if zl < 2 else 2)) % 8
    places = {zh: (zh, zl), 1 - zh: (z // 4, z % 4)}
    return [(places[h][0], y if y // 2 == g else 3 - y, c, x, places[h][1]) for h in range(2) for g in range(2)]


def z_shift(zh, zl, k):
    z = zh * 4 + zl
    z = (z + {1: 1, 2: 2 if z % 2 == 0 else -2, 3: -1}[k]) % 8
    return z // 4, z % 4


def offer_kernel(core_ref, x_ref, g_ref, out_ref):
    @pl.when(core_ref[0] == 0)
    def _():
        out_ref[:, :x_ref.shape[1]] = x_ref[...]
        out_ref[:, x_ref.shape[1]:] = jnp.zeros((x_ref.shape[0], out_ref.shape[1] - x_ref.shape[1]), BF16)

    @pl.when(core_ref[0] == 1)
    def _():
        out_ref[...] = g_ref[...]


def offer(core, samp_x, samp_g):
    return pl.pallas_call(
        offer_kernel,
        out_shape=jax.ShapeDtypeStruct(samp_g.shape, BF16),
        in_specs=[SMEM, VMEM, VMEM],
        out_specs=VMEM,
        compiler_params=pltpu.CompilerParams(vmem_limit_bytes=8 * MIB),
    )(core, samp_x, samp_g)


def pack_kernel(core_ref, x_ref, g_ref, other_ref, out_ref):
    count, size = x_ref.shape[0], out_ref.shape[2]

    @pl.when(core_ref[0] == 0)
    def _():
        for i in range(4):
            for zl in range(4):
                cols = slice((i * 4 + zl) * size, (i * 4 + zl + 1) * size)
                out_ref[i, zl * 2 * count:(zl * 2 + 1) * count, :] = g_ref[:, cols]
                out_ref[i, (zl * 2 + 1) * count:(zl * 2 + 2) * count, :] = other_ref[:, cols]

    @pl.when(core_ref[0] == 1)
    def _():
        for i in range(4):
            cols = slice(i * size, (i + 1) * size)
            out_ref[i, :count, :] = x_ref[:, cols]
            out_ref[i, count:2 * count, :] = other_ref[:, cols]
            out_ref[i, 2 * count:, :] = jnp.zeros((6 * count, size), BF16)


def pack(core, samp_x, samp_g, other, size):
    return pl.pallas_call(
        pack_kernel,
        out_shape=jax.ShapeDtypeStruct((4, 8 * samp_x.shape[0], size), BF16),
        in_specs=[SMEM] + [VMEM] * 3,
        out_specs=VMEM,
        compiler_params=pltpu.CompilerParams(vmem_limit_bytes=8 * MIB),
    )(core, samp_x, samp_g, other)


def deal_kernel(place_ref, held_ref, *outs):
    rows = held_ref.shape[1] // 4
    for k, out in enumerate(outs):
        start = pl.multiple_of(lax.rem(place_ref[0] + k * place_ref[1], 4) * rows, rows)
        for i in range(4):
            out[i * rows:(i + 1) * rows, :] = held_ref[i, pl.ds(start, rows), :]


def deal(place, held):
    return pl.pallas_call(
        deal_kernel,
        out_shape=(jax.ShapeDtypeStruct(held.shape[1:], BF16),) * 4,
        in_specs=[SMEM, VMEM],
        out_specs=(VMEM,) * 4,
        compiler_params=pltpu.CompilerParams(vmem_limit_bytes=8 * MIB),
    )(place, held)


def cov_kernel(scale, place_ref, *refs):
    pieces, chunks, (all_ref, panel_ref) = refs[:4], [refs[4].at[i] for i in range(4)], refs[5:]
    count, size = pieces[0].shape
    tile, sub = size // 4, size // 16
    for k, piece in enumerate(pieces):
        all_ref[k * count:(k + 1) * count, :] = piece[...]
    for r in range(4):
        cols = all_ref[:, r * tile:(r + 1) * tile]
        panel_ref[:, r * tile:] = gram(cols, all_ref[:, r * tile:]) * scale
        for k, chunk in enumerate(chunks):
            start = pl.multiple_of(lax.rem(place_ref[0] + k * place_ref[1], 4) * sub, sub)
            for t, (row, c) in enumerate(UPPER):
                if row == r:
                    chunk[t * sub:(t + 1) * sub, :] = panel_ref[
                        pl.ds(start, sub), c * tile:(c + 1) * tile].astype(BF16)


def cov(place, pieces, scale):
    count, size = pieces[0].shape
    tile, sub = size // 4, size // 16
    return pl.pallas_call(
        lambda *refs: cov_kernel(scale, *refs),
        out_shape=jax.ShapeDtypeStruct((4, len(UPPER) * sub, tile), BF16),
        in_specs=[SMEM] + [VMEM] * 4,
        out_specs=VMEM,
        scratch_shapes=[pltpu.VMEM((4 * count, size), BF16), pltpu.VMEM((tile, size), F32)],
        compiler_params=pltpu.CompilerParams(vmem_limit_bytes=16 * MIB),
    )(place, *pieces)


def rounds_kernel(damp_ref, pieces_ref, out_ref, a_ref, x_ref, xb_ref, p_ref):
    size = out_ref.shape[0]
    tile = size // 4
    sub = tile // 4
    damp = damp_ref[0]
    blocks = [slice(i * tile, (i + 1) * tile) for i in range(4)]

    def mirrored(ref, c, value):
        ref[:(c + 1) * tile, blocks[c]] = value
        for r in range(c):
            ref[blocks[c], blocks[r]] = value[blocks[r], :].T

    for i in range(4):
        for t, (r, c) in enumerate(UPPER):
            a_ref[r * tile + i * sub:r * tile + (i + 1) * sub, blocks[c]] = pieces_ref[i, t * sub:(t + 1) * sub, :]
    row = lax.broadcasted_iota(jnp.int32, (tile, tile), 0)
    col = lax.broadcasted_iota(jnp.int32, (tile, tile), 1)
    eye = row == col
    total = jnp.zeros((1, 1), F32)
    for r, c in UPPER:
        value = a_ref[blocks[r], blocks[c]].astype(F32)
        if r == c:
            value = value + jnp.where(eye, damp, 0.0)
            a_ref[blocks[r], blocks[c]] = value.astype(BF16)
            total += jnp.sum(value * value, keepdims=True)
        else:
            total += 2.0 * jnp.sum(value * value, keepdims=True)
            a_ref[blocks[c], blocks[r]] = a_ref[blocks[r], blocks[c]].T
    frob = jnp.sqrt(total)
    inv = 1.0 / frob
    inv_bf = inv.astype(BF16).astype(F32)
    for r in range(4):
        for c in range(4):
            product = (a_ref[blocks[r], blocks[c]].astype(F32) * inv_bf).astype(BF16).astype(F32)
            value = -product * inv_bf
            if r == c:
                value = value + jnp.where(eye, 2.0 * inv, 0.0)
            if r <= c:
                x_ref[blocks[r], blocks[c]] = value
            xb_ref[0, blocks[r], blocks[c]] = value.astype(BF16)
    for step in range(1, ITERS):
        now, later = xb_ref.at[(step - 1) % 2], xb_ref.at[step % 2]
        for c in (3, 2, 1, 0):
            mirrored(p_ref, c, dot(a_ref[:(c + 1) * tile, :], now[:, blocks[c]]).astype(BF16))
        for c in range(4):
            rows = slice(0, (c + 1) * tile)
            value = 2.0 * x_ref[rows, blocks[c]] - dot(p_ref[rows, :], now[:, blocks[c]])
            if step < ITERS - 1:
                x_ref[rows, blocks[c]] = value
                mirrored(later, c, value.astype(BF16))
            else:
                mirrored(out_ref, c, (value * (frob / 2.0 ** ITERS)).astype(BF16))


def rounds(damp, pieces):
    tile = pieces.shape[2]
    size = tile * 4
    return pl.pallas_call(
        rounds_kernel,
        out_shape=jax.ShapeDtypeStruct((size, size), BF16),
        in_specs=[SMEM, VMEM],
        out_specs=VMEM,
        scratch_shapes=[
            pltpu.VMEM((size, size), BF16),
            pltpu.VMEM((size, size), F32),
            pltpu.VMEM((2, size, size), BF16),
            pltpu.VMEM((size, size), BF16),
        ],
        cost_estimate=pl.CostEstimate(flops=16 * size ** 3, transcendentals=0, bytes_accessed=4 * size * size),
        compiler_params=pltpu.CompilerParams(vmem_limit_bytes=24 * MIB),
    )(damp, pieces)


def mix_kernel(place_ref, s_ref, w0, w1, w2, w3, out_ref, t_ref):
    tile, size = w0.shape
    half = place_ref[1]

    @pl.when(place_ref[0] == 1)
    def _():
        for i in range(2):
            rows = pl.ds(pl.multiple_of((2 * half + i) * tile, tile), tile)
            value = jnp.zeros((tile, size), F32)
            for b, w in enumerate((w0, w1, w2, w3)):
                cols = pl.ds(pl.multiple_of(lax.rem(2 * half + b, 4) * tile, tile), tile)
                value += dot(s_ref[rows, cols], w[...])
            t_ref[i * tile:(i + 1) * tile, :] = value.astype(BF16)
        out_ref[:2 * tile, :] = t_ref[...]


def mix(place, inverse, weights):
    tile, size = weights[0].shape
    return pl.pallas_call(
        mix_kernel,
        out_shape=jax.ShapeDtypeStruct(inverse.shape, BF16),
        in_specs=[SMEM] + [VMEM] * 5,
        out_specs=VMEM,
        scratch_shapes=[pltpu.VMEM((2 * tile, size), BF16)],
        input_output_aliases={1: 0},
        compiler_params=pltpu.CompilerParams(vmem_limit_bytes=16 * MIB),
    )(place, inverse, *weights)


def last_kernel(place_ref, mine_ref, other_ref, out_ref):
    tile = out_ref.shape[0]

    @pl.when(place_ref[0] == 0)
    def _():
        out_ref[...] = dot(other_ref[:tile, :], mine_ref[...]).astype(BF16)

    @pl.when(place_ref[0] == 1)
    def _():
        out_ref[...] = dot(mine_ref[tile:2 * tile, :], other_ref[...]).astype(BF16)


def last(place, mine, other, rows):
    return pl.pallas_call(
        last_kernel,
        out_shape=jax.ShapeDtypeStruct((rows, mine.shape[1]), BF16),
        in_specs=[SMEM] + [VMEM] * 2,
        out_specs=VMEM,
        compiler_params=pltpu.CompilerParams(vmem_limit_bytes=16 * MIB),
    )(place, mine, other)


def pick(parts, index):
    return lax.dynamic_index_in_dim(parts, index, 0, keepdims=False)


def on_device(activations, out_grads, sample_ids, damping, weight_grad):
    d, o = lax.axis_index("dp"), lax.axis_index("owner")
    zh, y, core = d // 8, d // 2 % 4, d % 2
    x, zl = o // 4, o % 4
    size = weight_grad.shape[1]
    scale = 1.0 / (sample_ids.shape[0] * 256)
    is_g = core == 0

    hot = (sample_ids[:, None] == jnp.arange(activations.shape[0], dtype=jnp.int32)[None]).astype(BF16)
    samp_g = dot(hot, out_grads).astype(BF16)
    activations, _ = lax.optimization_barrier((activations, samp_g))
    samp_x = dot(hot, activations).astype(BF16)
    other = moved(offer(core.reshape(1), samp_x, samp_g), lambda zh, y, c, x, zl: (zh, y, 1 - c, x, zl))

    held = dealt(
        pack(core.reshape(1), samp_x, samp_g, other, size),
        lambda *place: over_x(*place) if place[2] == 0 else over_blocks(*place),
    )

    samples = list(deal(jnp.stack([jnp.where(is_g, (zl + 2) % 4, 0), 1 - core]), held))
    for k in (1, 2, 3):
        samples[k] = moved(
            samples[k],
            lambda zh, y, c, x, zl: (z_shift(zh, zl, k)[0], y, 0, x, z_shift(zh, zl, k)[1]) if c == 0
            else (zh, y, 1, (x + k) % 4, zl),
        )

    chunks = cov(jnp.stack([jnp.where(is_g, 0, x), 1 - core]), samples, scale)
    chunks = dealt(chunks, lambda *place: over_y(*place) if place[2] == 0 else over_zl(*place))
    part = jnp.sum(chunks.astype(F32), axis=0).astype(BF16)

    def beside(zh, zl, by):
        z = (zh * 4 + zl + by) % 8
        return z // 4, z % 4

    here = moved(part, lambda zh, y, c, x, zl: (beside(zh, zl, 2)[0], y, 0, x, beside(zh, zl, 2)[1]) if c == 0
                 else (zh, y ^ 1, 1, x, zl))
    there = moved(part, lambda zh, y, c, x, zl: (beside(zh, zl, -2)[0], y, 0, x, beside(zh, zl, -2)[1]) if c == 0
                  else None)
    piece = (here.astype(F32) + there.astype(F32)).astype(BF16)

    pieces = dealt(
        jnp.broadcast_to(piece, (4,) + piece.shape),
        lambda *place: over_y(*place) if place[2] == 0 else over_x(*place),
    )

    own_w, _ = lax.optimization_barrier((weight_grad, piece))
    weights = [
        moved(own_w, lambda zh, y, c, x, zl: (zh, y, 1 - c, x, zl)),
        moved(own_w, lambda zh, y, c, x, zl: (zh, y ^ 1, 1, x, zl) if c == 0 else (zh, y, 0, x, zl)),
        moved(own_w, lambda zh, y, c, x, zl: (zh, y ^ 1, 1, x, zl) if c == 1 else None),
    ]
    damp = pick(damping, jnp.where(is_g, BLOCKS_A + o, zh * 2 + y // 2)).reshape(1)
    place = jnp.stack([core, y % 2])
    inverse, *weights = lax.optimization_barrier((rounds(damp, pieces), *weights))
    weights.insert(1, weight_grad)

    mine = mix(place, inverse, weights)
    other = moved(mine, lambda zh, y, c, x, zl: (zh, y, 1 - c, x, zl))
    return last(place, mine, other, weight_grad.shape[0])


def solution(mesh):
    placed = (
        P(("dp", "owner"), None),
        P(("dp", "owner"), None),
        P(("dp", "owner")),
        P(),
        P("dp", "owner"),
    )
    return jax.shard_map(
        on_device, mesh=mesh, in_specs=placed, out_specs=P("dp", "owner"), check_vma=False
    )
```

```python
import jax
import jax.numpy as jnp
from jax import lax
from jax.experimental import pallas as pl
from jax.experimental.pallas import tpu as pltpu
from jax.sharding import PartitionSpec as P

BLOCKS_A = 4
ITERS = 5
BF16 = jnp.bfloat16
F32 = jnp.float32
MIB = 2 ** 20
UPPER = [(r, c) for r in range(4) for c in range(r, 4)]
FIRST, SECOND = UPPER[:5], UPPER[5:]
SMEM = pl.BlockSpec(memory_space=pltpu.SMEM)
VMEM = pl.BlockSpec(memory_space=pltpu.VMEM)


def dot(a, b):
    return jnp.dot(a, b, preferred_element_type=F32)


def gram(a, b):
    return lax.dot_general(a, b, (((0,), (0,)), ((), ())), preferred_element_type=F32)


def linear(zh, y, c, x, zl):
    return ((zh * 4 + y) * 2 + c) * 16 + x * 4 + zl


def moved(value, where):
    pairs = []
    for source in range(256):
        c, x, zl = source // 16 % 2, source // 4 % 4, source % 4
        zh, y = source // 128, source // 32 % 4
        target = where(zh, y, c, x, zl)
        pairs.append((source, source if target is None else linear(*target)))
    assert len({target for _, target in pairs}) == 256
    return lax.ppermute(value, ("dp", "owner"), pairs)


def z_shift(zh, zl, k):
    z = zh * 4 + zl
    z = (z + {1: 1, 2: 2 if z % 2 == 0 else -2, 3: -1}[k]) % 8
    return z // 4, z % 4


def offer_kernel(core_ref, x_ref, g_ref, out_ref):
    @pl.when(core_ref[0] == 0)
    def _():
        out_ref[:, :x_ref.shape[1]] = x_ref[...]
        out_ref[:, x_ref.shape[1]:] = jnp.zeros((x_ref.shape[0], out_ref.shape[1] - x_ref.shape[1]), BF16)

    @pl.when(core_ref[0] == 1)
    def _():
        out_ref[...] = g_ref[...]


def offer(core, samp_x, samp_g):
    return pl.pallas_call(
        offer_kernel,
        out_shape=jax.ShapeDtypeStruct(samp_g.shape, BF16),
        in_specs=[SMEM, VMEM, VMEM],
        out_specs=VMEM,
        compiler_params=pltpu.CompilerParams(vmem_limit_bytes=8 * MIB),
    )(core, samp_x, samp_g)


def pack_kernel(place_ref, mine_ref, other_ref, *outs):
    count, size = mine_ref.shape[0], outs[0].shape[1]
    for k, out in enumerate(outs):
        for zl in range(4):
            index = lax.rem(place_ref[0] + k, 4) * 4 + zl
            cols = pl.ds(pl.multiple_of(index * size, size), size)
            out[zl * 2 * count:(zl * 2 + 1) * count, :] = mine_ref[:, cols]
            out[(zl * 2 + 1) * count:(zl * 2 + 2) * count, :] = other_ref[:, cols]


def pack(place, mine, other, size):
    return pl.pallas_call(
        pack_kernel,
        out_shape=(jax.ShapeDtypeStruct((8 * mine.shape[0], size), BF16),) * 4,
        in_specs=[SMEM, VMEM, VMEM],
        out_specs=(VMEM,) * 4,
        compiler_params=pltpu.CompilerParams(vmem_limit_bytes=8 * MIB),
    )(place, mine, other)


def deal_kernel(place_ref, h0, h1, h2, h3, kept_ref, come_ref, *outs):
    rows = h0.shape[0] // 4
    half = kept_ref.shape[0]

    @pl.when(place_ref[1] == 0)
    def _():
        for k, out in enumerate(outs):
            start = pl.multiple_of(lax.rem(place_ref[0] + k, 4) * rows, rows)
            for i, held in enumerate((h0, h1, h2, h3)):
                out[i * rows:(i + 1) * rows, :] = held[pl.ds(start, rows), :]

    @pl.when(place_ref[1] == 1)
    def _():
        for out in outs:
            out[:half, :] = kept_ref[...]
            out[half:, :] = come_ref[...]


def deal(place, held, kept, come):
    return pl.pallas_call(
        deal_kernel,
        out_shape=(jax.ShapeDtypeStruct(held[0].shape, BF16),) * 4,
        in_specs=[SMEM] + [VMEM] * 6,
        out_specs=(VMEM,) * 4,
        compiler_params=pltpu.CompilerParams(vmem_limit_bytes=8 * MIB),
    )(place, *held, kept, come)


def cov_kernel(scale, place_ref, *refs):
    pieces, (keep_a, send_a, keep_b, send_b), (all_ref, full_ref) = refs[:4], refs[4:8], refs[8:]
    count, size = pieces[0].shape
    tile, sub = size // 4, size // 16
    for k, piece in enumerate(pieces):
        all_ref[k * count:(k + 1) * count, :] = piece[...]
    for r in range(4):
        cols = all_ref[:, r * tile:(r + 1) * tile]
        full_ref[r * tile:(r + 1) * tile, r * tile:] = (gram(cols, all_ref[:, r * tile:]) * scale).astype(BF16)
    mine = place_ref[1]

    def put(out, slot, quarter, tiles):
        start = pl.multiple_of(quarter * sub, sub)
        for i, (r, c) in enumerate(tiles):
            at = (slot * len(tiles) + i) * sub
            out[at:at + sub, :] = full_ref[pl.ds(r * tile + start, sub), c * tile:(c + 1) * tile]

    @pl.when(place_ref[0] == 0)
    def _():
        for out, masks, tiles in (
            (keep_a, (0, 3), FIRST), (send_a, (1, 2), FIRST), (keep_b, (0, 1), SECOND), (send_b, (3, 2), SECOND)
        ):
            for slot, mask in enumerate(masks):
                put(out, slot, lax.bitwise_xor(mine, jnp.int32(mask)), tiles)

    @pl.when(place_ref[0] == 1)
    def _():
        for out in (keep_a, send_a, keep_b, send_b):
            for slot, tiles in enumerate((FIRST, SECOND)):
                put(out, slot, mine, tiles)


def cov(place, pieces, scale):
    count, size = pieces[0].shape
    tile, sub = size // 4, size // 16
    return pl.pallas_call(
        lambda *refs: cov_kernel(scale, *refs),
        out_shape=(jax.ShapeDtypeStruct((len(UPPER) * sub, tile), BF16),) * 4,
        in_specs=[SMEM] + [VMEM] * 4,
        out_specs=(VMEM,) * 4,
        scratch_shapes=[pltpu.VMEM((4 * count, size), BF16), pltpu.VMEM((size, size), BF16)],
        compiler_params=pltpu.CompilerParams(vmem_limit_bytes=16 * MIB),
    )(place, *pieces)


def rounds_kernel(place_ref, damp_ref, piece, r1a, r1b, r2a, r2b, out_ref, a_ref, x_ref, xb_ref, p_ref):
    size = out_ref.shape[0]
    tile = size // 4
    sub = tile // 4
    base, damp = place_ref[0], damp_ref[0]
    blocks = [slice(i * tile, (i + 1) * tile) for i in range(4)]

    def mirrored(ref, c, value):
        ref[:(c + 1) * tile, blocks[c]] = value
        for r in range(c):
            ref[blocks[c], blocks[r]] = value[blocks[r], :].T

    for source, part, mask, tiles in (
        (piece, 0, 0, FIRST), (r1a, 0, 3, FIRST), (r2a, 0, 1, FIRST), (r2a, 1, 2, FIRST),
        (piece, 1, 0, SECOND), (r1b, 0, 1, SECOND), (r2b, 0, 3, SECOND), (r2b, 1, 2, SECOND),
    ):
        start = pl.multiple_of(lax.bitwise_xor(base, jnp.int32(mask)) * sub, sub)
        for i, (r, c) in enumerate(tiles):
            at = (part * 5 + i) * sub
            a_ref[pl.ds(r * tile + start, sub), blocks[c]] = source[at:at + sub, :]
    row = lax.broadcasted_iota(jnp.int32, (tile, tile), 0)
    col = lax.broadcasted_iota(jnp.int32, (tile, tile), 1)
    eye = row == col
    total = jnp.zeros((1, 1), F32)
    for r, c in UPPER:
        value = a_ref[blocks[r], blocks[c]].astype(F32)
        if r == c:
            value = value + jnp.where(eye, damp, 0.0)
            a_ref[blocks[r], blocks[c]] = value.astype(BF16)
            total += jnp.sum(value * value, keepdims=True)
        else:
            total += 2.0 * jnp.sum(value * value, keepdims=True)
            a_ref[blocks[c], blocks[r]] = a_ref[blocks[r], blocks[c]].T
    frob = jnp.sqrt(total)
    inv = 1.0 / frob
    inv_bf = inv.astype(BF16).astype(F32)
    for r in range(4):
        for c in range(4):
            product = (a_ref[blocks[r], blocks[c]].astype(F32) * inv_bf).astype(BF16).astype(F32)
            value = -product * inv_bf
            if r == c:
                value = value + jnp.where(eye, 2.0 * inv, 0.0)
            if r <= c:
                x_ref[blocks[r], blocks[c]] = value
            xb_ref[0, blocks[r], blocks[c]] = value.astype(BF16)
    for step in range(1, ITERS):
        now, later = xb_ref.at[(step - 1) % 2], xb_ref.at[step % 2]
        for c in (3, 2, 1, 0):
            mirrored(p_ref, c, dot(a_ref[:(c + 1) * tile, :], now[:, blocks[c]]).astype(BF16))
        for c in range(4):
            rows = slice(0, (c + 1) * tile)
            value = 2.0 * x_ref[rows, blocks[c]] - dot(p_ref[rows, :], now[:, blocks[c]])
            if step < ITERS - 1:
                x_ref[rows, blocks[c]] = value
                mirrored(later, c, value.astype(BF16))
            else:
                mirrored(out_ref, c, (value * (frob / 2.0 ** ITERS)).astype(BF16))


def rounds(place, damp, pieces):
    tile = pieces[0].shape[1]
    size = tile * 4
    return pl.pallas_call(
        rounds_kernel,
        out_shape=jax.ShapeDtypeStruct((size, size), BF16),
        in_specs=[SMEM, SMEM] + [VMEM] * 5,
        out_specs=VMEM,
        scratch_shapes=[
            pltpu.VMEM((size, size), BF16),
            pltpu.VMEM((size, size), F32),
            pltpu.VMEM((2, size, size), BF16),
            pltpu.VMEM((size, size), BF16),
        ],
        cost_estimate=pl.CostEstimate(flops=16 * size ** 3, transcendentals=0, bytes_accessed=4 * size * size),
        compiler_params=pltpu.CompilerParams(vmem_limit_bytes=24 * MIB),
    )(place, damp, *pieces)


def mix_kernel(place_ref, s_ref, w0, w1, w2, w3, out_ref, t_ref):
    tile, size = w0.shape
    half = place_ref[1]

    @pl.when(place_ref[0] == 1)
    def _():
        for i in range(2):
            rows = pl.ds(pl.multiple_of((2 * half + i) * tile, tile), tile)
            value = jnp.zeros((tile, size), F32)
            for b, w in enumerate((w0, w1, w2, w3)):
                cols = pl.ds(pl.multiple_of(lax.rem(2 * half + b, 4) * tile, tile), tile)
                value += dot(s_ref[rows, cols], w[...])
            t_ref[i * tile:(i + 1) * tile, :] = value.astype(BF16)
        out_ref[:2 * tile, :] = t_ref[...]


def mix(place, inverse, weights):
    tile, size = weights[0].shape
    return pl.pallas_call(
        mix_kernel,
        out_shape=jax.ShapeDtypeStruct(inverse.shape, BF16),
        in_specs=[SMEM] + [VMEM] * 5,
        out_specs=VMEM,
        scratch_shapes=[pltpu.VMEM((2 * tile, size), BF16)],
        input_output_aliases={1: 0},
        compiler_params=pltpu.CompilerParams(vmem_limit_bytes=16 * MIB),
    )(place, inverse, *weights)


def last_kernel(place_ref, mine_ref, other_ref, out_ref):
    tile = out_ref.shape[0]

    @pl.when(place_ref[0] == 0)
    def _():
        out_ref[...] = dot(other_ref[:tile, :], mine_ref[...]).astype(BF16)

    @pl.when(place_ref[0] == 1)
    def _():
        out_ref[...] = dot(mine_ref[tile:2 * tile, :], other_ref[...]).astype(BF16)


def last(place, mine, other, rows):
    return pl.pallas_call(
        last_kernel,
        out_shape=jax.ShapeDtypeStruct((rows, mine.shape[1]), BF16),
        in_specs=[SMEM] + [VMEM] * 2,
        out_specs=VMEM,
        compiler_params=pltpu.CompilerParams(vmem_limit_bytes=16 * MIB),
    )(place, mine, other)


def pick(parts, index):
    return lax.dynamic_index_in_dim(parts, index, 0, keepdims=False)


def on_device(activations, out_grads, sample_ids, damping, weight_grad):
    d, o = lax.axis_index("dp"), lax.axis_index("owner")
    zh, y, core = d // 8, d // 2 % 4, d % 2
    x, zl = o // 4, o % 4
    size = weight_grad.shape[1]
    scale = 1.0 / (sample_ids.shape[0] * 256)
    is_g = core == 0

    hot = (sample_ids[:, None] == jnp.arange(activations.shape[0], dtype=jnp.int32)[None]).astype(BF16)
    samp_g = dot(hot, out_grads).astype(BF16)
    activations, _ = lax.optimization_barrier((activations, samp_g))
    samp_x = dot(hot, activations).astype(BF16)
    other = moved(offer(core.reshape(1), samp_x, samp_g), lambda zh, y, c, x, zl: (zh, y, 1 - c, x, zl))

    packed = pack(x.reshape(1), samp_g, other, size)
    held = [packed[0]]
    for k in (1, 2, 3):
        held.append(moved(packed[k], lambda zh, y, c, x, zl: (zh, y, 0, (x + k) % 4, zl) if c == 0 else None))

    both_x = jnp.concatenate([samp_x, other[:, :4 * size]])

    def over_z(zh, y, c, x, zl):
        z = (zh * 4 + zl + (-2 if zl < 2 else 2)) % 8
        return (z // 4, y, 1, x, z % 4) if c == 1 else None

    def columns(value, start, count):
        return lax.dynamic_slice_in_dim(value, start * size, count * size, 1)

    halves = jnp.concatenate([columns(both_x, zh * 2, 2), moved(columns(both_x, (1 - zh) * 2, 2), over_z)])
    kept = columns(halves, y // 2, 1)
    come = moved(columns(halves, 1 - y // 2, 1), lambda zh, y, c, x, zl: (zh, 3 - y, 1, x, zl) if c == 1 else None)

    samples = list(deal(jnp.stack([(zl + 2) % 4, core]), held, kept, come))
    for k in (1, 2, 3):
        samples[k] = moved(
            samples[k],
            lambda zh, y, c, x, zl: (z_shift(zh, zl, k)[0], y, 0, x, z_shift(zh, zl, k)[1]) if c == 0
            else (zh, y, 1, (x + k) % 4, zl),
        )

    keep_a, send_a, keep_b, send_b = cov(jnp.stack([core, jnp.where(is_g, y, x)]), samples, scale)
    half = keep_a.shape[0] // 2
    sum_a = keep_a.astype(F32) + moved(
        send_a, lambda zh, y, c, x, zl: (zh, y ^ 1, 0, x, zl) if c == 0 else (zh, y, 1, x, zl ^ 1)).astype(F32)
    sum_b = keep_b.astype(F32) + moved(
        send_b, lambda zh, y, c, x, zl: (zh, y ^ 3, 0, x, zl) if c == 0 else None).astype(F32)
    on_a = moved(
        jnp.where(is_g, sum_a[half:], sum_a[:half]).astype(BF16),
        lambda zh, y, c, x, zl: (zh, y ^ 3, 0, x, zl) if c == 0 else (zh, y, 1, x, zl ^ 2))
    on_b = moved(
        jnp.where(is_g, sum_b[half:], sum_a[half:]).astype(BF16),
        lambda zh, y, c, x, zl: (zh, y ^ 1, 0, x, zl) if c == 0 else (zh, y, 1, x, zl ^ 2))
    part = jnp.concatenate([
        sum_a[:half] + on_a.astype(F32),
        jnp.where(is_g, sum_b[:half], sum_a[half:]) + on_b.astype(F32),
    ]).astype(BF16)

    def beside(zh, zl, by):
        z = (zh * 4 + zl + by) % 8
        return z // 4, z % 4

    here = moved(part, lambda zh, y, c, x, zl: (beside(zh, zl, 2)[0], y, 0, x, beside(zh, zl, 2)[1]) if c == 0
                 else (zh, y ^ 1, 1, x, zl))
    there = moved(part, lambda zh, y, c, x, zl: (beside(zh, zl, -2)[0], y, 0, x, beside(zh, zl, -2)[1]) if c == 0
                  else None)
    piece = (here.astype(F32) + there.astype(F32)).astype(BF16)

    def swapped(value, mask):
        return moved(
            value, lambda zh, y, c, x, zl: (zh, y ^ mask, 0, x, zl) if c == 0 else (zh, y, 1, x ^ mask, zl))

    r1a, r1b = swapped(piece[:half], 3), swapped(piece[half:], 1)
    r2a = swapped(jnp.concatenate([piece[:half], r1a]), 1)
    r2b = swapped(jnp.concatenate([piece[half:], r1b]), 3)
    pieces = [piece, r1a, r1b, r2a, r2b]

    own_w, _ = lax.optimization_barrier((weight_grad, piece))
    weights = [
        moved(own_w, lambda zh, y, c, x, zl: (zh, y, 1 - c, x, zl)),
        moved(own_w, lambda zh, y, c, x, zl: (zh, y ^ 1, 1, x, zl) if c == 0 else (zh, y, 0, x, zl)),
        moved(own_w, lambda zh, y, c, x, zl: (zh, y ^ 1, 1, x, zl) if c == 1 else None),
    ]
    damp = pick(damping, jnp.where(is_g, BLOCKS_A + o, zh * 2 + y // 2)).reshape(1)
    place = jnp.stack([core, y % 2])
    inverse, *weights = lax.optimization_barrier((rounds(jnp.where(is_g, y, x).astype(jnp.int32).reshape(1), damp, pieces), *weights))
    weights.insert(1, weight_grad)

    mine = mix(place, inverse, weights)
    other = moved(mine, lambda zh, y, c, x, zl: (zh, y, 1 - c, x, zl))
    return last(place, mine, other, weight_grad.shape[0])


def solution(mesh):
    placed = (
        P(("dp", "owner"), None),
        P(("dp", "owner"), None),
        P(("dp", "owner")),
        P(),
        P("dp", "owner"),
    )
    return jax.shard_map(
        on_device, mesh=mesh, in_specs=placed, out_specs=P("dp", "owner"), check_vma=False
    )
```

```python
import jax
import jax.numpy as jnp
from jax import lax
from jax.experimental import pallas as pl
from jax.experimental.pallas import tpu as pltpu
from jax.sharding import PartitionSpec as P

BLOCKS_A = 4
ITERS = 5
BF16 = jnp.bfloat16
F32 = jnp.float32
MIB = 2 ** 20
UPPER = [(r, c) for r in range(8) for c in range(r, 8)]
PARTS = [UPPER[9 * i:9 * (i + 1)] for i in range(4)]
SMEM = pl.BlockSpec(memory_space=pltpu.SMEM)
VMEM = pl.BlockSpec(memory_space=pltpu.VMEM)


def dot(a, b):
    return jnp.dot(a, b, preferred_element_type=F32)


def gram(a, b):
    return lax.dot_general(a, b, (((0,), (0,)), ((), ())), preferred_element_type=F32)


def linear(zh, y, c, x, zl):
    return ((zh * 4 + y) * 2 + c) * 16 + x * 4 + zl


def moved(value, where):
    pairs = []
    for source in range(256):
        c, x, zl = source // 16 % 2, source // 4 % 4, source % 4
        zh, y = source // 128, source // 32 % 4
        target = where(zh, y, c, x, zl)
        pairs.append((source, source if target is None else linear(*target)))
    assert len({target for _, target in pairs}) == 256
    return lax.ppermute(value, ("dp", "owner"), pairs)


def z_shift(zh, zl, k):
    z = zh * 4 + zl
    z = (z + {1: 1, 2: 2 if z % 2 == 0 else -2, 3: -1}[k]) % 8
    return z // 4, z % 4


def offer_kernel(core_ref, x_ref, g_ref, out_ref):
    @pl.when(core_ref[0] == 0)
    def _():
        out_ref[:, :x_ref.shape[1]] = x_ref[...]
        out_ref[:, x_ref.shape[1]:] = jnp.zeros((x_ref.shape[0], out_ref.shape[1] - x_ref.shape[1]), BF16)

    @pl.when(core_ref[0] == 1)
    def _():
        out_ref[...] = g_ref[...]


def offer(core, samp_x, samp_g):
    return pl.pallas_call(
        offer_kernel,
        out_shape=jax.ShapeDtypeStruct(samp_g.shape, BF16),
        in_specs=[SMEM, VMEM, VMEM],
        out_specs=VMEM,
        compiler_params=pltpu.CompilerParams(vmem_limit_bytes=8 * MIB),
    )(core, samp_x, samp_g)


def pack_kernel(place_ref, mine_ref, other_ref, *outs):
    count, size = mine_ref.shape[0], outs[0].shape[1]
    for k, out in enumerate(outs):
        for zl in range(4):
            index = lax.rem(place_ref[0] + k, 4) * 4 + zl
            cols = pl.ds(pl.multiple_of(index * size, size), size)
            out[zl * 2 * count:(zl * 2 + 1) * count, :] = mine_ref[:, cols]
            out[(zl * 2 + 1) * count:(zl * 2 + 2) * count, :] = other_ref[:, cols]


def pack(place, mine, other, size):
    return pl.pallas_call(
        pack_kernel,
        out_shape=(jax.ShapeDtypeStruct((8 * mine.shape[0], size), BF16),) * 4,
        in_specs=[SMEM, VMEM, VMEM],
        out_specs=(VMEM,) * 4,
        compiler_params=pltpu.CompilerParams(vmem_limit_bytes=8 * MIB),
    )(place, mine, other)


def deal_kernel(place_ref, h0, h1, h2, h3, kept_ref, come_ref, *outs):
    rows = h0.shape[0] // 4
    half = kept_ref.shape[0]

    @pl.when(place_ref[1] == 0)
    def _():
        for k, out in enumerate(outs):
            start = pl.multiple_of(lax.rem(place_ref[0] + k, 4) * rows, rows)
            for i, held in enumerate((h0, h1, h2, h3)):
                out[i * rows:(i + 1) * rows, :] = held[pl.ds(start, rows), :]

    @pl.when(place_ref[1] == 1)
    def _():
        for out in outs:
            out[:half, :] = kept_ref[...]
            out[half:, :] = come_ref[...]


def deal(place, held, kept, come):
    return pl.pallas_call(
        deal_kernel,
        out_shape=(jax.ShapeDtypeStruct(held[0].shape, BF16),) * 4,
        in_specs=[SMEM] + [VMEM] * 6,
        out_specs=(VMEM,) * 4,
        compiler_params=pltpu.CompilerParams(vmem_limit_bytes=8 * MIB),
    )(place, *held, kept, come)


def cov_kernel(scale, place_ref, *refs):
    pieces, chunks, (all_ref, full_ref, parts_ref) = refs[:4], refs[4:8], refs[8:]
    count, size = pieces[0].shape
    tile, small = size // 4, size // 8
    for k, piece in enumerate(pieces):
        all_ref[k * count:(k + 1) * count, :] = piece[...]
    for r in range(4):
        cols = all_ref[:, r * tile:(r + 1) * tile]
        full_ref[r * tile:(r + 1) * tile, r * tile:] = (gram(cols, all_ref[:, r * tile:]) * scale).astype(BF16)
    for i, tiles in enumerate(PARTS):
        for t, (r, c) in enumerate(tiles):
            parts_ref[i, t * small:(t + 1) * small, :] = full_ref[
                r * small:(r + 1) * small, c * small:(c + 1) * small]
    for k, chunk in enumerate(chunks):
        chunk[...] = parts_ref[lax.rem(place_ref[0] + k * place_ref[1], 4)]


def cov(place, pieces, scale):
    count, size = pieces[0].shape
    part = (len(PARTS[0]) * size // 8, size // 8)
    return pl.pallas_call(
        lambda *refs: cov_kernel(scale, *refs),
        out_shape=(jax.ShapeDtypeStruct(part, BF16),) * 4,
        in_specs=[SMEM] + [VMEM] * 4,
        out_specs=(VMEM,) * 4,
        scratch_shapes=[
            pltpu.VMEM((4 * count, size), BF16), pltpu.VMEM((size, size), BF16), pltpu.VMEM((4,) + part, BF16)],
        compiler_params=pltpu.CompilerParams(vmem_limit_bytes=20 * MIB),
    )(place, *pieces)


def rounds_kernel(place_ref, damp_ref, p0, p1, p2, p3, out_ref, a_ref, x_ref, xb_ref, p_ref, parts_ref):
    size = out_ref.shape[0]
    tile, small = size // 4, size // 8
    base, damp = place_ref[0], damp_ref[0]
    blocks = [slice(i * tile, (i + 1) * tile) for i in range(4)]

    def mirrored(ref, c, value):
        ref[:(c + 1) * tile, blocks[c]] = value
        for r in range(c):
            ref[blocks[c], blocks[r]] = value[blocks[r], :].T

    for k, piece in enumerate((p0, p1, p2, p3)):
        parts_ref[lax.rem(base + 4 - k, 4)] = piece[...]
    for i, tiles in enumerate(PARTS):
        for t, (r, c) in enumerate(tiles):
            value = parts_ref[i, t * small:(t + 1) * small, :]
            rows, cols = slice(r * small, (r + 1) * small), slice(c * small, (c + 1) * small)
            a_ref[rows, cols] = value
            if r < c:
                a_ref[cols, rows] = value.T
    row = lax.broadcasted_iota(jnp.int32, (tile, tile), 0)
    col = lax.broadcasted_iota(jnp.int32, (tile, tile), 1)
    eye = row == col
    total = jnp.zeros((1, 1), F32)
    for r in range(4):
        for c in range(r, 4):
            value = a_ref[blocks[r], blocks[c]].astype(F32)
            if r == c:
                value = value + jnp.where(eye, damp, 0.0)
                a_ref[blocks[r], blocks[c]] = value.astype(BF16)
                total += jnp.sum(value * value, keepdims=True)
            else:
                total += 2.0 * jnp.sum(value * value, keepdims=True)
    frob = jnp.sqrt(total)
    inv = 1.0 / frob
    inv_bf = inv.astype(BF16).astype(F32)
    for r in range(4):
        for c in range(4):
            product = (a_ref[blocks[r], blocks[c]].astype(F32) * inv_bf).astype(BF16).astype(F32)
            value = -product * inv_bf
            if r == c:
                value = value + jnp.where(eye, 2.0 * inv, 0.0)
            if r <= c:
                x_ref[blocks[r], blocks[c]] = value
            xb_ref[0, blocks[r], blocks[c]] = value.astype(BF16)
    for step in range(1, ITERS):
        now, later = xb_ref.at[(step - 1) % 2], xb_ref.at[step % 2]
        for c in (3, 2, 1, 0):
            mirrored(p_ref, c, dot(a_ref[:(c + 1) * tile, :], now[:, blocks[c]]).astype(BF16))
        for c in range(4):
            rows = slice(0, (c + 1) * tile)
            value = 2.0 * x_ref[rows, blocks[c]] - dot(p_ref[rows, :], now[:, blocks[c]])
            if step < ITERS - 1:
                x_ref[rows, blocks[c]] = value
                mirrored(later, c, value.astype(BF16))
            else:
                mirrored(out_ref, c, (value * (frob / 2.0 ** ITERS)).astype(BF16))


def rounds(place, damp, pieces):
    size = pieces[0].shape[1] * 8
    return pl.pallas_call(
        rounds_kernel,
        out_shape=jax.ShapeDtypeStruct((size, size), BF16),
        in_specs=[SMEM, SMEM] + [VMEM] * 4,
        out_specs=VMEM,
        scratch_shapes=[
            pltpu.VMEM((size, size), BF16),
            pltpu.VMEM((size, size), F32),
            pltpu.VMEM((2, size, size), BF16),
            pltpu.VMEM((size, size), BF16),
            pltpu.VMEM((4,) + pieces[0].shape, BF16),
        ],
        cost_estimate=pl.CostEstimate(flops=16 * size ** 3, transcendentals=0, bytes_accessed=4 * size * size),
        compiler_params=pltpu.CompilerParams(vmem_limit_bytes=24 * MIB),
    )(place, damp, *pieces)


def mix_kernel(place_ref, s_ref, w0, w1, w2, w3, out_ref, t_ref):
    tile, size = w0.shape
    half = place_ref[2]

    @pl.when(place_ref[1] == 1)
    def _():
        for i in range(2):
            rows = pl.ds(pl.multiple_of((2 * half + i) * tile, tile), tile)
            value = jnp.zeros((tile, size), F32)
            for b, w in enumerate((w0, w1, w2, w3)):
                cols = pl.ds(pl.multiple_of(lax.rem(2 * half + b, 4) * tile, tile), tile)
                value += dot(s_ref[rows, cols], w[...])
            t_ref[i * tile:(i + 1) * tile, :] = value.astype(BF16)
        out_ref[:2 * tile, :] = t_ref[...]


def mix(place, inverse, weights):
    tile, size = weights[0].shape
    return pl.pallas_call(
        mix_kernel,
        out_shape=jax.ShapeDtypeStruct(inverse.shape, BF16),
        in_specs=[SMEM] + [VMEM] * 5,
        out_specs=VMEM,
        scratch_shapes=[pltpu.VMEM((2 * tile, size), BF16)],
        input_output_aliases={1: 0},
        compiler_params=pltpu.CompilerParams(vmem_limit_bytes=16 * MIB),
    )(place, inverse, *weights)


def last_kernel(place_ref, mine_ref, other_ref, out_ref):
    tile, size = out_ref.shape

    def put(rows, inverse):
        for i in range(size // tile):
            block = slice(i * tile, (i + 1) * tile)
            value = lax.dot_general(
                inverse[block, :], rows, (((1,), (1,)), ((), ())), preferred_element_type=F32)
            out_ref[:, block] = value.astype(BF16).T

    @pl.when(place_ref[1] == 0)
    def _():
        put(other_ref[:tile, :], mine_ref)

    @pl.when(place_ref[1] == 1)
    def _():
        put(mine_ref[tile:2 * tile, :], other_ref)


def last(place, mine, other, rows):
    return pl.pallas_call(
        last_kernel,
        out_shape=jax.ShapeDtypeStruct((rows, mine.shape[1]), BF16),
        in_specs=[SMEM] + [VMEM] * 2,
        out_specs=VMEM,
        compiler_params=pltpu.CompilerParams(vmem_limit_bytes=16 * MIB),
    )(place, mine, other)


def pick(parts, index):
    return lax.dynamic_index_in_dim(parts, index, 0, keepdims=False)


def on_device(activations, out_grads, sample_ids, damping, weight_grad):
    d, o = lax.axis_index("dp"), lax.axis_index("owner")
    zh, y, core = d // 8, d // 2 % 4, d % 2
    x, zl = o // 4, o % 4
    size = weight_grad.shape[1]
    scale = 1.0 / (sample_ids.shape[0] * 256)
    is_g = core == 0

    hot = (sample_ids[:, None] == jnp.arange(activations.shape[0], dtype=jnp.int32)[None]).astype(BF16)
    samp_g = dot(hot, out_grads).astype(BF16)
    activations, _ = lax.optimization_barrier((activations, samp_g))
    samp_x = dot(hot, activations).astype(BF16)
    other = moved(offer(core.reshape(1), samp_x, samp_g), lambda zh, y, c, x, zl: (zh, y, 1 - c, x, zl))

    packed = pack(x.reshape(1), samp_g, other, size)
    held = [packed[0]]
    for k in (1, 2, 3):
        held.append(moved(packed[k], lambda zh, y, c, x, zl: (zh, y, 0, (x + k) % 4, zl) if c == 0 else None))

    both_x = jnp.concatenate([samp_x, other[:, :4 * size]])

    def over_z(zh, y, c, x, zl):
        z = (zh * 4 + zl + (-2 if zl < 2 else 2)) % 8
        return (z // 4, y, 1, x, z % 4) if c == 1 else None

    def columns(value, start, count):
        return lax.dynamic_slice_in_dim(value, start * size, count * size, 1)

    halves = jnp.concatenate([columns(both_x, zh * 2, 2), moved(columns(both_x, (1 - zh) * 2, 2), over_z)])
    kept = columns(halves, y // 2, 1)
    come = moved(columns(halves, 1 - y // 2, 1), lambda zh, y, c, x, zl: (zh, 3 - y, 1, x, zl) if c == 1 else None)

    samples = list(deal(jnp.stack([(zl + 2) % 4, core]), held, kept, come))
    for k in (1, 2, 3):
        samples[k] = moved(
            samples[k],
            lambda zh, y, c, x, zl: (z_shift(zh, zl, k)[0], y, 0, x, z_shift(zh, zl, k)[1]) if c == 0
            else (zh, y, 1, (x + k) % 4, zl),
        )

    chunks = cov(jnp.stack([jnp.where(is_g, y, x), 1 - core]), samples, scale)
    total = chunks[0].astype(F32)
    for k in (1, 2, 3):
        total += moved(
            chunks[k],
            lambda zh, y, c, x, zl: (zh, (y + k) % 4, 0, x, zl) if c == 0 else (zh, y, 1, x, (zl + k) % 4),
        ).astype(F32)
    part = total.astype(BF16)

    def beside(zh, zl, by):
        z = (zh * 4 + zl + by) % 8
        return z // 4, z % 4

    here = moved(part, lambda zh, y, c, x, zl: (beside(zh, zl, 2)[0], y, 0, x, beside(zh, zl, 2)[1]) if c == 0
                 else (zh, y ^ 1, 1, x, zl))
    there = moved(part, lambda zh, y, c, x, zl: (beside(zh, zl, -2)[0], y, 0, x, beside(zh, zl, -2)[1]) if c == 0
                  else None)
    piece = (here.astype(F32) + there.astype(F32)).astype(BF16)

    pieces = [piece]
    for k in (1, 2, 3):
        pieces.append(moved(
            piece,
            lambda zh, y, c, x, zl: (zh, (y + k) % 4, 0, x, zl) if c == 0 else (zh, y, 1, (x + k) % 4, zl),
        ))

    own_w, _ = lax.optimization_barrier((weight_grad, piece))
    weights = [
        moved(own_w, lambda zh, y, c, x, zl: (zh, y, 1 - c, x, zl)),
        moved(own_w, lambda zh, y, c, x, zl: (zh, y ^ 1, 1, x, zl) if c == 0 else (zh, y, 0, x, zl)),
        moved(own_w, lambda zh, y, c, x, zl: (zh, y ^ 1, 1, x, zl) if c == 1 else None),
    ]
    damp = pick(damping, jnp.where(is_g, BLOCKS_A + o, zh * 2 + y // 2)).reshape(1)
    place = jnp.stack([jnp.where(is_g, y, x), core, y % 2])
    inverse, *weights = lax.optimization_barrier((rounds(place, damp, pieces), *weights))
    weights.insert(1, weight_grad)

    mine = mix(place, inverse, weights)
    other = moved(mine, lambda zh, y, c, x, zl: (zh, y, 1 - c, x, zl))
    return last(place, mine, other, weight_grad.shape[0])


def solution(mesh):
    placed = (
        P(("dp", "owner"), None),
        P(("dp", "owner"), None),
        P(("dp", "owner")),
        P(),
        P("dp", "owner"),
    )
    return jax.shard_map(
        on_device, mesh=mesh, in_specs=placed, out_specs=P("dp", "owner"), check_vma=False
    )
```

```python
import jax
import jax.numpy as jnp
from jax import lax
from jax.experimental import pallas as pl
from jax.experimental.pallas import tpu as pltpu
from jax.sharding import PartitionSpec as P

BLOCKS_A = 4
ITERS = 5
BF16 = jnp.bfloat16
F32 = jnp.float32
MIB = 2 ** 20
UPPER = [(r, c) for r in range(8) for c in range(r, 8)]
PARTS = [UPPER[9 * i:9 * (i + 1)] for i in range(4)]
SMEM = pl.BlockSpec(memory_space=pltpu.SMEM)
VMEM = pl.BlockSpec(memory_space=pltpu.VMEM)


def dot(a, b):
    return jnp.dot(a, b, preferred_element_type=F32)


def gram(a, b):
    return lax.dot_general(a, b, (((0,), (0,)), ((), ())), preferred_element_type=F32)


def linear(zh, y, c, x, zl):
    return ((zh * 4 + y) * 2 + c) * 16 + x * 4 + zl


def moved(value, where):
    pairs = []
    for source in range(256):
        c, x, zl = source // 16 % 2, source // 4 % 4, source % 4
        zh, y = source // 128, source // 32 % 4
        target = where(zh, y, c, x, zl)
        pairs.append((source, source if target is None else linear(*target)))
    assert len({target for _, target in pairs}) == 256
    return lax.ppermute(value, ("dp", "owner"), pairs)


def dealt(value, group_of):
    groups = []
    for device in range(256):
        c, x, zl = device // 16 % 2, device // 4 % 4, device % 4
        members = [linear(*member) for member in group_of(device // 128, device // 32 % 4, c, x, zl)]
        assert device in members
        if device == min(members):
            groups.append(members)
    assert sorted(sum(groups, [])) == list(range(256))
    return lax.all_to_all(
        value, ("dp", "owner"), split_axis=0, concat_axis=0, tiled=True, axis_index_groups=groups)


def over_plane(zh, y, c, x, zl):
    return [(zh, y, c, i, k) for i in range(4) for k in range(4)]


def over_blocks(zh, y, c, x, zl):
    z = (zh * 4 + zl + (-2 if zl < 2 else 2)) % 8
    places = {zh: (zh, zl), 1 - zh: (z // 4, z % 4)}
    return [
        (places[h][0], y if y // 2 == g else 3 - y, c, i, places[h][1])
        for i in range(4) for h in range(2) for g in range(2)
    ]


def offer_kernel(core_ref, x_ref, g_ref, out_ref):
    @pl.when(core_ref[0] == 0)
    def _():
        out_ref[:, :x_ref.shape[1]] = x_ref[...]
        out_ref[:, x_ref.shape[1]:] = jnp.zeros((x_ref.shape[0], out_ref.shape[1] - x_ref.shape[1]), BF16)

    @pl.when(core_ref[0] == 1)
    def _():
        out_ref[...] = g_ref[...]


def offer(core, samp_x, samp_g):
    return pl.pallas_call(
        offer_kernel,
        out_shape=jax.ShapeDtypeStruct(samp_g.shape, BF16),
        in_specs=[SMEM, VMEM, VMEM],
        out_specs=VMEM,
        compiler_params=pltpu.CompilerParams(vmem_limit_bytes=8 * MIB),
    )(core, samp_x, samp_g)


def pack_kernel(core_ref, x_ref, g_ref, other_ref, out_ref):
    count, size = x_ref.shape[0], out_ref.shape[2]

    def put(mine_ref, column):
        for part in range(16):
            cols = slice(column(part) * size, (column(part) + 1) * size)
            out_ref[part, :count, :] = mine_ref[:, cols]
            out_ref[part, count:, :] = other_ref[:, cols]

    @pl.when(core_ref[0] == 0)
    def _():
        put(g_ref, lambda part: part // 4 * 4 + (part + 2) % 4)

    @pl.when(core_ref[0] == 1)
    def _():
        put(x_ref, lambda part: part % 4)


def pack(core, samp_x, samp_g, other, size):
    return pl.pallas_call(
        pack_kernel,
        out_shape=jax.ShapeDtypeStruct((16, 2 * samp_x.shape[0], size), BF16),
        in_specs=[SMEM] + [VMEM] * 3,
        out_specs=VMEM,
        compiler_params=pltpu.CompilerParams(vmem_limit_bytes=8 * MIB),
    )(core, samp_x, samp_g, other)


def cov_kernel(scale, place_ref, *refs):
    all_ref, chunks, (full_ref, parts_ref) = refs[0], refs[1:5], refs[5:]
    size = all_ref.shape[1]
    tile, small = size // 4, size // 8
    for r in range(4):
        cols = all_ref[:, r * tile:(r + 1) * tile]
        full_ref[r * tile:(r + 1) * tile, r * tile:] = (gram(cols, all_ref[:, r * tile:]) * scale).astype(BF16)
    for i, tiles in enumerate(PARTS):
        for t, (r, c) in enumerate(tiles):
            parts_ref[i, t * small:(t + 1) * small, :] = full_ref[
                r * small:(r + 1) * small, c * small:(c + 1) * small]
    for k, chunk in enumerate(chunks):
        chunk[...] = parts_ref[lax.rem(place_ref[0] + k * place_ref[1], 4)]


def cov(place, samples, scale):
    size = samples.shape[1]
    part = (len(PARTS[0]) * size // 8, size // 8)
    return pl.pallas_call(
        lambda *refs: cov_kernel(scale, *refs),
        out_shape=(jax.ShapeDtypeStruct(part, BF16),) * 4,
        in_specs=[SMEM, VMEM],
        out_specs=(VMEM,) * 4,
        scratch_shapes=[pltpu.VMEM((size, size), BF16), pltpu.VMEM((4,) + part, BF16)],
        compiler_params=pltpu.CompilerParams(vmem_limit_bytes=20 * MIB),
    )(place, samples)


def rounds_kernel(place_ref, damp_ref, p0, p1, p2, p3, out_ref, a_ref, x_ref, xb_ref, p_ref, parts_ref):
    size = out_ref.shape[0]
    tile, small = size // 4, size // 8
    base, damp = place_ref[0], damp_ref[0]
    blocks = [slice(i * tile, (i + 1) * tile) for i in range(4)]

    def mirrored(ref, c, value):
        ref[:(c + 1) * tile, blocks[c]] = value
        for r in range(c):
            ref[blocks[c], blocks[r]] = value[blocks[r], :].T

    for k, piece in enumerate((p0, p1, p2, p3)):
        parts_ref[lax.rem(base + 4 - k, 4)] = piece[...]
    for i, tiles in enumerate(PARTS):
        for t, (r, c) in enumerate(tiles):
            value = parts_ref[i, t * small:(t + 1) * small, :]
            rows, cols = slice(r * small, (r + 1) * small), slice(c * small, (c + 1) * small)
            a_ref[rows, cols] = value
            if r < c:
                a_ref[cols, rows] = value.T
    row = lax.broadcasted_iota(jnp.int32, (tile, tile), 0)
    col = lax.broadcasted_iota(jnp.int32, (tile, tile), 1)
    eye = row == col
    total = jnp.zeros((1, 1), F32)
    for r in range(4):
        for c in range(r, 4):
            value = a_ref[blocks[r], blocks[c]].astype(F32)
            if r == c:
                value = value + jnp.where(eye, damp, 0.0)
                a_ref[blocks[r], blocks[c]] = value.astype(BF16)
                total += jnp.sum(value * value, keepdims=True)
            else:
                total += 2.0 * jnp.sum(value * value, keepdims=True)
    frob = jnp.sqrt(total)
    inv = 1.0 / frob
    inv_bf = inv.astype(BF16).astype(F32)
    for r in range(4):
        for c in range(4):
            product = (a_ref[blocks[r], blocks[c]].astype(F32) * inv_bf).astype(BF16).astype(F32)
            value = -product * inv_bf
            if r == c:
                value = value + jnp.where(eye, 2.0 * inv, 0.0)
            if r <= c:
                x_ref[blocks[r], blocks[c]] = value
            xb_ref[0, blocks[r], blocks[c]] = value.astype(BF16)
    for step in range(1, ITERS):
        now, later = xb_ref.at[(step - 1) % 2], xb_ref.at[step % 2]
        for c in (3, 2, 1, 0):
            mirrored(p_ref, c, dot(a_ref[:(c + 1) * tile, :], now[:, blocks[c]]).astype(BF16))
        for c in range(4):
            rows = slice(0, (c + 1) * tile)
            value = 2.0 * x_ref[rows, blocks[c]] - dot(p_ref[rows, :], now[:, blocks[c]])
            if step < ITERS - 1:
                x_ref[rows, blocks[c]] = value
                mirrored(later, c, value.astype(BF16))
            else:
                mirrored(out_ref, c, (value * (frob / 2.0 ** ITERS)).astype(BF16))


def rounds(place, damp, pieces):
    size = pieces[0].shape[1] * 8
    return pl.pallas_call(
        rounds_kernel,
        out_shape=jax.ShapeDtypeStruct((size, size), BF16),
        in_specs=[SMEM, SMEM] + [VMEM] * 4,
        out_specs=VMEM,
        scratch_shapes=[
            pltpu.VMEM((size, size), BF16),
            pltpu.VMEM((size, size), F32),
            pltpu.VMEM((2, size, size), BF16),
            pltpu.VMEM((size, size), BF16),
            pltpu.VMEM((4,) + pieces[0].shape, BF16),
        ],
        cost_estimate=pl.CostEstimate(flops=16 * size ** 3, transcendentals=0, bytes_accessed=4 * size * size),
        compiler_params=pltpu.CompilerParams(vmem_limit_bytes=24 * MIB),
    )(place, damp, *pieces)


def mix_kernel(place_ref, s_ref, w0, w1, w2, w3, out_ref, t_ref):
    tile, size = w0.shape
    half = place_ref[2]

    @pl.when(place_ref[1] == 1)
    def _():
        for i in range(2):
            rows = pl.ds(pl.multiple_of((2 * half + i) * tile, tile), tile)
            value = jnp.zeros((tile, size), F32)
            for b, w in enumerate((w0, w1, w2, w3)):
                cols = pl.ds(pl.multiple_of(lax.rem(2 * half + b, 4) * tile, tile), tile)
                value += dot(s_ref[rows, cols], w[...])
            t_ref[i * tile:(i + 1) * tile, :] = value.astype(BF16)
        out_ref[:2 * tile, :] = t_ref[...]


def mix(place, inverse, weights):
    tile, size = weights[0].shape
    return pl.pallas_call(
        mix_kernel,
        out_shape=jax.ShapeDtypeStruct(inverse.shape, BF16),
        in_specs=[SMEM] + [VMEM] * 5,
        out_specs=VMEM,
        scratch_shapes=[pltpu.VMEM((2 * tile, size), BF16)],
        input_output_aliases={1: 0},
        compiler_params=pltpu.CompilerParams(vmem_limit_bytes=16 * MIB),
    )(place, inverse, *weights)


def last_kernel(place_ref, mine_ref, other_ref, out_ref):
    tile, size = out_ref.shape

    def put(rows, inverse):
        for i in range(size // tile):
            block = slice(i * tile, (i + 1) * tile)
            value = lax.dot_general(
                inverse[block, :], rows, (((1,), (1,)), ((), ())), preferred_element_type=F32)
            out_ref[:, block] = value.astype(BF16).T

    @pl.when(place_ref[1] == 0)
    def _():
        put(other_ref[:tile, :], mine_ref)

    @pl.when(place_ref[1] == 1)
    def _():
        put(mine_ref[tile:2 * tile, :], other_ref)


def last(place, mine, other, rows):
    return pl.pallas_call(
        last_kernel,
        out_shape=jax.ShapeDtypeStruct((rows, mine.shape[1]), BF16),
        in_specs=[SMEM] + [VMEM] * 2,
        out_specs=VMEM,
        compiler_params=pltpu.CompilerParams(vmem_limit_bytes=16 * MIB),
    )(place, mine, other)


def pick(parts, index):
    return lax.dynamic_index_in_dim(parts, index, 0, keepdims=False)


def on_device(activations, out_grads, sample_ids, damping, weight_grad):
    d, o = lax.axis_index("dp"), lax.axis_index("owner")
    zh, y, core = d // 8, d // 2 % 4, d % 2
    x, zl = o // 4, o % 4
    size = weight_grad.shape[1]
    scale = 1.0 / (sample_ids.shape[0] * 256)
    is_g = core == 0

    hot = (sample_ids[:, None] == jnp.arange(activations.shape[0], dtype=jnp.int32)[None]).astype(BF16)
    samp_g = dot(hot, out_grads).astype(BF16)
    activations, _ = lax.optimization_barrier((activations, samp_g))
    samp_x = dot(hot, activations).astype(BF16)
    other = moved(offer(core.reshape(1), samp_x, samp_g), lambda zh, y, c, x, zl: (zh, y, 1 - c, x, zl))

    samples = dealt(
        pack(core.reshape(1), samp_x, samp_g, other, size),
        lambda *place: over_plane(*place) if place[2] == 0 else over_blocks(*place),
    ).reshape(-1, size)

    chunks = cov(jnp.stack([jnp.where(is_g, y, x), 1 - core]), samples, scale)
    total = chunks[0].astype(F32)
    for k in (1, 2, 3):
        total += moved(
            chunks[k],
            lambda zh, y, c, x, zl: (zh, (y + k) % 4, 0, x, zl) if c == 0 else (zh, y, 1, x, (zl + k) % 4),
        ).astype(F32)
    part = total.astype(BF16)

    def beside(zh, zl, by):
        z = (zh * 4 + zl + by) % 8
        return z // 4, z % 4

    here = moved(part, lambda zh, y, c, x, zl: (beside(zh, zl, 2)[0], y, 0, x, beside(zh, zl, 2)[1]) if c == 0
                 else (zh, y ^ 1, 1, x, zl))
    there = moved(part, lambda zh, y, c, x, zl: (beside(zh, zl, -2)[0], y, 0, x, beside(zh, zl, -2)[1]) if c == 0
                  else None)
    piece = (here.astype(F32) + there.astype(F32)).astype(BF16)

    pieces = [piece]
    for k in (1, 2, 3):
        pieces.append(moved(
            piece,
            lambda zh, y, c, x, zl: (zh, (y + k) % 4, 0, x, zl) if c == 0 else (zh, y, 1, (x + k) % 4, zl),
        ))

    own_w, _ = lax.optimization_barrier((weight_grad, piece))
    weights = [
        moved(own_w, lambda zh, y, c, x, zl: (zh, y, 1 - c, x, zl)),
        moved(own_w, lambda zh, y, c, x, zl: (zh, y ^ 1, 1, x, zl) if c == 0 else (zh, y, 0, x, zl)),
        moved(own_w, lambda zh, y, c, x, zl: (zh, y ^ 1, 1, x, zl) if c == 1 else None),
    ]
    damp = pick(damping, jnp.where(is_g, BLOCKS_A + o, zh * 2 + y // 2)).reshape(1)
    place = jnp.stack([jnp.where(is_g, y, x), core, y % 2])
    inverse, *weights = lax.optimization_barrier((rounds(place, damp, pieces), *weights))
    weights.insert(1, weight_grad)

    mine = mix(place, inverse, weights)
    other = moved(mine, lambda zh, y, c, x, zl: (zh, y, 1 - c, x, zl))
    return last(place, mine, other, weight_grad.shape[0])


def solution(mesh):
    placed = (
        P(("dp", "owner"), None),
        P(("dp", "owner"), None),
        P(("dp", "owner")),
        P(),
        P("dp", "owner"),
    )
    return jax.shard_map(
        on_device, mesh=mesh, in_specs=placed, out_specs=P("dp", "owner"), check_vma=False
    )
```

```python
import jax
import jax.numpy as jnp
from jax import lax
from jax.experimental import pallas as pl
from jax.experimental.pallas import tpu as pltpu
from jax.sharding import PartitionSpec as P

BLOCKS_A = 4
ITERS = 5
BF16 = jnp.bfloat16
F32 = jnp.float32
MIB = 2 ** 20
UPPER = [(r, c) for r in range(8) for c in range(r, 8)]
PARTS = [UPPER[9 * i:9 * (i + 1)] for i in range(4)]
SMEM = pl.BlockSpec(memory_space=pltpu.SMEM)
VMEM = pl.BlockSpec(memory_space=pltpu.VMEM)
ANY = pl.BlockSpec(memory_space=pl.ANY)


def dot(a, b):
    return jnp.dot(a, b, preferred_element_type=F32)


def gram(a, b):
    return lax.dot_general(a, b, (((0,), (0,)), ((), ())), preferred_element_type=F32)


def linear(zh, y, c, x, zl):
    return ((zh * 4 + y) * 2 + c) * 16 + x * 4 + zl


def moved(value, where):
    pairs = []
    for source in range(256):
        c, x, zl = source // 16 % 2, source // 4 % 4, source % 4
        zh, y = source // 128, source // 32 % 4
        target = where(zh, y, c, x, zl)
        pairs.append((source, source if target is None else linear(*target)))
    assert len({target for _, target in pairs}) == 256
    return lax.ppermute(value, ("dp", "owner"), pairs)


def dealt(value, group_of):
    groups = []
    for device in range(256):
        c, x, zl = device // 16 % 2, device // 4 % 4, device % 4
        members = [linear(*member) for member in group_of(device // 128, device // 32 % 4, c, x, zl)]
        assert device in members
        if device == min(members):
            groups.append(members)
    assert sorted(sum(groups, [])) == list(range(256))
    return lax.all_to_all(
        value, ("dp", "owner"), split_axis=0, concat_axis=0, tiled=True, axis_index_groups=groups)


def over_plane(zh, y, c, x, zl):
    return [(zh, y, c, i, k) for i in range(4) for k in range(4)]


def over_blocks(zh, y, c, x, zl):
    z = (zh * 4 + zl + (-2 if zl < 2 else 2)) % 8
    places = {zh: (zh, zl), 1 - zh: (z // 4, z % 4)}
    return [
        (places[h][0], y if y // 2 == g else 3 - y, c, i, places[h][1])
        for i in range(4) for h in range(2) for g in range(2)
    ]


def offer_kernel(core_ref, x_ref, g_ref, out_ref):
    @pl.when(core_ref[0] == 0)
    def _():
        out_ref[:, :x_ref.shape[1]] = x_ref[...]
        out_ref[:, x_ref.shape[1]:] = jnp.zeros((x_ref.shape[0], out_ref.shape[1] - x_ref.shape[1]), BF16)

    @pl.when(core_ref[0] == 1)
    def _():
        out_ref[...] = g_ref[...]


def offer(core, samp_x, samp_g):
    return pl.pallas_call(
        offer_kernel,
        out_shape=jax.ShapeDtypeStruct(samp_g.shape, BF16),
        in_specs=[SMEM, VMEM, VMEM],
        out_specs=VMEM,
        compiler_params=pltpu.CompilerParams(vmem_limit_bytes=8 * MIB),
    )(core, samp_x, samp_g)


def pack_kernel(core_ref, x_ref, g_ref, other_ref, out_ref):
    count, size = x_ref.shape[0], out_ref.shape[2]

    def put(mine_ref, column):
        for part in range(16):
            cols = slice(column(part) * size, (column(part) + 1) * size)
            out_ref[part, :count, :] = mine_ref[:, cols]
            out_ref[part, count:, :] = other_ref[:, cols]

    @pl.when(core_ref[0] == 0)
    def _():
        put(g_ref, lambda part: part // 4 * 4 + (part + 2) % 4)

    @pl.when(core_ref[0] == 1)
    def _():
        put(x_ref, lambda part: part % 4)


def pack(core, samp_x, samp_g, other, size):
    return pl.pallas_call(
        pack_kernel,
        out_shape=jax.ShapeDtypeStruct((16, 2 * samp_x.shape[0], size), BF16),
        in_specs=[SMEM] + [VMEM] * 3,
        out_specs=VMEM,
        compiler_params=pltpu.CompilerParams(vmem_limit_bytes=8 * MIB),
    )(core, samp_x, samp_g, other)


def cov_kernel(scale, place_ref, *refs):
    all_ref, chunks, (full_ref, parts_ref) = refs[0], refs[1:5], refs[5:]
    size = all_ref.shape[1]
    tile, small = size // 4, size // 8
    for r in range(4):
        cols = all_ref[:, r * tile:(r + 1) * tile]
        full_ref[r * tile:(r + 1) * tile, r * tile:] = (gram(cols, all_ref[:, r * tile:]) * scale).astype(BF16)
    for i, tiles in enumerate(PARTS):
        for t, (r, c) in enumerate(tiles):
            parts_ref[i, t * small:(t + 1) * small, :] = full_ref[
                r * small:(r + 1) * small, c * small:(c + 1) * small]
    for k, chunk in enumerate(chunks):
        chunk[...] = parts_ref[lax.rem(place_ref[0] + k * place_ref[1], 4)]


def cov(place, samples, scale):
    size = samples.shape[1]
    part = (len(PARTS[0]) * size // 8, size // 8)
    return pl.pallas_call(
        lambda *refs: cov_kernel(scale, *refs),
        out_shape=(jax.ShapeDtypeStruct(part, BF16),) * 4,
        in_specs=[SMEM, VMEM],
        out_specs=(VMEM,) * 4,
        scratch_shapes=[pltpu.VMEM((size, size), BF16), pltpu.VMEM((4,) + part, BF16)],
        compiler_params=pltpu.CompilerParams(vmem_limit_bytes=20 * MIB),
    )(place, samples)


def rounds_kernel(place_ref, damp_ref, p0, p1, p2, p3, w0, w1, w2, w3, out_ref,
                  a_ref, x_ref, xb_ref, p_ref, parts_ref, w_ref, sems):
    size = out_ref.shape[0]
    tile, small = size // 4, size // 8
    base, core, half, damp = place_ref[0], place_ref[1], place_ref[2], damp_ref[0]
    loads = [pltpu.make_async_copy(w, w_ref.at[i], sems.at[i]) for i, w in enumerate((w0, w1, w2, w3))]
    for load in loads:
        load.start()
    blocks = [slice(i * tile, (i + 1) * tile) for i in range(4)]

    def mirrored(ref, c, value):
        ref[:(c + 1) * tile, blocks[c]] = value
        for r in range(c):
            ref[blocks[c], blocks[r]] = value[blocks[r], :].T

    for k, piece in enumerate((p0, p1, p2, p3)):
        parts_ref[lax.rem(base + 4 - k, 4)] = piece[...]
    for i, tiles in enumerate(PARTS):
        for t, (r, c) in enumerate(tiles):
            value = parts_ref[i, t * small:(t + 1) * small, :]
            rows, cols = slice(r * small, (r + 1) * small), slice(c * small, (c + 1) * small)
            a_ref[rows, cols] = value
            if r < c:
                a_ref[cols, rows] = value.T
    row = lax.broadcasted_iota(jnp.int32, (tile, tile), 0)
    col = lax.broadcasted_iota(jnp.int32, (tile, tile), 1)
    eye = row == col
    total = jnp.zeros((1, 1), F32)
    for r in range(4):
        for c in range(r, 4):
            value = a_ref[blocks[r], blocks[c]].astype(F32)
            if r == c:
                value = value + jnp.where(eye, damp, 0.0)
                a_ref[blocks[r], blocks[c]] = value.astype(BF16)
                total += jnp.sum(value * value, keepdims=True)
            else:
                total += 2.0 * jnp.sum(value * value, keepdims=True)
    frob = jnp.sqrt(total)
    inv = 1.0 / frob
    inv_bf = inv.astype(BF16).astype(F32)
    for r in range(4):
        for c in range(4):
            product = (a_ref[blocks[r], blocks[c]].astype(F32) * inv_bf).astype(BF16).astype(F32)
            value = -product * inv_bf
            if r == c:
                value = value + jnp.where(eye, 2.0 * inv, 0.0)
            if r <= c:
                x_ref[blocks[r], blocks[c]] = value
            xb_ref[0, blocks[r], blocks[c]] = value.astype(BF16)
    for step in range(1, ITERS):
        now, later = xb_ref.at[(step - 1) % 2], xb_ref.at[step % 2]
        for c in (3, 2, 1, 0):
            mirrored(p_ref, c, dot(a_ref[:(c + 1) * tile, :], now[:, blocks[c]]).astype(BF16))
        for c in range(4):
            rows = slice(0, (c + 1) * tile)
            value = 2.0 * x_ref[rows, blocks[c]] - dot(p_ref[rows, :], now[:, blocks[c]])
            if step < ITERS - 1:
                x_ref[rows, blocks[c]] = value
                mirrored(later, c, value.astype(BF16))
            else:
                mirrored(out_ref, c, (value * (frob / 2.0 ** ITERS)).astype(BF16))

    for load in loads:
        load.wait()

    @pl.when(core == 1)
    def _():
        for i in range(2):
            rows = pl.ds(pl.multiple_of((2 * half + i) * tile, tile), tile)
            value = jnp.zeros((tile, size), F32)
            for b in range(4):
                cols = pl.ds(pl.multiple_of(lax.rem(2 * half + b, 4) * tile, tile), tile)
                value += dot(out_ref[rows, cols], w_ref[b])
            p_ref[blocks[i], :] = value.astype(BF16)
        out_ref[:2 * tile, :] = p_ref[:2 * tile, :]


def rounds(place, damp, pieces, weights):
    tile, size = weights[0].shape
    return pl.pallas_call(
        rounds_kernel,
        out_shape=jax.ShapeDtypeStruct((size, size), BF16),
        in_specs=[SMEM, SMEM] + [VMEM] * 4 + [ANY] * 4,
        out_specs=VMEM,
        scratch_shapes=[
            pltpu.VMEM((size, size), BF16),
            pltpu.VMEM((size, size), F32),
            pltpu.VMEM((2, size, size), BF16),
            pltpu.VMEM((size, size), BF16),
            pltpu.VMEM((4,) + pieces[0].shape, BF16),
            pltpu.VMEM((4, tile, size), BF16),
            pltpu.SemaphoreType.DMA((4,)),
        ],
        compiler_params=pltpu.CompilerParams(vmem_limit_bytes=28 * MIB),
    )(place, damp, *pieces, *weights)


def last_kernel(place_ref, mine_ref, other_ref, out_ref):
    tile, size = out_ref.shape

    def put(rows, inverse):
        for i in range(size // tile):
            block = slice(i * tile, (i + 1) * tile)
            value = lax.dot_general(
                inverse[block, :], rows, (((1,), (1,)), ((), ())), preferred_element_type=F32)
            out_ref[:, block] = value.astype(BF16).T

    @pl.when(place_ref[1] == 0)
    def _():
        put(other_ref[:tile, :], mine_ref)

    @pl.when(place_ref[1] == 1)
    def _():
        put(mine_ref[tile:2 * tile, :], other_ref)


def last(place, mine, other, rows):
    return pl.pallas_call(
        last_kernel,
        out_shape=jax.ShapeDtypeStruct((rows, mine.shape[1]), BF16),
        in_specs=[SMEM] + [VMEM] * 2,
        out_specs=VMEM,
        compiler_params=pltpu.CompilerParams(vmem_limit_bytes=16 * MIB),
    )(place, mine, other)


def pick(parts, index):
    return lax.dynamic_index_in_dim(parts, index, 0, keepdims=False)


def on_device(activations, out_grads, sample_ids, damping, weight_grad):
    d, o = lax.axis_index("dp"), lax.axis_index("owner")
    zh, y, core = d // 8, d // 2 % 4, d % 2
    x, zl = o // 4, o % 4
    size = weight_grad.shape[1]
    scale = 1.0 / (sample_ids.shape[0] * 256)
    is_g = core == 0

    hot = (sample_ids[:, None] == jnp.arange(activations.shape[0], dtype=jnp.int32)[None]).astype(BF16)
    samp_g = dot(hot, out_grads).astype(BF16)
    activations, _ = lax.optimization_barrier((activations, samp_g))
    samp_x = dot(hot, activations).astype(BF16)
    other = moved(offer(core.reshape(1), samp_x, samp_g), lambda zh, y, c, x, zl: (zh, y, 1 - c, x, zl))

    packed = pack(core.reshape(1), samp_x, samp_g, other, size)
    samples = dealt(
        packed, lambda *place: over_plane(*place) if place[2] == 0 else over_blocks(*place),
    ).reshape(-1, size)

    own_w, _ = lax.optimization_barrier((weight_grad, packed))
    weights = [
        moved(own_w, lambda zh, y, c, x, zl: (zh, y, 1 - c, x, zl)),
        moved(own_w, lambda zh, y, c, x, zl: (zh, y ^ 1, 1, x, zl) if c == 0 else (zh, y, 0, x, zl)),
        moved(own_w, lambda zh, y, c, x, zl: (zh, y ^ 1, 1, x, zl) if c == 1 else None),
    ]
    samples, weights = lax.optimization_barrier((samples, weights))
    weights.insert(1, weight_grad)

    chunks = cov(jnp.stack([jnp.where(is_g, y, x), 1 - core]), samples, scale)
    total = chunks[0].astype(F32)
    for k in (1, 2, 3):
        total += moved(
            chunks[k],
            lambda zh, y, c, x, zl: (zh, (y + k) % 4, 0, x, zl) if c == 0 else (zh, y, 1, x, (zl + k) % 4),
        ).astype(F32)
    part = total.astype(BF16)

    def beside(zh, zl, by):
        z = (zh * 4 + zl + by) % 8
        return z // 4, z % 4

    here = moved(part, lambda zh, y, c, x, zl: (beside(zh, zl, 2)[0], y, 0, x, beside(zh, zl, 2)[1]) if c == 0
                 else (zh, y ^ 1, 1, x, zl))
    there = moved(part, lambda zh, y, c, x, zl: (beside(zh, zl, -2)[0], y, 0, x, beside(zh, zl, -2)[1]) if c == 0
                  else None)
    piece = (here.astype(F32) + there.astype(F32)).astype(BF16)

    pieces = [piece]
    for k in (1, 2, 3):
        pieces.append(moved(
            piece,
            lambda zh, y, c, x, zl: (zh, (y + k) % 4, 0, x, zl) if c == 0 else (zh, y, 1, (x + k) % 4, zl),
        ))

    damp = pick(damping, jnp.where(is_g, BLOCKS_A + o, zh * 2 + y // 2)).reshape(1)
    place = jnp.stack([jnp.where(is_g, y, x), core, y % 2])
    mine = rounds(place, damp, pieces, weights)
    other = moved(mine, lambda zh, y, c, x, zl: (zh, y, 1 - c, x, zl))
    return last(place, mine, other, weight_grad.shape[0])


def solution(mesh):
    placed = (
        P(("dp", "owner"), None),
        P(("dp", "owner"), None),
        P(("dp", "owner")),
        P(),
        P("dp", "owner"),
    )
    return jax.shard_map(
        on_device, mesh=mesh, in_specs=placed, out_specs=P("dp", "owner"), check_vma=False
    )
```

```python
import jax
import jax.numpy as jnp
from jax import lax
from jax.experimental import pallas as pl
from jax.experimental.pallas import tpu as pltpu
from jax.sharding import PartitionSpec as P

BLOCKS_A = 4
ITERS = 5
BF16 = jnp.bfloat16
F32 = jnp.float32
MIB = 2 ** 20
UPPER = [(r, c) for r in range(8) for c in range(r, 8)]
LARGE = [(r, c) for r in range(4) for c in range(r, 4)]
PARTS = [UPPER[9 * i:9 * (i + 1)] for i in range(4)]
SMEM = pl.BlockSpec(memory_space=pltpu.SMEM)
VMEM = pl.BlockSpec(memory_space=pltpu.VMEM)
ANY = pl.BlockSpec(memory_space=pl.ANY)


def dot(a, b):
    return jnp.dot(a, b, preferred_element_type=F32)


def gram(a, b):
    return lax.dot_general(a, b, (((0,), (0,)), ((), ())), preferred_element_type=F32)


def linear(zh, y, c, x, zl):
    return ((zh * 4 + y) * 2 + c) * 16 + x * 4 + zl


def moved(value, where):
    pairs = []
    for source in range(256):
        c, x, zl = source // 16 % 2, source // 4 % 4, source % 4
        zh, y = source // 128, source // 32 % 4
        target = where(zh, y, c, x, zl)
        pairs.append((source, source if target is None else linear(*target)))
    assert len({target for _, target in pairs}) == 256
    return lax.ppermute(value, ("dp", "owner"), pairs)


def dealt(value, group_of):
    groups = []
    for device in range(256):
        c, x, zl = device // 16 % 2, device // 4 % 4, device % 4
        members = [linear(*member) for member in group_of(device // 128, device // 32 % 4, c, x, zl)]
        assert device in members
        if device == min(members):
            groups.append(members)
    assert sorted(sum(groups, [])) == list(range(256))
    return lax.all_to_all(
        value, ("dp", "owner"), split_axis=0, concat_axis=0, tiled=True, axis_index_groups=groups)


def over_plane(zh, y, c, x, zl):
    return [(zh, y, c, i, k) for i in range(4) for k in range(4)]


def over_blocks(zh, y, c, x, zl):
    z = (zh * 4 + zl + (-2 if zl < 2 else 2)) % 8
    places = {zh: (zh, zl), 1 - zh: (z // 4, z % 4)}
    return [
        (places[h][0], y if y // 2 == g else 3 - y, c, i, places[h][1])
        for i in range(4) for h in range(2) for g in range(2)
    ]


def offer_kernel(core_ref, x_ref, g_ref, out_ref):
    @pl.when(core_ref[0] == 0)
    def _():
        out_ref[:, :x_ref.shape[1]] = x_ref[...]
        out_ref[:, x_ref.shape[1]:] = jnp.zeros((x_ref.shape[0], out_ref.shape[1] - x_ref.shape[1]), BF16)

    @pl.when(core_ref[0] == 1)
    def _():
        out_ref[...] = g_ref[...]


def offer(core, samp_x, samp_g):
    return pl.pallas_call(
        offer_kernel,
        out_shape=jax.ShapeDtypeStruct(samp_g.shape, BF16),
        in_specs=[SMEM, VMEM, VMEM],
        out_specs=VMEM,
        compiler_params=pltpu.CompilerParams(vmem_limit_bytes=8 * MIB),
    )(core, samp_x, samp_g)


def pack_kernel(core_ref, x_ref, g_ref, other_ref, out_ref):
    count, size = x_ref.shape[0], out_ref.shape[2]

    def put(mine_ref, column):
        for part in range(16):
            cols = slice(column(part) * size, (column(part) + 1) * size)
            out_ref[part, :count, :] = mine_ref[:, cols]
            out_ref[part, count:, :] = other_ref[:, cols]

    @pl.when(core_ref[0] == 0)
    def _():
        put(g_ref, lambda part: part // 4 * 4 + (part + 2) % 4)

    @pl.when(core_ref[0] == 1)
    def _():
        put(x_ref, lambda part: part % 4)


def pack(core, samp_x, samp_g, other, size):
    return pl.pallas_call(
        pack_kernel,
        out_shape=jax.ShapeDtypeStruct((16, 2 * samp_x.shape[0], size), BF16),
        in_specs=[SMEM] + [VMEM] * 3,
        out_specs=VMEM,
        compiler_params=pltpu.CompilerParams(vmem_limit_bytes=8 * MIB),
    )(core, samp_x, samp_g, other)


def cov_kernel(scale, place_ref, *refs):
    all_ref, chunks, (full_ref, parts_ref) = refs[0], refs[1:5], refs[5:]
    size = all_ref.shape[1]
    tile, small = size // 4, size // 8
    for r in range(4):
        cols = all_ref[:, r * tile:(r + 1) * tile]
        full_ref[r * tile:(r + 1) * tile, r * tile:] = (gram(cols, all_ref[:, r * tile:]) * scale).astype(BF16)
    for i, tiles in enumerate(PARTS):
        for t, (r, c) in enumerate(tiles):
            parts_ref[i, t * small:(t + 1) * small, :] = full_ref[
                r * small:(r + 1) * small, c * small:(c + 1) * small]
    for k, chunk in enumerate(chunks):
        chunk[...] = parts_ref[lax.rem(place_ref[0] + k * place_ref[1], 4)]


def cov(place, samples, scale):
    size = samples.shape[1]
    part = (len(PARTS[0]) * size // 8, size // 8)
    return pl.pallas_call(
        lambda *refs: cov_kernel(scale, *refs),
        out_shape=(jax.ShapeDtypeStruct(part, BF16),) * 4,
        in_specs=[SMEM, VMEM],
        out_specs=(VMEM,) * 4,
        scratch_shapes=[pltpu.VMEM((size, size), BF16), pltpu.VMEM((4,) + part, BF16)],
        compiler_params=pltpu.CompilerParams(vmem_limit_bytes=20 * MIB),
    )(place, samples)


def rounds_kernel(place_ref, damp_ref, p0, p1, p2, p3, w0, w1, w2, w3, out_ref,
                  a_ref, x_ref, xb_ref, p_ref, parts_ref, w_ref, sems):
    size = a_ref.shape[0]
    tile, small = size // 4, size // 8
    base, core, half, damp = place_ref[0], place_ref[1], place_ref[2], damp_ref[0]
    loads = [pltpu.make_async_copy(w, w_ref.at[i], sems.at[i]) for i, w in enumerate((w0, w1, w2, w3))]
    for load in loads:
        load.start()
    blocks = [slice(i * tile, (i + 1) * tile) for i in range(4)]

    def mirrored(ref, c, value):
        ref[:(c + 1) * tile, blocks[c]] = value
        for r in range(c):
            ref[blocks[c], blocks[r]] = value[blocks[r], :].T

    for k, piece in enumerate((p0, p1, p2, p3)):
        parts_ref[lax.rem(base + 4 - k, 4)] = piece[...]
    for i, tiles in enumerate(PARTS):
        for t, (r, c) in enumerate(tiles):
            value = parts_ref[i, t * small:(t + 1) * small, :]
            rows, cols = slice(r * small, (r + 1) * small), slice(c * small, (c + 1) * small)
            a_ref[rows, cols] = value
            if r < c:
                a_ref[cols, rows] = value.T
    row = lax.broadcasted_iota(jnp.int32, (tile, tile), 0)
    col = lax.broadcasted_iota(jnp.int32, (tile, tile), 1)
    eye = row == col
    total = jnp.zeros((1, 1), F32)
    for r in range(4):
        for c in range(r, 4):
            value = a_ref[blocks[r], blocks[c]].astype(F32)
            if r == c:
                value = value + jnp.where(eye, damp, 0.0)
                a_ref[blocks[r], blocks[c]] = value.astype(BF16)
                total += jnp.sum(value * value, keepdims=True)
            else:
                total += 2.0 * jnp.sum(value * value, keepdims=True)
    frob = jnp.sqrt(total)
    inv = 1.0 / frob
    inv_bf = inv.astype(BF16).astype(F32)
    for r in range(4):
        for c in range(4):
            product = (a_ref[blocks[r], blocks[c]].astype(F32) * inv_bf).astype(BF16).astype(F32)
            value = -product * inv_bf
            if r == c:
                value = value + jnp.where(eye, 2.0 * inv, 0.0)
            if r <= c:
                x_ref[blocks[r], blocks[c]] = value
            xb_ref[0, blocks[r], blocks[c]] = value.astype(BF16)
    for step in range(1, ITERS):
        now, later = xb_ref.at[(step - 1) % 2], xb_ref.at[step % 2]
        for c in (3, 2, 1, 0):
            mirrored(p_ref, c, dot(a_ref[:(c + 1) * tile, :], now[:, blocks[c]]).astype(BF16))
        for c in range(4):
            rows = slice(0, (c + 1) * tile)
            value = 2.0 * x_ref[rows, blocks[c]] - dot(p_ref[rows, :], now[:, blocks[c]])
            if step < ITERS - 1:
                x_ref[rows, blocks[c]] = value
                mirrored(later, c, value.astype(BF16))
            else:
                value = (value * (frob / 2.0 ** ITERS)).astype(BF16)
                mirrored(later, c, value)
                for r in range(c + 1):
                    at = LARGE.index((r, c)) * tile
                    out_ref[at:at + tile, :] = value[blocks[r], :]

    for load in loads:
        load.wait()

    @pl.when(core == 1)
    def _():
        for i in range(2):
            rows = pl.ds(pl.multiple_of((2 * half + i) * tile, tile), tile)
            value = jnp.zeros((tile, size), F32)
            for b in range(4):
                cols = pl.ds(pl.multiple_of(lax.rem(2 * half + b, 4) * tile, tile), tile)
                value += dot(xb_ref[(ITERS - 1) % 2, rows, cols], w_ref[b])
            for b in range(4):
                at = (i * 4 + b) * tile
                out_ref[at:at + tile, :] = value[:, blocks[b]].astype(BF16)


def rounds(place, damp, pieces, weights):
    tile, size = weights[0].shape
    return pl.pallas_call(
        rounds_kernel,
        out_shape=jax.ShapeDtypeStruct((len(LARGE) * tile, tile), BF16),
        in_specs=[SMEM, SMEM] + [VMEM] * 4 + [ANY] * 4,
        out_specs=VMEM,
        scratch_shapes=[
            pltpu.VMEM((size, size), BF16),
            pltpu.VMEM((size, size), F32),
            pltpu.VMEM((2, size, size), BF16),
            pltpu.VMEM((size, size), BF16),
            pltpu.VMEM((4,) + pieces[0].shape, BF16),
            pltpu.VMEM((4, tile, size), BF16),
            pltpu.SemaphoreType.DMA((4,)),
        ],
        compiler_params=pltpu.CompilerParams(vmem_limit_bytes=28 * MIB),
    )(place, damp, *pieces, *weights)


def last_kernel(place_ref, mine_ref, other_ref, out_ref):
    tile = out_ref.shape[0]

    def put(rows_ref, first, upper_ref):
        for n in range(4):
            value = jnp.zeros((tile, tile), F32)
            for k in range(4):
                at = LARGE.index((min(k, n), max(k, n))) * tile
                contracted = 0 if k <= n else 1
                value += lax.dot_general(
                    rows_ref[(first + k) * tile:(first + k + 1) * tile, :], upper_ref[at:at + tile, :],
                    (((1,), (contracted,)), ((), ())), preferred_element_type=F32)
            out_ref[:, n * tile:(n + 1) * tile] = value.astype(BF16)

    @pl.when(place_ref[1] == 0)
    def _():
        put(other_ref, 0, mine_ref)

    @pl.when(place_ref[1] == 1)
    def _():
        put(mine_ref, 4, other_ref)


def last(place, mine, other, rows):
    return pl.pallas_call(
        last_kernel,
        out_shape=jax.ShapeDtypeStruct((rows, 4 * rows), BF16),
        in_specs=[SMEM] + [VMEM] * 2,
        out_specs=VMEM,
        compiler_params=pltpu.CompilerParams(vmem_limit_bytes=16 * MIB),
    )(place, mine, other)


def pick(parts, index):
    return lax.dynamic_index_in_dim(parts, index, 0, keepdims=False)


def on_device(activations, out_grads, sample_ids, damping, weight_grad):
    d, o = lax.axis_index("dp"), lax.axis_index("owner")
    zh, y, core = d // 8, d // 2 % 4, d % 2
    x, zl = o // 4, o % 4
    size = weight_grad.shape[1]
    scale = 1.0 / (sample_ids.shape[0] * 256)
    is_g = core == 0

    hot = (sample_ids[:, None] == jnp.arange(activations.shape[0], dtype=jnp.int32)[None]).astype(BF16)
    samp_g = dot(hot, out_grads).astype(BF16)
    activations, _ = lax.optimization_barrier((activations, samp_g))
    samp_x = dot(hot, activations).astype(BF16)
    other = moved(offer(core.reshape(1), samp_x, samp_g), lambda zh, y, c, x, zl: (zh, y, 1 - c, x, zl))

    packed = pack(core.reshape(1), samp_x, samp_g, other, size)
    samples = dealt(
        packed, lambda *place: over_plane(*place) if place[2] == 0 else over_blocks(*place),
    ).reshape(-1, size)

    own_w, _ = lax.optimization_barrier((weight_grad, packed))
    weights = [
        moved(own_w, lambda zh, y, c, x, zl: (zh, y, 1 - c, x, zl)),
        moved(own_w, lambda zh, y, c, x, zl: (zh, y ^ 1, 1, x, zl) if c == 0 else (zh, y, 0, x, zl)),
        moved(own_w, lambda zh, y, c, x, zl: (zh, y ^ 1, 1, x, zl) if c == 1 else None),
    ]
    samples, weights = lax.optimization_barrier((samples, weights))
    weights.insert(1, weight_grad)

    chunks = cov(jnp.stack([jnp.where(is_g, y, x), 1 - core]), samples, scale)
    total = chunks[0].astype(F32)
    for k in (1, 2, 3):
        total += moved(
            chunks[k],
            lambda zh, y, c, x, zl: (zh, (y + k) % 4, 0, x, zl) if c == 0 else (zh, y, 1, x, (zl + k) % 4),
        ).astype(F32)
    part = total.astype(BF16)

    def beside(zh, zl, by):
        z = (zh * 4 + zl + by) % 8
        return z // 4, z % 4

    here = moved(part, lambda zh, y, c, x, zl: (beside(zh, zl, 2)[0], y, 0, x, beside(zh, zl, 2)[1]) if c == 0
                 else (zh, y ^ 1, 1, x, zl))
    there = moved(part, lambda zh, y, c, x, zl: (beside(zh, zl, -2)[0], y, 0, x, beside(zh, zl, -2)[1]) if c == 0
                  else None)
    piece = (here.astype(F32) + there.astype(F32)).astype(BF16)

    pieces = [piece]
    for k in (1, 2, 3):
        pieces.append(moved(
            piece,
            lambda zh, y, c, x, zl: (zh, (y + k) % 4, 0, x, zl) if c == 0 else (zh, y, 1, (x + k) % 4, zl),
        ))

    damp = pick(damping, jnp.where(is_g, BLOCKS_A + o, zh * 2 + y // 2)).reshape(1)
    place = jnp.stack([jnp.where(is_g, y, x), core, y % 2])
    mine = rounds(place, damp, pieces, weights)
    other = moved(mine, lambda zh, y, c, x, zl: (zh, y, 1 - c, x, zl))
    return last(place, mine, other, weight_grad.shape[0])


def solution(mesh):
    placed = (
        P(("dp", "owner"), None),
        P(("dp", "owner"), None),
        P(("dp", "owner")),
        P(),
        P("dp", "owner"),
    )
    return jax.shard_map(
        on_device, mesh=mesh, in_specs=placed, out_specs=P("dp", "owner"), check_vma=False
    )
```

```python
import jax
import jax.numpy as jnp
from jax import lax
from jax.experimental import pallas as pl
from jax.experimental.pallas import tpu as pltpu
from jax.sharding import PartitionSpec as P

BLOCKS_A = 4
ITERS = 5
BF16 = jnp.bfloat16
F32 = jnp.float32
MIB = 2 ** 20
UPPER = [(r, c) for r in range(8) for c in range(r, 8)]
LARGE = [(r, c) for r in range(4) for c in range(r, 4)]
PARTS = [UPPER[9 * i:9 * (i + 1)] for i in range(4)]
SMEM = pl.BlockSpec(memory_space=pltpu.SMEM)
VMEM = pl.BlockSpec(memory_space=pltpu.VMEM)
ANY = pl.BlockSpec(memory_space=pl.ANY)


def dot(a, b):
    return jnp.dot(a, b, preferred_element_type=F32)


def gram(a, b):
    return lax.dot_general(a, b, (((0,), (0,)), ((), ())), preferred_element_type=F32)


def linear(zh, y, c, x, zl):
    return ((zh * 4 + y) * 2 + c) * 16 + x * 4 + zl


def moved(value, where):
    pairs = []
    for source in range(256):
        c, x, zl = source // 16 % 2, source // 4 % 4, source % 4
        zh, y = source // 128, source // 32 % 4
        target = where(zh, y, c, x, zl)
        pairs.append((source, source if target is None else linear(*target)))
    assert len({target for _, target in pairs}) == 256
    return lax.ppermute(value, ("dp", "owner"), pairs)


def dealt(value, group_of):
    groups = []
    for device in range(256):
        c, x, zl = device // 16 % 2, device // 4 % 4, device % 4
        members = [linear(*member) for member in group_of(device // 128, device // 32 % 4, c, x, zl)]
        assert device in members
        if device == min(members):
            groups.append(members)
    assert sorted(sum(groups, [])) == list(range(256))
    return lax.all_to_all(
        value, ("dp", "owner"), split_axis=0, concat_axis=0, tiled=True, axis_index_groups=groups)


def over_plane(zh, y, c, x, zl):
    return [(zh, y, c, i, k) for i in range(4) for k in range(4)]


def over_blocks(zh, y, c, x, zl):
    z = (zh * 4 + zl + (-2 if zl < 2 else 2)) % 8
    places = {zh: (zh, zl), 1 - zh: (z // 4, z % 4)}
    return [
        (places[h][0], y if y // 2 == g else 3 - y, c, i, places[h][1])
        for i in range(4) for h in range(2) for g in range(2)
    ]


def offer_kernel(core_ref, x_ref, g_ref, out_ref):
    @pl.when(core_ref[0] == 0)
    def _():
        out_ref[:, :x_ref.shape[1]] = x_ref[...]
        out_ref[:, x_ref.shape[1]:] = jnp.zeros((x_ref.shape[0], out_ref.shape[1] - x_ref.shape[1]), BF16)

    @pl.when(core_ref[0] == 1)
    def _():
        out_ref[...] = g_ref[...]


def offer(core, samp_x, samp_g):
    return pl.pallas_call(
        offer_kernel,
        out_shape=jax.ShapeDtypeStruct(samp_g.shape, BF16),
        in_specs=[SMEM, VMEM, VMEM],
        out_specs=VMEM,
        compiler_params=pltpu.CompilerParams(vmem_limit_bytes=8 * MIB),
    )(core, samp_x, samp_g)


def pack_kernel(core_ref, x_ref, g_ref, other_ref, out_ref):
    count, size = x_ref.shape[0], out_ref.shape[2]

    def put(mine_ref, column):
        for part in range(16):
            cols = slice(column(part) * size, (column(part) + 1) * size)
            out_ref[part, :count, :] = mine_ref[:, cols]
            out_ref[part, count:, :] = other_ref[:, cols]

    @pl.when(core_ref[0] == 0)
    def _():
        put(g_ref, lambda part: part // 4 * 4 + (part + 2) % 4)

    @pl.when(core_ref[0] == 1)
    def _():
        put(x_ref, lambda part: part % 4)


def pack(core, samp_x, samp_g, other, size):
    return pl.pallas_call(
        pack_kernel,
        out_shape=jax.ShapeDtypeStruct((16, 2 * samp_x.shape[0], size), BF16),
        in_specs=[SMEM] + [VMEM] * 3,
        out_specs=VMEM,
        compiler_params=pltpu.CompilerParams(vmem_limit_bytes=8 * MIB),
    )(core, samp_x, samp_g, other)


def cov_kernel(scale, place_ref, *refs):
    all_ref, chunks, (full_ref, parts_ref) = refs[0], refs[1:5], refs[5:]
    size = all_ref.shape[1]
    tile, small = size // 4, size // 8
    for r in range(4):
        cols = all_ref[:, r * tile:(r + 1) * tile]
        full_ref[r * tile:(r + 1) * tile, r * tile:] = (gram(cols, all_ref[:, r * tile:]) * scale).astype(BF16)
    for i, tiles in enumerate(PARTS):
        for t, (r, c) in enumerate(tiles):
            parts_ref[i, t * small:(t + 1) * small, :] = full_ref[
                r * small:(r + 1) * small, c * small:(c + 1) * small]
    for k, chunk in enumerate(chunks):
        chunk[...] = parts_ref[lax.rem(place_ref[0] + k * place_ref[1], 4)]


def cov(place, samples, scale):
    size = samples.shape[1]
    part = (len(PARTS[0]) * size // 8, size // 8)
    return pl.pallas_call(
        lambda *refs: cov_kernel(scale, *refs),
        out_shape=(jax.ShapeDtypeStruct(part, BF16),) * 4,
        in_specs=[SMEM, VMEM],
        out_specs=(VMEM,) * 4,
        scratch_shapes=[pltpu.VMEM((size, size), BF16), pltpu.VMEM((4,) + part, BF16)],
        compiler_params=pltpu.CompilerParams(vmem_limit_bytes=20 * MIB),
    )(place, samples)


def rounds_kernel(place_ref, damp_ref, p0, p1, p2, p3, w0, w1, w2, w3, out_ref,
                  a_ref, x_ref, xb_ref, p_ref, parts_ref, w_ref, sems):
    size = a_ref.shape[0]
    tile, small = size // 4, size // 8
    base, core, half, damp = place_ref[0], place_ref[1], place_ref[2], damp_ref[0]
    loads = [pltpu.make_async_copy(w, w_ref.at[i], sems.at[i]) for i, w in enumerate((w0, w1, w2, w3))]
    for load in loads:
        load.start()
    blocks = [slice(i * tile, (i + 1) * tile) for i in range(4)]

    def mirrored(ref, c, value):
        ref[:(c + 1) * tile, blocks[c]] = value
        for r in range(c):
            ref[blocks[c], blocks[r]] = value[blocks[r], :].T

    for k, piece in enumerate((p0, p1, p2, p3)):
        parts_ref[lax.rem(base + 4 - k, 4)] = piece[...]
    for i, tiles in enumerate(PARTS):
        for t, (r, c) in enumerate(tiles):
            value = parts_ref[i, t * small:(t + 1) * small, :]
            rows, cols = slice(r * small, (r + 1) * small), slice(c * small, (c + 1) * small)
            a_ref[rows, cols] = value
            if r < c:
                a_ref[cols, rows] = value.T
    row = lax.broadcasted_iota(jnp.int32, (tile, tile), 0)
    col = lax.broadcasted_iota(jnp.int32, (tile, tile), 1)
    eye = row == col
    total = jnp.zeros((1, 1), F32)
    for r in range(4):
        for c in range(r, 4):
            value = a_ref[blocks[r], blocks[c]].astype(F32)
            if r == c:
                value = value + jnp.where(eye, damp, 0.0)
                a_ref[blocks[r], blocks[c]] = value.astype(BF16)
                total += jnp.sum(value * value, keepdims=True)
            else:
                total += 2.0 * jnp.sum(value * value, keepdims=True)
    frob = jnp.sqrt(total)
    inv = 1.0 / frob
    inv_bf = inv.astype(BF16).astype(F32)
    for r in range(4):
        for c in range(4):
            product = (a_ref[blocks[r], blocks[c]].astype(F32) * inv_bf).astype(BF16).astype(F32)
            value = -product * inv_bf
            if r == c:
                value = value + jnp.where(eye, 2.0 * inv, 0.0)
            if r <= c:
                x_ref[blocks[r], blocks[c]] = value
            xb_ref[0, blocks[r], blocks[c]] = value.astype(BF16)
    for step in range(1, ITERS):
        now, later = xb_ref.at[(step - 1) % 2], xb_ref.at[step % 2]
        for c in (3, 2, 1, 0):
            mirrored(p_ref, c, dot(a_ref[:(c + 1) * tile, :], now[:, blocks[c]]).astype(BF16))
        for c in range(4):
            rows = slice(0, (c + 1) * tile)
            value = 2.0 * x_ref[rows, blocks[c]] - dot(p_ref[rows, :], now[:, blocks[c]])
            if step < ITERS - 1:
                x_ref[rows, blocks[c]] = value
                mirrored(later, c, value.astype(BF16))
            else:
                value = (value * (frob / 2.0 ** ITERS)).astype(BF16)
                mirrored(later, c, value)
                for r in range(c + 1):
                    at = LARGE.index((r, c)) * tile
                    out_ref[at:at + tile, :] = value[blocks[r], :]

    for load in loads:
        load.wait()

    @pl.when(core == 1)
    def _():
        for i in range(2):
            rows = pl.ds(pl.multiple_of((2 * half + i) * tile, tile), tile)
            value = jnp.zeros((tile, size), F32)
            for b in range(4):
                cols = pl.ds(pl.multiple_of(lax.rem(2 * half + b, 4) * tile, tile), tile)
                value += dot(xb_ref[(ITERS - 1) % 2, rows, cols], w_ref[b])
            for b in range(4):
                at = (i * 4 + b) * tile
                out_ref[at:at + tile, :] = value[:, blocks[b]].astype(BF16)


def rounds(place, damp, pieces, weights):
    tile, size = weights[0].shape
    return pl.pallas_call(
        rounds_kernel,
        out_shape=jax.ShapeDtypeStruct((len(LARGE) * tile, tile), BF16),
        in_specs=[SMEM, SMEM] + [VMEM] * 4 + [ANY] * 4,
        out_specs=VMEM,
        scratch_shapes=[
            pltpu.VMEM((size, size), BF16),
            pltpu.VMEM((size, size), F32),
            pltpu.VMEM((2, size, size), BF16),
            pltpu.VMEM((size, size), BF16),
            pltpu.VMEM((4,) + pieces[0].shape, BF16),
            pltpu.VMEM((4, tile, size), BF16),
            pltpu.SemaphoreType.DMA((4,)),
        ],
        compiler_params=pltpu.CompilerParams(vmem_limit_bytes=28 * MIB),
    )(place, damp, *pieces, *weights)


def last_kernel(place_ref, mine_ref, other_ref, out_ref):
    tile = out_ref.shape[0]

    def put(rows_ref, first, upper_ref):
        for n in range(4):
            value = jnp.zeros((tile, tile), F32)
            for k in range(4):
                at = LARGE.index((min(k, n), max(k, n))) * tile
                contracted = 0 if k <= n else 1
                value += lax.dot_general(
                    rows_ref[(first + k) * tile:(first + k + 1) * tile, :], upper_ref[at:at + tile, :],
                    (((1,), (contracted,)), ((), ())), preferred_element_type=F32)
            out_ref[:, n * tile:(n + 1) * tile] = value.astype(BF16)

    @pl.when(place_ref[1] == 0)
    def _():
        put(other_ref, 0, mine_ref)

    @pl.when(place_ref[1] == 1)
    def _():
        put(mine_ref, 4, other_ref)


def last(place, mine, other, rows):
    return pl.pallas_call(
        last_kernel,
        out_shape=jax.ShapeDtypeStruct((rows, 4 * rows), BF16),
        in_specs=[SMEM] + [VMEM] * 2,
        out_specs=VMEM,
        compiler_params=pltpu.CompilerParams(vmem_limit_bytes=16 * MIB),
    )(place, mine, other)


def pick(parts, index):
    return lax.dynamic_index_in_dim(parts, index, 0, keepdims=False)


def on_device(activations, out_grads, sample_ids, damping, weight_grad):
    d, o = lax.axis_index("dp"), lax.axis_index("owner")
    zh, y, core = d // 8, d // 2 % 4, d % 2
    x, zl = o // 4, o % 4
    size = weight_grad.shape[1]
    scale = 1.0 / (sample_ids.shape[0] * 256)
    is_g = core == 0

    hot = (sample_ids[:, None] == jnp.arange(activations.shape[0], dtype=jnp.int32)[None]).astype(BF16)
    samp_g = dot(hot, out_grads).astype(BF16)
    activations, _ = lax.optimization_barrier((activations, samp_g))
    samp_x = dot(hot, activations).astype(BF16)
    other = moved(offer(core.reshape(1), samp_x, samp_g), lambda zh, y, c, x, zl: (zh, y, 1 - c, x, zl))

    packed = pack(core.reshape(1), samp_x, samp_g, other, size)
    samples = dealt(
        packed, lambda *place: over_plane(*place) if place[2] == 0 else over_blocks(*place),
    ).reshape(-1, size)

    own_w, _ = lax.optimization_barrier((weight_grad, packed))
    weights = [
        moved(own_w, lambda zh, y, c, x, zl: (zh, y, 1 - c, x, zl)),
        moved(own_w, lambda zh, y, c, x, zl: (zh, y ^ 1, 1, x, zl) if c == 0 else (zh, y, 0, x, zl)),
        moved(own_w, lambda zh, y, c, x, zl: (zh, y ^ 1, 1, x, zl) if c == 1 else None),
    ]
    samples, weights = lax.optimization_barrier((samples, weights))
    weights.insert(1, weight_grad)

    chunks = cov(jnp.stack([jnp.where(is_g, y, x), 1 - core]), samples, scale)
    total = chunks[0].astype(F32)
    for k in (1, 2, 3):
        total += moved(
            chunks[k],
            lambda zh, y, c, x, zl: (zh, (y + k) % 4, 0, x, zl) if c == 0 else (zh, y, 1, x, (zl + k) % 4),
        ).astype(F32)
    part = total.astype(BF16)

    def beside(zh, zl, by):
        z = (zh * 4 + zl + by) % 8
        return z // 4, z % 4

    halves = jnp.split(part, 2)
    here = [moved(half, lambda zh, y, c, x, zl: (beside(zh, zl, 2)[0], y, 0, x, beside(zh, zl, 2)[1]) if c == 0
                  else (zh, y ^ 1, 1, x, zl)) for half in halves]
    there = [moved(half, lambda zh, y, c, x, zl: (beside(zh, zl, -2)[0], y, 0, x, beside(zh, zl, -2)[1]) if c == 0
                   else None) for half in halves]
    piece = jnp.concatenate([(h.astype(F32) + t.astype(F32)).astype(BF16) for h, t in zip(here, there)])

    pieces = [piece]
    for k in (1, 2, 3):
        pieces.append(moved(
            piece,
            lambda zh, y, c, x, zl: (zh, (y + k) % 4, 0, x, zl) if c == 0 else (zh, y, 1, (x + k) % 4, zl),
        ))

    damp = pick(damping, jnp.where(is_g, BLOCKS_A + o, zh * 2 + y // 2)).reshape(1)
    place = jnp.stack([jnp.where(is_g, y, x), core, y % 2])
    mine = rounds(place, damp, pieces, weights)
    other = moved(mine, lambda zh, y, c, x, zl: (zh, y, 1 - c, x, zl))
    return last(place, mine, other, weight_grad.shape[0])


def solution(mesh):
    placed = (
        P(("dp", "owner"), None),
        P(("dp", "owner"), None),
        P(("dp", "owner")),
        P(),
        P("dp", "owner"),
    )
    return jax.shard_map(
        on_device, mesh=mesh, in_specs=placed, out_specs=P("dp", "owner"), check_vma=False
    )
```

```python
import jax
import jax.numpy as jnp
from jax import lax
from jax.experimental import pallas as pl
from jax.experimental.pallas import tpu as pltpu
from jax.sharding import PartitionSpec as P

BLOCKS_A = 4
ITERS = 5
BF16 = jnp.bfloat16
F32 = jnp.float32
MIB = 2 ** 20
UPPER = [(r, c) for r in range(8) for c in range(r, 8)]
LARGE = [(r, c) for r in range(4) for c in range(r, 4)]
PARTS = [UPPER[9 * i:9 * (i + 1)] for i in range(4)]
SMEM = pl.BlockSpec(memory_space=pltpu.SMEM)
VMEM = pl.BlockSpec(memory_space=pltpu.VMEM)
ANY = pl.BlockSpec(memory_space=pl.ANY)


def dot(a, b):
    return jnp.dot(a, b, preferred_element_type=F32)


def gram(a, b):
    return lax.dot_general(a, b, (((0,), (0,)), ((), ())), preferred_element_type=F32)


def linear(zh, y, c, x, zl):
    return ((zh * 4 + y) * 2 + c) * 16 + x * 4 + zl


def moved(value, where):
    pairs = []
    for source in range(256):
        c, x, zl = source // 16 % 2, source // 4 % 4, source % 4
        zh, y = source // 128, source // 32 % 4
        target = where(zh, y, c, x, zl)
        pairs.append((source, source if target is None else linear(*target)))
    assert len({target for _, target in pairs}) == 256
    return lax.ppermute(value, ("dp", "owner"), pairs)


def dealt(value, group_of):
    groups = []
    for device in range(256):
        c, x, zl = device // 16 % 2, device // 4 % 4, device % 4
        members = [linear(*member) for member in group_of(device // 128, device // 32 % 4, c, x, zl)]
        assert device in members
        if device == min(members):
            groups.append(members)
    assert sorted(sum(groups, [])) == list(range(256))
    return lax.all_to_all(
        value, ("dp", "owner"), split_axis=0, concat_axis=0, tiled=True, axis_index_groups=groups)


def over_plane(zh, y, c, x, zl):
    return [(zh, y, c, i, k) for i in range(4) for k in range(4)]


def over_blocks(zh, y, c, x, zl):
    z = (zh * 4 + zl + (-2 if zl < 2 else 2)) % 8
    places = {zh: (zh, zl), 1 - zh: (z // 4, z % 4)}
    return [
        (places[h][0], y if y // 2 == g else 3 - y, c, i, places[h][1])
        for i in range(4) for h in range(2) for g in range(2)
    ]


def offer_kernel(core_ref, x_ref, g_ref, out_ref):
    @pl.when(core_ref[0] == 0)
    def _():
        out_ref[:, :x_ref.shape[1]] = x_ref[...]
        out_ref[:, x_ref.shape[1]:] = jnp.zeros((x_ref.shape[0], out_ref.shape[1] - x_ref.shape[1]), BF16)

    @pl.when(core_ref[0] == 1)
    def _():
        out_ref[...] = g_ref[...]


def offer(core, samp_x, samp_g):
    return pl.pallas_call(
        offer_kernel,
        out_shape=jax.ShapeDtypeStruct(samp_g.shape, BF16),
        in_specs=[SMEM, VMEM, VMEM],
        out_specs=VMEM,
        compiler_params=pltpu.CompilerParams(vmem_limit_bytes=8 * MIB),
    )(core, samp_x, samp_g)


def pack_kernel(core_ref, x_ref, g_ref, other_ref, out_ref):
    count, size = x_ref.shape[0], out_ref.shape[2]

    def put(mine_ref, column):
        for part in range(16):
            cols = slice(column(part) * size, (column(part) + 1) * size)
            out_ref[part, :count, :] = mine_ref[:, cols]
            out_ref[part, count:, :] = other_ref[:, cols]

    @pl.when(core_ref[0] == 0)
    def _():
        put(g_ref, lambda part: part // 4 * 4 + (part + 2) % 4)

    @pl.when(core_ref[0] == 1)
    def _():
        put(x_ref, lambda part: part % 4)


def pack(core, samp_x, samp_g, other, size):
    return pl.pallas_call(
        pack_kernel,
        out_shape=jax.ShapeDtypeStruct((16, 2 * samp_x.shape[0], size), BF16),
        in_specs=[SMEM] + [VMEM] * 3,
        out_specs=VMEM,
        compiler_params=pltpu.CompilerParams(vmem_limit_bytes=8 * MIB),
    )(core, samp_x, samp_g, other)


def cov_kernel(scale, place_ref, *refs):
    all_ref, chunks, (full_ref, parts_ref) = refs[0], refs[1:5], refs[5:]
    size = all_ref.shape[1]
    tile, small = size // 4, size // 8
    for r in range(4):
        cols = all_ref[:, r * tile:(r + 1) * tile]
        full_ref[r * tile:(r + 1) * tile, r * tile:] = (gram(cols, all_ref[:, r * tile:]) * scale).astype(BF16)
    for i, tiles in enumerate(PARTS):
        for t, (r, c) in enumerate(tiles):
            parts_ref[i, t * small:(t + 1) * small, :] = full_ref[
                r * small:(r + 1) * small, c * small:(c + 1) * small]
    for k, chunk in enumerate(chunks):
        chunk[...] = parts_ref[lax.rem(place_ref[0] + k * place_ref[1], 4)]


def cov(place, samples, scale):
    size = samples.shape[1]
    part = (len(PARTS[0]) * size // 8, size // 8)
    return pl.pallas_call(
        lambda *refs: cov_kernel(scale, *refs),
        out_shape=(jax.ShapeDtypeStruct(part, BF16),) * 4,
        in_specs=[SMEM, VMEM],
        out_specs=(VMEM,) * 4,
        scratch_shapes=[pltpu.VMEM((size, size), BF16), pltpu.VMEM((4,) + part, BF16)],
        compiler_params=pltpu.CompilerParams(vmem_limit_bytes=20 * MIB),
    )(place, samples)


def rounds_kernel(place_ref, damp_ref, p0, p1, p2, p3, w0, w1, w2, w3, out_ref,
                  a_ref, x_ref, xb_ref, p_ref, parts_ref, w_ref, sems):
    size = a_ref.shape[0]
    tile, small = size // 4, size // 8
    base, core, half, damp = place_ref[0], place_ref[1], place_ref[2], damp_ref[0]
    loads = [pltpu.make_async_copy(w, w_ref.at[i], sems.at[i]) for i, w in enumerate((w0, w1, w2, w3))]
    for load in loads:
        load.start()
    blocks = [slice(i * tile, (i + 1) * tile) for i in range(4)]

    def mirrored(ref, c, value):
        ref[:(c + 1) * tile, blocks[c]] = value
        for r in range(c):
            ref[blocks[c], blocks[r]] = value[blocks[r], :].T

    for k, piece in enumerate((p0, p1, p2, p3)):
        parts_ref[lax.rem(base + 4 - k, 4)] = piece[...]
    for i, tiles in enumerate(PARTS):
        for t, (r, c) in enumerate(tiles):
            value = parts_ref[i, t * small:(t + 1) * small, :]
            rows, cols = slice(r * small, (r + 1) * small), slice(c * small, (c + 1) * small)
            a_ref[rows, cols] = value
            if r < c:
                a_ref[cols, rows] = value.T
    row = lax.broadcasted_iota(jnp.int32, (tile, tile), 0)
    col = lax.broadcasted_iota(jnp.int32, (tile, tile), 1)
    eye = row == col
    total = jnp.zeros((1, 1), F32)
    for r in range(4):
        for c in range(r, 4):
            value = a_ref[blocks[r], blocks[c]].astype(F32)
            if r == c:
                value = value + jnp.where(eye, damp, 0.0)
                a_ref[blocks[r], blocks[c]] = value.astype(BF16)
                total += jnp.sum(value * value, keepdims=True)
            else:
                total += 2.0 * jnp.sum(value * value, keepdims=True)
    frob = jnp.sqrt(total)
    inv = 1.0 / frob
    inv_bf = inv.astype(BF16).astype(F32)
    for r in range(4):
        for c in range(4):
            product = (a_ref[blocks[r], blocks[c]].astype(F32) * inv_bf).astype(BF16).astype(F32)
            value = -product * inv_bf
            if r == c:
                value = value + jnp.where(eye, 2.0 * inv, 0.0)
            if r <= c:
                x_ref[blocks[r], blocks[c]] = value
            xb_ref[0, blocks[r], blocks[c]] = value.astype(BF16)
    for step in range(1, ITERS):
        now, later = xb_ref.at[(step - 1) % 2], xb_ref.at[step % 2]
        for c in (3, 2, 1, 0):
            mirrored(p_ref, c, dot(a_ref[:(c + 1) * tile, :], now[:, blocks[c]]).astype(BF16))
        for c in range(4):
            rows = slice(0, (c + 1) * tile)
            value = 2.0 * x_ref[rows, blocks[c]] - dot(p_ref[rows, :], now[:, blocks[c]])
            if step < ITERS - 1:
                x_ref[rows, blocks[c]] = value
                mirrored(later, c, value.astype(BF16))
            else:
                value = (value * (frob / 2.0 ** ITERS)).astype(BF16)
                mirrored(later, c, value)
                for r in range(c + 1):
                    at = LARGE.index((r, c)) * tile
                    out_ref[at:at + tile, :] = value[blocks[r], :]

    for load in loads:
        load.wait()

    @pl.when(core == 1)
    def _():
        for i in range(2):
            rows = pl.ds(pl.multiple_of((2 * half + i) * tile, tile), tile)
            value = jnp.zeros((tile, size), F32)
            for b in range(4):
                cols = pl.ds(pl.multiple_of(lax.rem(2 * half + b, 4) * tile, tile), tile)
                value += dot(xb_ref[(ITERS - 1) % 2, rows, cols], w_ref[b])
            for b in range(4):
                at = (i * 4 + b) * tile
                out_ref[at:at + tile, :] = value[:, blocks[b]].astype(BF16)


def rounds(place, damp, pieces, weights):
    tile, size = weights[0].shape
    return pl.pallas_call(
        rounds_kernel,
        out_shape=jax.ShapeDtypeStruct((len(LARGE) * tile, tile), BF16),
        in_specs=[SMEM, SMEM] + [VMEM] * 4 + [ANY] * 4,
        out_specs=VMEM,
        scratch_shapes=[
            pltpu.VMEM((size, size), BF16),
            pltpu.VMEM((size, size), F32),
            pltpu.VMEM((2, size, size), BF16),
            pltpu.VMEM((size, size), BF16),
            pltpu.VMEM((4,) + pieces[0].shape, BF16),
            pltpu.VMEM((4, tile, size), BF16),
            pltpu.SemaphoreType.DMA((4,)),
        ],
        compiler_params=pltpu.CompilerParams(vmem_limit_bytes=28 * MIB),
    )(place, damp, *pieces, *weights)


def last_kernel(place_ref, mine_ref, other_ref, out_ref):
    tile = out_ref.shape[0]

    def put(rows_ref, first, upper_ref):
        for n in range(4):
            value = jnp.zeros((tile, tile), F32)
            for k in range(4):
                at = LARGE.index((min(k, n), max(k, n))) * tile
                contracted = 0 if k <= n else 1
                value += lax.dot_general(
                    rows_ref[(first + k) * tile:(first + k + 1) * tile, :], upper_ref[at:at + tile, :],
                    (((1,), (contracted,)), ((), ())), preferred_element_type=F32)
            out_ref[:, n * tile:(n + 1) * tile] = value.astype(BF16)

    @pl.when(place_ref[1] == 0)
    def _():
        put(other_ref, 0, mine_ref)

    @pl.when(place_ref[1] == 1)
    def _():
        put(mine_ref, 4, other_ref)


def last(place, mine, other, rows):
    return pl.pallas_call(
        last_kernel,
        out_shape=jax.ShapeDtypeStruct((rows, 4 * rows), BF16),
        in_specs=[SMEM] + [VMEM] * 2,
        out_specs=VMEM,
        compiler_params=pltpu.CompilerParams(vmem_limit_bytes=16 * MIB),
    )(place, mine, other)


def pick(parts, index):
    return lax.dynamic_index_in_dim(parts, index, 0, keepdims=False)


def on_device(activations, out_grads, sample_ids, damping, weight_grad):
    d, o = lax.axis_index("dp"), lax.axis_index("owner")
    zh, y, core = d // 8, d // 2 % 4, d % 2
    x, zl = o // 4, o % 4
    size = weight_grad.shape[1]
    scale = 1.0 / (sample_ids.shape[0] * 256)
    is_g = core == 0

    hot = (sample_ids[:, None] == jnp.arange(activations.shape[0], dtype=jnp.int32)[None]).astype(BF16)
    samp_g = dot(hot, out_grads).astype(BF16)
    activations, _ = lax.optimization_barrier((activations, samp_g))
    samp_x = dot(hot, activations).astype(BF16)
    other = moved(offer(core.reshape(1), samp_x, samp_g), lambda zh, y, c, x, zl: (zh, y, 1 - c, x, zl))

    packed = pack(core.reshape(1), samp_x, samp_g, other, size)
    samples = dealt(
        packed, lambda *place: over_plane(*place) if place[2] == 0 else over_blocks(*place),
    ).reshape(-1, size)

    own_w, _ = lax.optimization_barrier((weight_grad, packed))
    weights = [
        moved(own_w, lambda zh, y, c, x, zl: (zh, y, 1 - c, x, zl)),
        moved(own_w, lambda zh, y, c, x, zl: (zh, y ^ 1, 1, x, zl) if c == 0 else (zh, y, 0, x, zl)),
        moved(own_w, lambda zh, y, c, x, zl: (zh, y ^ 1, 1, x, zl) if c == 1 else None),
    ]
    chunks = cov(jnp.stack([jnp.where(is_g, y, x), 1 - core]), samples, scale)
    chunks, weights = lax.optimization_barrier((chunks, weights))
    weights.insert(1, weight_grad)
    total = chunks[0].astype(F32)
    for k in (1, 2, 3):
        total += moved(
            chunks[k],
            lambda zh, y, c, x, zl: (zh, (y + k) % 4, 0, x, zl) if c == 0 else (zh, y, 1, x, (zl + k) % 4),
        ).astype(F32)
    part = total.astype(BF16)

    def beside(zh, zl, by):
        z = (zh * 4 + zl + by) % 8
        return z // 4, z % 4

    here = moved(part, lambda zh, y, c, x, zl: (beside(zh, zl, 2)[0], y, 0, x, beside(zh, zl, 2)[1]) if c == 0
                 else (zh, y ^ 1, 1, x, zl))
    there = moved(part, lambda zh, y, c, x, zl: (beside(zh, zl, -2)[0], y, 0, x, beside(zh, zl, -2)[1]) if c == 0
                  else None)
    piece = (here.astype(F32) + there.astype(F32)).astype(BF16)

    pieces = [piece]
    for k in (1, 2, 3):
        pieces.append(moved(
            piece,
            lambda zh, y, c, x, zl: (zh, (y + k) % 4, 0, x, zl) if c == 0 else (zh, y, 1, (x + k) % 4, zl),
        ))

    damp = pick(damping, jnp.where(is_g, BLOCKS_A + o, zh * 2 + y // 2)).reshape(1)
    place = jnp.stack([jnp.where(is_g, y, x), core, y % 2])
    mine = rounds(place, damp, pieces, weights)
    other = moved(mine, lambda zh, y, c, x, zl: (zh, y, 1 - c, x, zl))
    return last(place, mine, other, weight_grad.shape[0])


def solution(mesh):
    placed = (
        P(("dp", "owner"), None),
        P(("dp", "owner"), None),
        P(("dp", "owner")),
        P(),
        P("dp", "owner"),
    )
    return jax.shard_map(
        on_device, mesh=mesh, in_specs=placed, out_specs=P("dp", "owner"), check_vma=False
    )
```
